32 devices in a mesh: seq: 8 (over z, y), batch: 4 (over x, core).
Axes of the slice: x: 2, y: 2, z: 4, core: 2. Of those that a mesh axis runs over, the one named last changes fastest.
Arguments:
- layer_entries: bfloat16 [1024, 8, 2048], P('seq', 'batch'), may hold values from -6 to 6
- incoming_adjoint: bfloat16 [1024, 8, 2048], P('seq', 'batch'), may hold values from -6 to 6
- mixing_rescale_scalers: bfloat16 [2048], P(('seq', 'batch')), may hold values from 0.5 to 1.5
- triple_projector_matrix: bfloat16 [2048, 6144], P(('seq', 'batch')), may hold values from -0.1875 to 0.1875
- context_exit_matrix: bfloat16 [2048, 2048], P(('seq', 'batch')), may hold values from -0.5 to 0.5
- dense_center_scaler: bfloat16 [2048], P(('seq', 'batch')), may hold values from 0.5 to 1.5
- dense_center_offset: bfloat16 [2048], P(('seq', 'batch')), may hold values from -1.5 to 1.5
- expand_matrix: bfloat16 [2048, 8192], P(('seq', 'batch')), may hold values from -0.125 to 0.125
- shrink_matrix: bfloat16 [8192, 2048], P(('seq', 'batch')), may hold values from -0.0625 to 0.0625
- span_chooser_initial: bfloat16 [2048, 256], P(('seq', 'batch')), may hold values from -0.125 to 0.125
- span_chooser_final: bfloat16 [256, 4], P(('seq', 'batch')), may hold values from -0.375 to 0.375
- heat_divisor: float32 [1], replicated, may hold values from 0.7 to 1.4
- sample_channel_fourths: int32 [8], P('batch'), may hold values from 1 to 4
- element_preset_span: int32 [1024, 8], P('seq', 'batch'), may hold values from 0 to 4, as said below
- spot_group_table: int32 [8], replicated, may hold values from 0 to 7, each once
Outputs:
- output: bfloat16 [1024, 8, 2048], P('seq', 'batch')
- grad_tokens: bfloat16 [1024, 8, 2048], P('seq', 'batch')
- grad_gain_attn: float32 [2048], P(('seq', 'batch'))
- grad_w_qkv: float32 [2048, 6144], P(('seq', 'batch'))
- grad_w_out: float32 [2048, 2048], P(('seq', 'batch'))
- grad_gain_ffn: float32 [2048], P(('seq', 'batch'))
- grad_bias_ffn: float32 [2048], P(('seq', 'batch'))
- grad_w_up: float32 [2048, 8192], P(('seq', 'batch'))
- grad_w_down: float32 [8192, 2048], P(('seq', 'batch'))
- grad_router_in: float32 [2048, 256], P(('seq', 'batch'))
- grad_router_out: float32 [256, 4], P(('seq', 'batch'))
The draws below stay inside these ranges and needn't reach their ends.
Inputs may be any that keep to these rules, and one draw needn't show every extreme that they name: A permutation: index j of seq holds block spot_group_table[j] of the positions of every sequence. `element_preset_span`: 0 lets the router mix the widths; k > 0 gives the token the k-th nested width, its first k * 2048 hidden units.
All inputs are finite; a program needn't handle non-finite values.
Results may differ from the reference program's by a relative error of at most 0.02.
Values may be sent and summed in bfloat16 or wider, within the bound.
No kernel may reach another device: no remote copies, remote signals or barrier semaphores. Data moves between devices by JAX's collectives and lax.ppermute only.
A program may use at most 576 MiB of HBM per device.

```python
import math
import jax
import jax.numpy as jnp
from jax import lax

D = 2048
H = 16
HD = 128
FF = 8192
RH = 256
BLOCK = 128
LENGTH = 1024
SEQS = 8
N_SEQ = 8


def draw_element_preset_span(key, part):
    key = jax.random.fold_in(key, 7)
    pick_key, width_key = jax.random.split(key)
    picked = jax.random.randint(pick_key, (LENGTH, SEQS), 0, 4)
    widths = jax.random.randint(width_key, (LENGTH, SEQS), 1, 5)
    return jnp.where(picked == 0, widths, 0).astype(jnp.int32)


def place_ends(array, rng, least, high):
    index_at = [jax.random.randint(jax.random.fold_in(rng, axis), (), 0, length) for axis, length in enumerate(array.shape)]
    main_axis = array.shape.index(max(array.shape))
    next_to = index_at[:main_axis] + [(index_at[main_axis] + 1) % array.shape[main_axis]] + index_at[main_axis + 1:]
    return array.at[tuple(index_at)].set(least).at[tuple(next_to)].set(high)


def steps_of(stream_key, shape, pieces, smallest, high):
    gain, own = 1.0, jax.random.fold_in(stream_key, 6)
    for position, shards_of in pieces:
        heights = jnp.exp(jax.random.uniform(jax.random.fold_in(own, position), (shards_of,), jnp.float32, smallest / len(pieces), high / len(pieces)))
        gain = gain * jnp.repeat(heights, shape[position] // shards_of).reshape([-1 if axis == position else 1 for axis in range(len(shape))])
    return gain


def bell_draw(rng, extent, spread, limit, cuts=(), held_as=jnp.bfloat16):
    values = jax.random.normal(rng, extent, jnp.float32) * spread
    if len(cuts) > 0:
        values = steps_of(rng, extent, cuts, -0.22, 0.18) * values
    return jnp.clip(values, min=-limit, max=limit).astype(held_as)


def setup_inputs(seed: int = 0) -> dict:
    key_of = jax.random.split(jax.random.key(seed), 16)
    return {
        "layer_entries": bell_draw(key_of[0], (LENGTH, SEQS, D), 1.0, 6.0, ((0, 8), (1, 4))),
        "incoming_adjoint": bell_draw(key_of[1], (LENGTH, SEQS, D), 1.0, 6.0, ((0, 8), (1, 4))),
        "mixing_rescale_scalers": jnp.clip(1.0 + 0.1 * jax.random.normal(key_of[2], (D,), jnp.float32), 0.5, 1.5).astype(jnp.bfloat16),
        "triple_projector_matrix": bell_draw(key_of[3], (D, 3 * D), (D // 2) ** -0.5, 0.1875, ((0, 32),)),
        "context_exit_matrix": bell_draw(key_of[4], (D, D), (D // 16) ** -0.5, 0.5, ((0, 32),)),
        "dense_center_scaler": jnp.clip(1.0 + 0.1 * jax.random.normal(key_of[5], (D,), jnp.float32), 0.5, 1.5).astype(jnp.bfloat16),
        "dense_center_offset": bell_draw(key_of[6], (D,), 0.3, 1.5, ((0, 32),)),
        "expand_matrix": bell_draw(key_of[7], (D, FF), D ** -0.5, 0.125, ((0, 32),)),
        "shrink_matrix": bell_draw(key_of[8], (FF, D), FF ** -0.5, 0.0625, ((0, 32),)),
        "span_chooser_initial": bell_draw(key_of[9], (D, RH), D ** -0.5, 0.125, ((0, 32),)),
        "span_chooser_final": bell_draw(key_of[10], (RH, 4), RH ** -0.5, 0.375, ((0, 32),)),
        "heat_divisor": jnp.clip(jax.random.uniform(key_of[11], (1,), jnp.float32, 0.7, 1.4), 0.7, 1.4),
        "sample_channel_fourths": place_ends(jax.random.randint(key_of[12], (SEQS,), 1, 5), jax.random.fold_in(key_of[12], 1), 1, 4).astype(jnp.int32),
        "element_preset_span": draw_element_preset_span(jax.random.fold_in(key_of[15], 71), 0),
        "spot_group_table": jax.random.permutation(key_of[14], N_SEQ).astype(jnp.int32),
    }


@jax.custom_vjp
def low(v):
    return lax.optimization_barrier(v.astype(jnp.bfloat16)).astype(jnp.float32)

@jax.custom_vjp
def low_back(v):
    return v

def low_keep(v):
    return (low(v), None)

def low_pass(kept, grad):
    return (grad,)

def back_keep(v):
    return (v, None)

def back_low(kept, grad):
    return (low(grad),)
low.defvjp(low_keep, low_pass)
low_back.defvjp(back_keep, back_low)
epsilon = 1e-05
theta_base = 10000.0
neg_large = -1e+30

def matmul_hi(left_mat, right_mat):
    return jnp.dot(left_mat, right_mat, precision=lax.Precision.HIGHEST, preferred_element_type=jnp.float32)

def rotate_half(values):
    lead_half, tail_half = jnp.split(values, 2, axis=-1)
    return jnp.concatenate([-tail_half, lead_half], axis=-1)

def rotary(values, positions):
    half_dim = HD // 2
    inverse = theta_base ** (-(jnp.arange(half_dim).astype(jnp.float32) * (2.0 / HD)))
    angles = positions.astype(jnp.float32)[:, None] * inverse[None, :]
    cosine_table = jnp.concatenate([jnp.cos(angles), jnp.cos(angles)], axis=1)[:, None, :]
    sine_table = jnp.concatenate([jnp.sin(angles), jnp.sin(angles)], axis=1)[:, None, :]
    return values * cosine_table + rotate_half(values) * sine_table

def attention(queries, keys, values, positions):
    length = queries.shape[0]
    row_block = math.gcd(512, length)
    score_scale = 1.0 / math.sqrt(HD)

    def one_block(block_args):
        query_part, place_part = block_args
        scores = jnp.einsum('qhd,khd->hqk', query_part, keys, precision=lax.Precision.HIGHEST) * score_scale
        scores = low_back(scores)
        allowed = positions[None, :] <= place_part[:, None]
        masked = jnp.where(allowed[None, :, :], scores, neg_large)
        probs = low(jax.nn.softmax(masked, axis=-1))
        return jnp.einsum('hqk,khd->qhd', probs, values, precision=lax.Precision.HIGHEST)
    blocks_out = lax.map(jax.checkpoint(one_block), (queries.reshape(length // row_block, row_block, H, HD), positions.reshape(length // row_block, row_block)))
    return blocks_out.reshape(length, H, HD)

def layer(params, inputs, positions, active, forced, smoothing_coefficient):
    mixing_rescale_scalers, triple_projector_matrix, context_exit_matrix, dense_center_scaler, dense_center_offset, expand_matrix, shrink_matrix, span_chooser_initial, span_chooser_final = params
    length = inputs.shape[0]
    inv_rms = lax.rsqrt(lax.optimization_barrier(jnp.mean(inputs * inputs, axis=1, keepdims=True)) + epsilon)
    normed = low(inputs * inv_rms * mixing_rescale_scalers)
    joint = low_back(matmul_hi(normed, triple_projector_matrix))
    query_raw, key_raw, value_raw = jnp.split(joint, 3, axis=1)
    queries = low(rotary(query_raw.reshape(length, H, HD), positions))
    keys = low(rotary(key_raw.reshape(length, H, HD), positions))
    values = low(value_raw.reshape(length, H, HD))
    heads_out = attention(queries, keys, values, positions) * active[None, :, None]
    attended = low(low_back(heads_out.reshape(length, D)))
    hidden = inputs + low_back(matmul_hi(attended, context_exit_matrix))
    centre = lax.optimization_barrier(jnp.mean(hidden, axis=1, keepdims=True))
    centered = hidden - centre
    variance = lax.optimization_barrier(jnp.mean(centered * centered, axis=1, keepdims=True))
    normal = centered * lax.rsqrt(variance + epsilon)
    ffn_in = low(normal * dense_center_scaler + dense_center_offset)
    pre_gate = low_back(matmul_hi(ffn_in, span_chooser_initial))
    squashed = low(jnp.tanh(pre_gate))
    logits = low_back(matmul_hi(squashed, span_chooser_final))
    routed = jax.nn.softmax(logits / smoothing_coefficient, axis=1)
    chosen = (forced[:, None] - 1 == jnp.arange(4)[None, :]).astype(jnp.float32)
    width_mix = jnp.where(forced[:, None] > 0, chosen, routed)
    upper_ones = (jnp.arange(4)[:, None] >= jnp.arange(4)[None, :]).astype(jnp.float32)
    band_scale = matmul_hi(width_mix, upper_ones)
    up_proj = low_back(matmul_hi(ffn_in, expand_matrix))
    rectified = jnp.maximum(up_proj, 0.0)
    activated = (rectified * rectified).reshape(length, 4, FF // 4) * band_scale[:, :, None]
    gated_act = low(activated.reshape(length, FF))
    return hidden + matmul_hi(gated_act, shrink_matrix)

def reference(layer_entries, incoming_adjoint, mixing_rescale_scalers, triple_projector_matrix, context_exit_matrix, dense_center_scaler, dense_center_offset, expand_matrix, shrink_matrix, span_chooser_initial, span_chooser_final, heat_divisor, sample_channel_fourths, element_preset_span, spot_group_table):
    row_ids = jnp.arange(LENGTH).astype(jnp.int32)
    positions = (spot_group_table[row_ids // BLOCK] * BLOCK + row_ids % BLOCK).astype(jnp.int32)
    params = tuple((weight.astype(jnp.float32) for weight in (mixing_rescale_scalers, triple_projector_matrix, context_exit_matrix, dense_center_scaler, dense_center_offset, expand_matrix, shrink_matrix, span_chooser_initial, span_chooser_final)))
    smoothing_coefficient = heat_divisor[0]
    head_band = (jnp.arange(H) // (H // 4)).astype(jnp.int32)

    def per_sequence(totals, seq_item):
        seq_inputs, seq_cot, groups, seq_forced = seq_item
        active = (head_band < groups).astype(jnp.float32)

        def run_layer(weights_tuple, layer_in):
            return layer(weights_tuple, layer_in, positions, active, seq_forced, smoothing_coefficient)
        seq_out, pullback = jax.vjp(run_layer, params, seq_inputs)
        grads, grad_in = pullback(seq_cot)
        totals = jax.tree.map(jnp.add, totals, grads)
        return (totals, (seq_out, grad_in))
    zero_grads = jax.tree.map(jnp.zeros_like, params)
    seq_items = (jnp.transpose(layer_entries.astype(jnp.float32), (1, 0, 2)), jnp.transpose(incoming_adjoint.astype(jnp.float32), (1, 0, 2)), sample_channel_fourths, jnp.transpose(element_preset_span, (1, 0)))
    totals, (outputs, grads_in) = lax.scan(per_sequence, zero_grads, seq_items)
    output = jnp.transpose(outputs, (1, 0, 2)).astype(jnp.bfloat16)
    grad_tokens = jnp.transpose(grads_in, (1, 0, 2)).astype(jnp.bfloat16)
    return (output, grad_tokens, totals[0], totals[1], totals[2], totals[3], totals[4], totals[5], totals[6], totals[7], totals[8])
```

```python
import functools
import math

import jax
import jax.numpy as jnp
from jax import lax
from jax.experimental import pallas as pl
from jax.experimental.pallas import tpu as pltpu
from jax.sharding import Mesh, PartitionSpec as P

H = 16
HD = 128
FF = 8192
RH = 256
RING = 4
SEQS = 2
GROUP_HEADS = H // RING
GROUP_WIDTH = GROUP_HEADS * HD
SCALE = 1.0 / math.sqrt(HD)
VMEM_LIMIT = 48 * 1024 * 1024

epsilon = 1e-05
theta_base = 10000.0
neg_large = -1e30
bf16 = jnp.bfloat16
f32 = jnp.float32
PLANE = ("yb", "bx", "bc")
EVERY = ("za",) + PLANE
SWAP = [(0, 1), (1, 0)]


def dot(left_mat, right_mat):
    return lax.dot_general(
        left_mat, right_mat, (((1,), (0,)), ((), ())), preferred_element_type=f32
    )


def dot_rows(left_mat, right_mat):
    return lax.dot_general(
        left_mat, right_mat, (((0,), (0,)), ((), ())), preferred_element_type=f32
    )


def dot_cols(left_mat, right_mat):
    return lax.dot_general(
        left_mat, right_mat, (((1,), (1,)), ((), ())), preferred_element_type=f32
    )


def onward(block, axis):
    size = lax.axis_size(axis)
    return lax.ppermute(block, axis, [(i, (i + 1) % size) for i in range(size)])


def add_low(left, right):
    return (left.astype(f32) + right.astype(f32)).astype(left.dtype)


def ring_gather(block, axis):
    slots = [block]
    for _ in range(1, lax.axis_size(axis)):
        slots.append(onward(slots[-1], axis))
    return slots


def ring_scatter(parts, axis):
    running = parts[1]()
    for slot in range(2, lax.axis_size(axis)):
        moved = onward(running, axis)
        running = add_low(parts[slot](), moved)
    moved = onward(running, axis)
    return parts[0]().astype(f32) + moved.astype(f32)


EARLY = [(0, 0, 0), (0, 1, 0), (1, 0, 0), (1, 0, 1)]
LATE = [(0, 0, 1), (0, 1, 1), (1, 1, 0), (1, 1, 1)]
CHUNKS = [(h, x, y, c) for c in (0, 1) for h, x, y in EARLY + LATE]


def swap(block, axis):
    return lax.ppermute(block, axis, SWAP)


def plane_gather(block):
    half = block.shape[0] // 2
    first, second = block[:half], block[half:]
    early = jnp.concatenate(
        [first, swap(first, "bx"), second, swap(second, "yb")], axis=0
    )
    late = jnp.concatenate(
        [swap(early[: 2 * half], "yb"), swap(early[2 * half :], "bx")], axis=0
    )
    return jnp.concatenate([early, late, swap(early, "bc"), swap(late, "bc")], axis=0)


def plane_scatter(chunks):
    both = add_low(chunks[:8], swap(chunks[8:], "bc"))
    first = add_low(both[0:2], swap(both[4:6], "yb"))
    second = add_low(both[2:4], swap(both[6:8], "bx"))
    first_sum = first[0].astype(f32) + swap(first[1], "bx").astype(f32)
    second_sum = second[0].astype(f32) + swap(second[1], "yb").astype(f32)
    return jnp.stack([first_sum, second_sum])


def rope_kernel(joint_ref, cos_ref, sin_ref, query_ref, key_ref, value_ref):
    cosine, sine = cos_ref[0], sin_ref[0]
    for head in range(GROUP_HEADS):
        for part, out_ref in ((0, query_ref), (1, key_ref)):
            at = part * GROUP_WIDTH + head * HD
            raw = joint_ref[0, 0, :, at : at + HD]
            turned = raw * cosine + pltpu.roll(raw, HD // 2, 1) * sine
            out_ref[0, 0, :, head * HD : (head + 1) * HD] = turned.astype(bf16)
    value_ref[0, 0] = joint_ref[0, 0, :, 2 * GROUP_WIDTH :].astype(bf16)


def rope(joint, cosine, sine):
    slots, seqs, block_len, width = joint.shape
    rows = lambda w: pl.BlockSpec((1, 1, block_len, w), lambda s, b: (s, b, 0, 0))
    table = pl.BlockSpec((1, block_len, HD), lambda s, b: (s, 0, 0))
    out = jax.ShapeDtypeStruct((slots, seqs, block_len, GROUP_WIDTH), bf16)
    return pl.pallas_call(
        rope_kernel,
        grid=(slots, seqs),
        in_specs=[rows(width), table, table],
        out_specs=[rows(GROUP_WIDTH)] * 3,
        out_shape=[out] * 3,
        compiler_params=pltpu.CompilerParams(vmem_limit_bytes=VMEM_LIMIT),
        name="rope",
    )(joint, cosine, sine)


def rope_back_kernel(*refs):
    dq_ref, dk_ref, dv_ref, mk_ref, mv_ref, cos_ref, sin_ref, out_ref = refs
    cosine, sine = cos_ref[0], sin_ref[0]
    for head in range(GROUP_HEADS):
        at = slice(head * HD, (head + 1) * HD)
        grad_query = dq_ref[0, 0, :, at]
        grad_key = dk_ref[0, 0, :, at].astype(f32) + mk_ref[0, 0, :, at].astype(f32)
        for part, grad in ((0, grad_query), (1, grad_key)):
            turned = grad * cosine - pltpu.roll(grad, HD // 2, 1) * sine
            start = part * GROUP_WIDTH + head * HD
            out_ref[0, 0, :, start : start + HD] = turned.astype(bf16)
    out_ref[0, 0, :, 2 * GROUP_WIDTH :] = (
        dv_ref[0, 0].astype(f32) + mv_ref[0, 0].astype(f32)
    ).astype(bf16)


def rope_back(grads, cosine, sine):
    slots, seqs, block_len, _ = grads[0].shape
    rows = lambda w: pl.BlockSpec((1, 1, block_len, w), lambda s, b: (s, b, 0, 0))
    table = pl.BlockSpec((1, block_len, HD), lambda s, b: (s, 0, 0))
    return pl.pallas_call(
        rope_back_kernel,
        grid=(slots, seqs),
        in_specs=[rows(GROUP_WIDTH)] * 5 + [table, table],
        out_specs=rows(3 * GROUP_WIDTH),
        out_shape=jax.ShapeDtypeStruct(
            (slots, seqs, block_len, 3 * GROUP_WIDTH), bf16
        ),
        compiler_params=pltpu.CompilerParams(vmem_limit_bytes=VMEM_LIMIT),
        name="rope_back",
    )(*grads, cosine, sine)


def flat(ref):
    slots, _, block_len, width = ref.shape
    return ref[:, 0].reshape(slots * block_len, width)


def attend_kernel(pieces, *refs):
    active_ref, query_ref = refs[:2]
    key_refs, value_refs = refs[2 : 2 + pieces], refs[2 + pieces : 2 + 2 * pieces]
    qplace_ref, kplace_ref, out_ref, low_ref, log_ref = refs[2 + 2 * pieces :]
    queries = flat(query_ref)
    query_places = qplace_ref[...]
    masked = []
    for piece, key_ref in enumerate(key_refs):
        scores = dot_cols(queries, flat(key_ref)) * SCALE
        allowed = kplace_ref[piece] <= query_places
        masked.append(jnp.where(allowed, scores, neg_large))
    top = functools.reduce(
        jnp.maximum, [jnp.max(m, axis=1, keepdims=True) for m in masked]
    )
    total, gathered = 0.0, 0.0
    for scores, value_ref in zip(masked, value_refs):
        weights = jnp.exp(scores - top)
        total = total + jnp.sum(weights, axis=1, keepdims=True)
        gathered = gathered + dot(weights.astype(bf16), flat(value_ref))
    result = gathered / total
    out_ref[:, 0] = result.reshape(out_ref.shape[0], out_ref.shape[2], HD)
    kept = active_ref[pl.program_id(0)]
    low_ref[:, 0] = (
        (result * kept).astype(bf16).reshape(out_ref.shape[0], out_ref.shape[2], HD)
    )
    log_ref[0, 0] = top + jnp.log(total)


def attend(active, queries, keys, values, query_places, key_places):
    slots, seqs, block_len, width = queries.shape
    rows = slots * block_len
    heads = width // HD
    pieces = len(keys)
    tile = pl.BlockSpec((slots, 1, block_len, HD), lambda s, h: (0, s, 0, h))
    return pl.pallas_call(
        functools.partial(attend_kernel, pieces),
        grid=(seqs, heads),
        in_specs=[pl.BlockSpec(memory_space=pltpu.SMEM)]
        + [tile] * (1 + 2 * pieces)
        + [
            pl.BlockSpec((rows, 1), lambda s, h: (0, 0)),
            pl.BlockSpec((pieces, 1, rows), lambda s, h: (0, 0, 0)),
        ],
        out_specs=[
            tile,
            tile,
            pl.BlockSpec((1, 1, rows, 1), lambda s, h: (s, h, 0, 0)),
        ],
        out_shape=[
            jax.ShapeDtypeStruct(queries.shape, f32),
            jax.ShapeDtypeStruct(queries.shape, bf16),
            jax.ShapeDtypeStruct((seqs, heads, rows, 1), f32),
        ],
        compiler_params=pltpu.CompilerParams(vmem_limit_bytes=VMEM_LIMIT),
        name="attend",
    )(active, queries, *keys, *values, query_places, key_places)


def attend_back_kernel(pieces, *refs):
    query_ref = refs[0]
    key_refs, value_refs = refs[1 : 1 + pieces], refs[1 + pieces : 1 + 2 * pieces]
    rest = refs[1 + 2 * pieces :]
    grad_ref, out_ref, log_ref, qplace_ref, kplace_ref, dq_ref = rest[:6]
    dk_refs, dv_refs = rest[6 : 6 + pieces], rest[6 + pieces :]
    queries, grads = flat(query_ref), flat(grad_ref)
    query_places = qplace_ref[...]
    dots = jnp.sum(grads.astype(f32) * flat(out_ref), axis=1, keepdims=True)
    log_norm = log_ref[0, 0]
    grad_query = 0.0
    shape = (query_ref.shape[0], query_ref.shape[2], HD)
    for piece in range(pieces):
        keys, values = flat(key_refs[piece]), flat(value_refs[piece])
        scores = dot_cols(queries, keys) * SCALE
        allowed = kplace_ref[piece] <= query_places
        probs = jnp.exp(jnp.where(allowed, scores - log_norm, neg_large))
        grad_probs = dot_cols(grads, values)
        dv_refs[piece][:, 0] = (
            dot_rows(probs.astype(bf16), grads)
            .astype(dv_refs[piece].dtype)
            .reshape(shape)
        )
        grad_scores = (probs * (grad_probs - dots)).astype(bf16)
        dk_refs[piece][:, 0] = (
            (dot_rows(grad_scores, queries) * SCALE)
            .astype(dk_refs[piece].dtype)
            .reshape(shape)
        )
        grad_query = grad_query + dot(grad_scores, keys)
    dq_ref[:, 0] = (grad_query * SCALE).reshape(shape)


def attend_back(queries, keys, values, grads, out, logs, query_places, key_places):
    slots, seqs, block_len, width = queries.shape
    rows = slots * block_len
    heads = width // HD
    pieces = len(keys)
    tile = pl.BlockSpec((slots, 1, block_len, HD), lambda s, h: (0, s, 0, h))
    wide = jax.ShapeDtypeStruct(queries.shape, f32)
    low = jax.ShapeDtypeStruct(queries.shape, bf16)
    found = pl.pallas_call(
        functools.partial(attend_back_kernel, pieces),
        grid=(seqs, heads),
        in_specs=[tile] * (3 + 2 * pieces)
        + [
            pl.BlockSpec((1, 1, rows, 1), lambda s, h: (s, h, 0, 0)),
            pl.BlockSpec((rows, 1), lambda s, h: (0, 0)),
            pl.BlockSpec((pieces, 1, rows), lambda s, h: (0, 0, 0)),
        ],
        out_specs=[tile] * (1 + 2 * pieces),
        out_shape=[wide] + ([wide] + [low] * (pieces - 1)) * 2,
        compiler_params=pltpu.CompilerParams(vmem_limit_bytes=VMEM_LIMIT),
        name="attend_back",
    )(queries, *keys, *values, grads, out, logs, query_places, key_places)
    return found[0], found[1 : 1 + pieces], found[1 + pieces :]


def per_device(
    layer_entries,
    incoming_adjoint,
    mixing_rescale_scalers,
    triple_projector_matrix,
    context_exit_matrix,
    dense_center_scaler,
    dense_center_offset,
    expand_matrix,
    shrink_matrix,
    span_chooser_initial,
    span_chooser_final,
    heat_divisor,
    sample_channel_fourths,
    element_preset_span,
    spot_group_table,
):
    block_len, seqs, width = layer_entries.shape
    tokens = block_len * seqs
    ring, plane = lax.axis_size("za"), lax.axis_size("yb")
    cores = lax.axis_size("bc")
    group = plane * lax.axis_size("bx") * cores
    devices = ring * group
    paired = plane == 2 and lax.axis_size("bx") == 2 and cores == 2
    za, yb = lax.axis_index("za"), lax.axis_index("yb")
    bx, bc = lax.axis_index("bx"), lax.axis_index("bc")
    rows = width // devices
    hidden_rows = FF // devices
    out_rows = span_chooser_final.shape[0] * 4

    def home(array):
        return jnp.transpose(array, (1, 0, 2)).reshape(tokens, width)

    def back(array):
        return jnp.transpose(array.reshape(seqs, block_len, width), (1, 0, 2))

    entries, adjoint = home(layer_entries), home(incoming_adjoint)

    vector = jnp.concatenate(
        [
            mixing_rescale_scalers,
            dense_center_scaler,
            dense_center_offset,
            span_chooser_final.reshape(-1),
            jnp.zeros((RH - 3 * rows - out_rows,), bf16),
        ]
    )
    forced_home = jnp.transpose(element_preset_span, (1, 0)).reshape(tokens)
    pad_rows = -(rows + 2) % 16
    pack_rows = rows + 2 + pad_rows
    pack = jnp.concatenate(
        [
            span_chooser_initial,
            vector[None],
            forced_home.astype(bf16).reshape(1, RH),
            jnp.zeros((pad_rows, RH), bf16),
        ],
        axis=0,
    )
    packs = lax.all_gather(pack, EVERY, axis=0, tiled=False)
    route_in = packs[:, :rows].reshape(width, RH)
    vectors = packs[:, rows]
    gain_one = vectors[:, :rows].reshape(1, width).astype(f32)
    gain_two = vectors[:, rows : 2 * rows].reshape(1, width).astype(f32)
    bias_two = vectors[:, 2 * rows : 3 * rows].reshape(1, width).astype(f32)
    route_out = vectors[:, 3 * rows : 3 * rows + out_rows].reshape(RH, 4)
    forced_all = packs[:, rows + 1]

    qkv_cut = jnp.transpose(
        triple_projector_matrix.reshape(rows, 3, ring, GROUP_WIDTH), (2, 0, 1, 3)
    ).reshape(ring, rows, 3 * GROUP_WIDTH)
    qkv_cut = lax.all_to_all(qkv_cut, "za", 0, 0, tiled=True)
    qkv_own = lax.all_gather(qkv_cut, PLANE, axis=1, tiled=False).reshape(
        width, 3 * GROUP_WIDTH
    )
    out_own = lax.all_gather(context_exit_matrix, PLANE, axis=0, tiled=True)
    up_cut = jnp.transpose(
        expand_matrix.reshape(rows, ring, group, hidden_rows), (2, 0, 1, 3)
    ).reshape(group, rows, ring * hidden_rows)
    up_cut = lax.all_to_all(up_cut, PLANE, 0, 0, tiled=True)
    up_own = lax.all_gather(
        up_cut.reshape(group * rows, ring * hidden_rows), "za", axis=0, tiled=True
    )
    down_own = lax.all_gather(shrink_matrix, "za", axis=0, tiled=True)

    slot_ids = jnp.arange(ring, dtype=jnp.int32)
    table_ids = jnp.arange(spot_group_table.shape[0], dtype=jnp.int32)

    def places_of(piece):
        index = ((za - slot_ids) % ring) * plane + (yb - piece) % plane
        spots = jnp.sum(
            jnp.where(index[:, None] == table_ids[None, :], spot_group_table, 0), axis=1
        )
        return spots[:, None] * block_len + jnp.arange(block_len, dtype=jnp.int32)

    all_places = [places_of(piece) for piece in range(plane)]
    query_places = all_places[0].reshape(ring * block_len, 1)
    key_places = jnp.stack(all_places).reshape(plane, 1, ring * block_len)
    half = HD // 2
    inverse = theta_base ** (-(jnp.arange(half, dtype=f32) * (2.0 / HD)))
    angles = all_places[0].astype(f32)[:, :, None] * inverse
    cosine = jnp.concatenate([jnp.cos(angles), jnp.cos(angles)], axis=-1)
    sine = jnp.concatenate([-jnp.sin(angles), jnp.sin(angles)], axis=-1)
    active = (za < sample_channel_fourths).astype(f32)
    active_rows = jnp.broadcast_to(
        active[None, :, None, None], (ring, seqs, block_len, 1)
    ).reshape(ring * tokens, 1)

    entry_slots = jnp.concatenate(ring_gather(entries, "za"), axis=0).astype(f32)
    inv_rms = lax.rsqrt(
        jnp.mean(entry_slots * entry_slots, axis=1, keepdims=True) + epsilon
    )
    scaled_slots = entry_slots * inv_rms
    normed = (scaled_slots * gain_one).astype(bf16)
    joint = dot(normed, qkv_own).reshape(ring, seqs, block_len, 3 * GROUP_WIDTH)
    queries, keys, values = rope(joint, cosine, sine)
    all_keys = ring_gather(keys, "yb")
    all_values = ring_gather(values, "yb")
    heads_out, attended, logs = attend(
        active, queries, all_keys, all_values, query_places, key_places
    )
    attended = attended.reshape(ring * tokens, GROUP_WIDTH)
    inputs = entries.astype(f32)
    hidden = inputs + ring_scatter(
        [
            lambda s=s: dot(attended[s * tokens : (s + 1) * tokens], out_own).astype(
                bf16
            )
            for s in range(ring)
        ],
        "za",
    )

    centre = jnp.mean(hidden, axis=1, keepdims=True)
    centered = hidden - centre
    variance = jnp.mean(centered * centered, axis=1, keepdims=True)
    inv_std = lax.rsqrt(variance + epsilon)
    normal = centered * inv_std
    ffn_in = (normal * gain_two + bias_two).astype(bf16)

    if paired:
        spread, gather_back = (
            plane_gather,
            lambda terms: plane_scatter(
                terms.reshape((16, block_len) + terms.shape[1:])
            ).reshape((tokens,) + terms.shape[1:]),
        )
        at = jnp.stack(
            [
                (
                    (za * group + ((yb ^ y) * 2 + (bx ^ x)) * 2 + (bc ^ c)) * seqs + h
                ).astype(jnp.int32)
                for h, x, y, c in CHUNKS
            ]
        )
    else:
        spread = lambda block: lax.all_gather(block, PLANE, axis=0, tiled=True)
        gather_back = lambda terms: lax.psum_scatter(
            terms, PLANE, scatter_dimension=0, tiled=True
        ).astype(f32)
        at = za * group * seqs + jnp.arange(group * seqs, dtype=jnp.int32)
    wide_in, wide_adjoint = spread(ffn_in), spread(adjoint)
    wide_tokens = wide_in.shape[0]
    picks = (at[:, None] == jnp.arange(devices * seqs)[None, :]).astype(bf16)
    wide_forced = dot(picks, forced_all.reshape(devices * seqs, block_len)).reshape(
        wide_tokens
    )

    temperature = heat_divisor[0]

    def router(block, forced):
        squashed = jnp.tanh(dot(block, route_in))
        logits = dot(squashed.astype(bf16), route_out)
        routed = jax.nn.softmax(logits / temperature, axis=1)
        is_forced = (forced > 0)[:, None]
        chosen = forced[:, None] - 1 == jnp.arange(4, dtype=forced.dtype)[None, :]
        mix = jnp.where(is_forced, chosen.astype(f32), routed)
        scale = jnp.stack(
            [
                mix[:, 0] + mix[:, 1] + mix[:, 2] + mix[:, 3],
                mix[:, 1] + mix[:, 2] + mix[:, 3],
                mix[:, 2] + mix[:, 3],
                mix[:, 3],
            ],
            axis=1,
        )
        return squashed, routed, is_forced, scale

    band_scale = router(wide_in, wide_forced)[3]
    scale_wide = jnp.broadcast_to(
        band_scale[:, :, None], (wide_tokens, 4, hidden_rows)
    ).reshape(wide_tokens, 4 * hidden_rows)

    rectified = jnp.maximum(dot(wide_in, up_own), 0.0)
    activated = rectified * rectified
    gated = (activated * scale_wide).astype(bf16)
    grad_gated = dot_cols(wide_adjoint, down_own)
    grad_up = (grad_gated * scale_wide * (2.0 * rectified)).astype(bf16)
    grad_band = jnp.sum(
        (grad_gated * activated).reshape(wide_tokens, 4, hidden_rows), axis=2
    )
    grad_in_terms = dot_cols(grad_up, up_own).astype(bf16)
    grad_ffn_in = gather_back(grad_in_terms)
    grad_band_home = gather_back(grad_band)
    output = hidden + gather_back(dot(gated, down_own).astype(bf16))
    result = back(output.astype(bf16))
    down_terms = dot_rows(gated, wide_adjoint).astype(bf16)
    up_terms = dot_rows(wide_in, grad_up).astype(bf16)
    grad_down = lax.psum_scatter(
        down_terms, "za", scatter_dimension=0, tiled=True
    ).astype(f32)
    up_terms = lax.psum_scatter(up_terms, "za", scatter_dimension=0, tiled=True)
    up_terms = lax.all_to_all(
        up_terms.reshape(group, rows, ring * hidden_rows), PLANE, 0, 0, tiled=True
    )
    grad_wup = (
        jnp.transpose(up_terms.reshape(group, rows, ring, hidden_rows), (1, 2, 0, 3))
        .reshape(rows, FF)
        .astype(f32)
    )

    squashed, routed, is_forced, _ = router(ffn_in, forced_home)
    grad_mix = jnp.cumsum(grad_band_home, axis=1)
    grad_logits = jnp.where(
        is_forced,
        0.0,
        routed
        * (grad_mix - jnp.sum(routed * grad_mix, axis=1, keepdims=True))
        / temperature,
    ).astype(bf16)
    grad_route_out = dot_rows(squashed.astype(bf16), grad_logits)
    grad_pre = (dot_cols(grad_logits, route_out) * (1.0 - squashed * squashed)).astype(
        bf16
    )
    grad_route_in = dot_rows(ffn_in, grad_pre)
    grad_ffn_in = grad_ffn_in + dot_cols(grad_pre, route_in)
    grad_gain_two = jnp.sum(grad_ffn_in * normal, axis=0)
    grad_bias_two = jnp.sum(grad_ffn_in, axis=0)
    grad_normal = grad_ffn_in * gain_two
    grad_hidden = adjoint.astype(f32) + inv_std * (
        grad_normal
        - jnp.mean(grad_normal, axis=1, keepdims=True)
        - normal * jnp.mean(grad_normal * normal, axis=1, keepdims=True)
    )
    small = jnp.concatenate(
        [
            grad_gain_two.reshape(devices, rows),
            grad_bias_two.reshape(devices, rows),
            grad_route_out.reshape(devices, out_rows),
            jnp.zeros((devices, RH - 2 * rows - out_rows), f32),
        ],
        axis=1,
    )
    small_rows = rows + 1 + (-(rows + 1) % 8)
    small_pack = jnp.concatenate(
        [
            grad_route_in.reshape(devices, rows, RH),
            small[:, None],
            jnp.zeros((devices, small_rows - rows - 1, RH), f32),
        ],
        axis=1,
    )
    small_sum = lax.psum_scatter(
        small_pack.reshape(devices * small_rows, RH),
        EVERY,
        scatter_dimension=0,
        tiled=True,
    )

    grad_attn = jnp.concatenate(ring_gather(grad_hidden.astype(bf16), "za"), axis=0)
    grad_heads = (
        (dot_cols(grad_attn, out_own) * active_rows)
        .astype(bf16)
        .reshape(ring, seqs, block_len, GROUP_WIDTH)
    )
    grad_query, grad_keys, grad_values = attend_back(
        queries,
        all_keys,
        all_values,
        grad_heads,
        heads_out,
        logs,
        query_places,
        key_places,
    )

    def from_others(grads):
        if plane == 1:
            return jnp.zeros_like(grads[0])
        running = grads[1]
        for slot in range(2, plane):
            running = add_low(grads[slot], onward(running, "yb"))
        return onward(running, "yb")

    grad_joint = rope_back(
        (
            grad_query,
            grad_keys[0],
            grad_values[0],
            from_others(grad_keys),
            from_others(grad_values),
        ),
        cosine,
        sine,
    ).reshape(ring * tokens, 3 * GROUP_WIDTH)
    grad_out_terms = dot_rows(attended, grad_attn).astype(bf16)
    grad_wout = lax.psum_scatter(
        grad_out_terms, PLANE, scatter_dimension=0, tiled=True
    ).astype(f32)
    normed_terms = dot_cols(grad_joint, qkv_own)
    grad_gain_terms = jnp.sum(normed_terms * scaled_slots, axis=0)
    gain_high = grad_gain_terms.astype(bf16)
    gain_low = (grad_gain_terms - gain_high.astype(f32)).astype(bf16)
    qkv_terms = jnp.concatenate(
        [
            dot_rows(normed, grad_joint).astype(bf16),
            gain_high[:, None],
            gain_low[:, None],
            jnp.zeros((width, HD - 2), bf16),
        ],
        axis=1,
    )
    wide_cols = 3 * GROUP_WIDTH + HD
    qkv_terms = lax.psum_scatter(
        qkv_terms.reshape(ring, group, rows, wide_cols),
        PLANE,
        scatter_dimension=1,
        tiled=False,
    )
    qkv_terms = lax.all_to_all(qkv_terms, "za", 0, 0, tiled=True).astype(f32)
    grad_wqkv = jnp.transpose(
        qkv_terms[:, :, : 3 * GROUP_WIDTH].reshape(ring, rows, 3, GROUP_WIDTH),
        (1, 2, 0, 3),
    ).reshape(rows, 3 * width)
    grad_gain_one = jnp.sum(
        qkv_terms[:, :, 3 * GROUP_WIDTH] + qkv_terms[:, :, 3 * GROUP_WIDTH + 1], axis=0
    )
    low_terms = normed_terms.astype(bf16)
    grad_normed = ring_scatter(
        [lambda s=s: low_terms[s * tokens : (s + 1) * tokens] for s in range(ring)],
        "za",
    )
    inv_home = lax.rsqrt(jnp.mean(inputs * inputs, axis=1, keepdims=True) + epsilon)
    scaled = inputs * inv_home
    grad_scaled = grad_normed * gain_one
    grad_inputs = grad_hidden + inv_home * (
        grad_scaled - scaled * jnp.mean(grad_scaled * scaled, axis=1, keepdims=True)
    )
    grad_tokens = back(grad_inputs.astype(bf16))
    return (
        result,
        grad_tokens,
        grad_gain_one,
        grad_wqkv,
        grad_wout,
        small_sum[rows, :rows],
        small_sum[rows, rows : 2 * rows],
        grad_wup,
        grad_down,
        small_sum[:rows],
        small_sum[rows, 2 * rows : 2 * rows + out_rows].reshape(out_rows // 4, 4),
    )


def solution(mesh):
    seq, batch = mesh.shape["seq"], mesh.shape["batch"]
    inner = Mesh(
        mesh.devices.reshape(RING, seq // RING, batch // 2, 2),
        ("za", "yb", "bx", "bc"),
    )
    along, across = ("za", "yb"), ("bx", "bc")
    tokens = P(along, across, None)
    vector = P(along + across)
    matrix = P(along + across, None)
    return jax.shard_map(
        per_device,
        mesh=inner,
        in_specs=(
            tokens,
            tokens,
            vector,
            matrix,
            matrix,
            vector,
            vector,
            matrix,
            matrix,
            matrix,
            matrix,
            P(),
            P(across),
            P(along, across),
            P(),
        ),
        out_specs=(
            tokens,
            tokens,
            vector,
            matrix,
            matrix,
            vector,
            vector,
            matrix,
            matrix,
            matrix,
            matrix,
        ),
        check_vma=False,
    )
```

```python
import functools
import math

import jax
import jax.numpy as jnp
from jax import lax
from jax.experimental import pallas as pl
from jax.experimental.pallas import tpu as pltpu
from jax.sharding import Mesh, PartitionSpec as P

H = 16
HD = 128
FF = 8192
RH = 256
RING = 4
SEQS = 2
GROUP_HEADS = H // RING
GROUP_WIDTH = GROUP_HEADS * HD
SCALE = 1.0 / math.sqrt(HD)
VMEM_LIMIT = 48 * 1024 * 1024
TILE = 256
LANES = 128

epsilon = 1e-05
theta_base = 10000.0
neg_large = -1e30
bf16 = jnp.bfloat16
f32 = jnp.float32
PLANE = ("yb", "bx", "bc")
EVERY = ("za",) + PLANE
SWAP = [(0, 1), (1, 0)]


def dot(left_mat, right_mat):
    return lax.dot_general(
        left_mat, right_mat, (((1,), (0,)), ((), ())), preferred_element_type=f32
    )


def dot_rows(left_mat, right_mat):
    return lax.dot_general(
        left_mat, right_mat, (((0,), (0,)), ((), ())), preferred_element_type=f32
    )


def dot_cols(left_mat, right_mat):
    return lax.dot_general(
        left_mat, right_mat, (((1,), (1,)), ((), ())), preferred_element_type=f32
    )


def onward(block, axis):
    size = lax.axis_size(axis)
    return lax.ppermute(block, axis, [(i, (i + 1) % size) for i in range(size)])


def after(value, *others):
    return lax.optimization_barrier((value, others))[0]


def add_low(left, right):
    return (left.astype(f32) + right.astype(f32)).astype(left.dtype)


def ring_gather(block, axis):
    slots = [block]
    for _ in range(1, lax.axis_size(axis)):
        slots.append(onward(slots[-1], axis))
    return slots


def ring_scatter(parts, axis, hops=None):
    running = parts[1]()
    for slot in range(2, lax.axis_size(axis)):
        moved = onward(running, axis)
        if hops is not None:
            hops.append(moved)
        running = add_low(parts[slot](), moved)
    moved = onward(running, axis)
    return parts[0]().astype(f32) + moved.astype(f32)


def in_order(slots, axis):
    size = lax.axis_size(axis)
    run = slots[::-1] + slots[:0:-1]
    rows = slots[0].shape[0]
    start = (size - 1 - lax.axis_index(axis)) * rows
    return lax.dynamic_slice_in_dim(
        jnp.concatenate(run, axis=0), start, size * rows, axis=0
    )


def gather_in_order(block, axis):
    return in_order(ring_gather(block, axis), axis)


def rotate(pieces, axis):
    size, me = lax.axis_size(axis), lax.axis_index(axis)
    came = [pieces(me)]
    for far in range(1, size):
        route = [(i, (i + far) % size) for i in range(size)]
        came.append(lax.ppermute(pieces((me + far) % size), axis, route))
    return came


def exchange(pieces, axis):
    return in_order(
        rotate(lambda i: lax.dynamic_index_in_dim(pieces, i, 0), axis), axis
    )


EARLY = [(0, 0, 0), (0, 1, 0), (1, 0, 0), (1, 0, 1)]
LATE = [(0, 0, 1), (0, 1, 1), (1, 1, 0), (1, 1, 1)]
CHUNKS = [(h, x, y, c) for part in (EARLY, LATE) for c in (0, 1) for h, x, y in part]


def swap(block, axis):
    return lax.ppermute(block, axis, SWAP)


def plane_gather(block, between=lambda early: ()):
    half = block.shape[0] // 2
    first, second = block[:half], block[half:]
    early = jnp.concatenate(
        [first, swap(first, "bx"), second, swap(second, "yb")], axis=0
    )
    late = jnp.concatenate(
        [swap(early[: 2 * half], "yb"), swap(early[2 * half :], "bx")], axis=0
    )
    groups = [(early, swap(early, "bc"))]
    late = after(late, between(groups[0]))
    return groups + [(late, swap(late, "bc"))]


def plane_scatter_late(terms):
    late = add_low(terms[0], swap(terms[1], "bc"))
    half = late.shape[0] // 2
    return late, swap(late[:half], "yb"), swap(late[half:], "bx")


def plane_scatter(terms, came):
    rows = terms[0].shape[0] // 4
    early = add_low(terms[0], swap(terms[1], "bc"))
    first = add_low(early[: 2 * rows], came[1])
    second = add_low(early[2 * rows :], came[2])
    first_sum = first[:rows].astype(f32) + swap(first[rows:], "bx").astype(f32)
    second_sum = second[:rows].astype(f32) + swap(second[rows:], "yb").astype(f32)
    return jnp.concatenate([first_sum, second_sum], axis=0)


def keep_and_swap(blocks, axis, dim):
    me = lax.axis_index(axis)
    kept = lax.dynamic_index_in_dim(blocks, me, dim, keepdims=False)
    sent = lax.dynamic_index_in_dim(blocks, 1 - me, dim, keepdims=False)
    return add_low(kept, swap(sent, axis))


def plane_reduce(blocks, steps=None):
    both = keep_and_swap(blocks, "bc", 3)
    middle = blocks.shape[-1] // 2
    first = keep_and_swap(both[..., :middle], "yb", 1)
    second = keep_and_swap(both[..., middle:], "bx", 2)
    if steps is not None:
        steps.extend([both, (first, second)])
    first = keep_and_swap(first, "bx", 1)
    second = keep_and_swap(second, "yb", 1)
    if steps is not None:
        steps.append((first, second))
    return jnp.concatenate([first, second], axis=-1)


def rope_kernel(joint_ref, cos_ref, sin_ref, query_ref, both_ref):
    cosine, sine = cos_ref[...], sin_ref[...]
    for head in range(GROUP_HEADS):
        for part, out_ref in ((0, query_ref), (1, both_ref)):
            at = part * GROUP_WIDTH + head * HD
            raw = joint_ref[0, :, at : at + HD]
            turned = raw * cosine + pltpu.roll(raw, HD // 2, 1) * sine
            out_ref[0, :, head * HD : (head + 1) * HD] = turned.astype(bf16)
    both_ref[0, :, GROUP_WIDTH:] = joint_ref[0, :, 2 * GROUP_WIDTH :].astype(bf16)


def rope(joint, cosine, sine):
    seqs, block_len, width = joint.shape
    rows = lambda w: pl.BlockSpec((1, block_len, w), lambda b: (b, 0, 0))
    table = pl.BlockSpec((block_len, HD), lambda b: (0, 0))
    return pl.pallas_call(
        rope_kernel,
        grid=(seqs,),
        in_specs=[rows(3 * GROUP_WIDTH), table, table],
        out_specs=[rows(GROUP_WIDTH), rows(2 * GROUP_WIDTH)],
        out_shape=[
            jax.ShapeDtypeStruct((seqs, block_len, GROUP_WIDTH), bf16),
            jax.ShapeDtypeStruct((seqs, block_len, 2 * GROUP_WIDTH), bf16),
        ],
        compiler_params=pltpu.CompilerParams(vmem_limit_bytes=VMEM_LIMIT),
        name="rope",
    )(joint, cosine, sine)


def turn_back(grad, cosine, sine):
    return (grad * cosine - pltpu.roll(grad, HD // 2, 1) * sine).astype(bf16)


def query_back_kernel(terms, *refs):
    cos_ref, sin_ref, out_ref = refs[terms:]
    cosine, sine = cos_ref[0], sin_ref[0]
    for seq in range(out_ref.shape[1]):
        for head in range(GROUP_HEADS):
            at = slice(head * HD, (head + 1) * HD)
            grad = sum(ref[0, seq, :, at].astype(f32) for ref in refs[:terms])
            out_ref[0, seq, :, at] = turn_back(grad, cosine, sine)


def both_back_kernel(terms, *refs):
    key_refs, value_refs = refs[:terms], refs[terms : 2 * terms]
    cos_ref, sin_ref, _, out_ref = refs[2 * terms :]

    @pl.when(pl.program_id(1) == 0)
    def _():
        cosine, sine = cos_ref[0], sin_ref[0]
        for seq in range(out_ref.shape[1]):
            for head in range(GROUP_HEADS):
                at = slice(head * HD, (head + 1) * HD)
                grad = sum(ref[0, seq, :, at].astype(f32) for ref in key_refs)
                out_ref[0, seq, :, at] = turn_back(grad, cosine, sine)

    @pl.when(pl.program_id(1) == 1)
    def _():
        total = sum(ref[0].astype(f32) for ref in value_refs)
        out_ref[0] = total.astype(bf16)


def joint_shape(grad):
    return jax.ShapeDtypeStruct(grad.shape[:3] + (3 * GROUP_WIDTH,), bf16)


def query_back(grads, cosine, sine):
    slots, seqs, block_len, width = grads[0].shape
    rows = pl.BlockSpec((1, seqs, block_len, width), lambda s: (s, 0, 0, 0))
    table = pl.BlockSpec((1, block_len, HD), lambda s: (s, 0, 0))
    return pl.pallas_call(
        functools.partial(query_back_kernel, len(grads)),
        grid=(slots,),
        in_specs=[rows] * len(grads) + [table, table],
        out_specs=rows,
        out_shape=joint_shape(grads[0]),
        compiler_params=pltpu.CompilerParams(vmem_limit_bytes=VMEM_LIMIT),
        name="query_back",
    )(*grads, cosine, sine)


def both_back(keys, values, cosine, sine, joint):
    slots, seqs, block_len, width = keys[0].shape
    rows = pl.BlockSpec((1, seqs, block_len, width), lambda s, j: (s, 0, 0, 0))
    table = pl.BlockSpec((1, block_len, HD), lambda s, j: (s, 0, 0))
    terms = len(keys)
    return pl.pallas_call(
        functools.partial(both_back_kernel, terms),
        grid=(slots, 2),
        in_specs=[rows] * (2 * terms)
        + [table, table, pl.BlockSpec(memory_space=pl.ANY)],
        out_specs=pl.BlockSpec(
            (1, seqs, block_len, width), lambda s, j: (s, 0, 0, 1 + j)
        ),
        out_shape=joint_shape(keys[0]),
        input_output_aliases={2 * terms + 2: 0},
        compiler_params=pltpu.CompilerParams(vmem_limit_bytes=VMEM_LIMIT),
        name="both_back",
    )(*keys, *values, cosine, sine, joint)


def flat(ref):
    slots, _, block_len, width = ref.shape
    return ref[:, 0].reshape(slots * block_len, width)


def end_to_end(refs):
    return jnp.concatenate([ref[0] for ref in refs], axis=0)


def by_piece(refs, slots):
    return [refs[i : i + slots] for i in range(0, len(refs), slots)]


def attend_kernel(slots, pieces, *refs):
    active_ref, query_refs = refs[0], refs[1 : 1 + slots]
    rest = refs[1 + slots :]
    key_refs = by_piece(rest[: pieces * slots], slots)
    value_refs = by_piece(rest[pieces * slots : 2 * pieces * slots], slots)
    qplace_ref, kplace_ref, out_ref, low_ref, log_ref = rest[2 * pieces * slots :]
    queries = end_to_end(query_refs)
    query_places = qplace_ref[...]
    masked = []
    for piece in range(pieces):
        scores = dot_cols(queries, end_to_end(key_refs[piece])) * SCALE
        allowed = kplace_ref[piece] <= query_places
        masked.append(jnp.where(allowed, scores, neg_large))
    top = functools.reduce(
        jnp.maximum, [jnp.max(m, axis=1, keepdims=True) for m in masked]
    )
    total, gathered = 0.0, 0.0
    for piece in range(pieces):
        weights = jnp.exp(masked[piece] - top)
        total = total + jnp.sum(weights, axis=1, keepdims=True)
        gathered = gathered + dot(weights.astype(bf16), end_to_end(value_refs[piece]))
    result = gathered / total
    out_ref[:, 0] = result.reshape(out_ref.shape[0], out_ref.shape[2], HD)
    kept = active_ref[pl.program_id(0)]
    low_ref[:, 0] = (
        (result * kept).astype(bf16).reshape(out_ref.shape[0], out_ref.shape[2], HD)
    )
    log_ref[0, 0] = top + jnp.log(total)


def attend(active, queries, boths, query_places, key_places):
    slots, pieces = len(queries), len(boths)
    seqs, block_len, width = queries[0].shape
    rows = slots * block_len
    heads = width // HD
    own = pl.BlockSpec((1, block_len, HD), lambda s, h: (s, 0, h))
    value = pl.BlockSpec((1, block_len, HD), lambda s, h: (s, 0, heads + h))
    tile = pl.BlockSpec((slots, 1, block_len, HD), lambda s, h: (0, s, 0, h))
    every = [both for piece in boths for both in piece]
    shape = (slots, seqs, block_len, width)
    return pl.pallas_call(
        functools.partial(attend_kernel, slots, pieces),
        grid=(seqs, heads),
        in_specs=[pl.BlockSpec(memory_space=pltpu.SMEM)]
        + [own] * slots
        + [own] * len(every)
        + [value] * len(every)
        + [
            pl.BlockSpec((rows, 1), lambda s, h: (0, 0)),
            pl.BlockSpec((pieces, 1, rows), lambda s, h: (0, 0, 0)),
        ],
        out_specs=[
            tile,
            tile,
            pl.BlockSpec((1, 1, rows, 1), lambda s, h: (s, h, 0, 0)),
        ],
        out_shape=[
            jax.ShapeDtypeStruct(shape, f32),
            jax.ShapeDtypeStruct(shape, bf16),
            jax.ShapeDtypeStruct((seqs, heads, rows, 1), f32),
        ],
        compiler_params=pltpu.CompilerParams(vmem_limit_bytes=VMEM_LIMIT),
        name="attend",
    )(active, *queries, *every, *every, query_places, key_places)


def attend_back_kernel(slots, pieces, *refs):
    query_refs, rest = refs[:slots], refs[slots:]
    key_refs = by_piece(rest[: pieces * slots], slots)
    value_refs = by_piece(rest[pieces * slots : 2 * pieces * slots], slots)
    rest = rest[2 * pieces * slots :]
    grad_refs, rest = rest[:slots], rest[slots:]
    out_ref, log_ref, qplace_ref, kplace_ref, dq_ref = rest[:5]
    dk_refs, dv_refs = rest[5 : 5 + pieces], rest[5 + pieces :]
    queries, grads = end_to_end(query_refs), end_to_end(grad_refs)
    query_places = qplace_ref[...]
    dots = jnp.sum(grads.astype(f32) * flat(out_ref), axis=1, keepdims=True)
    log_norm = log_ref[0, 0]
    grad_query = 0.0
    shape = (slots, query_refs[0].shape[1], HD)
    for piece in range(pieces):
        keys, values = end_to_end(key_refs[piece]), end_to_end(value_refs[piece])
        scores = dot_cols(queries, keys) * SCALE
        allowed = kplace_ref[piece] <= query_places
        probs = jnp.exp(jnp.where(allowed, scores - log_norm, neg_large))
        grad_probs = dot_cols(grads, values)
        dv_refs[piece][:, 0] = (
            dot_rows(probs.astype(bf16), grads)
            .astype(dv_refs[piece].dtype)
            .reshape(shape)
        )
        grad_scores = (probs * (grad_probs - dots)).astype(bf16)
        dk_refs[piece][:, 0] = (
            (dot_rows(grad_scores, queries) * SCALE)
            .astype(dk_refs[piece].dtype)
            .reshape(shape)
        )
        grad_query = grad_query + dot(grad_scores, keys)
    dq_ref[:, 0] = (grad_query * SCALE).reshape(shape)


def attend_back(queries, boths, grads, out, logs, query_places, key_places, name):
    slots, pieces = len(queries), len(boths)
    seqs, block_len, width = queries[0].shape
    rows = slots * block_len
    heads = width // HD
    own = pl.BlockSpec((1, block_len, HD), lambda s, h: (s, 0, h))
    value = pl.BlockSpec((1, block_len, HD), lambda s, h: (s, 0, heads + h))
    tile = pl.BlockSpec((slots, 1, block_len, HD), lambda s, h: (0, s, 0, h))
    every = [both for piece in boths for both in piece]
    shape = (slots, seqs, block_len, width)
    wide = jax.ShapeDtypeStruct(shape, f32)
    low = jax.ShapeDtypeStruct(shape, bf16)
    found = pl.pallas_call(
        functools.partial(attend_back_kernel, slots, pieces),
        grid=(seqs, heads),
        in_specs=[own] * slots
        + [own] * len(every)
        + [value] * len(every)
        + [own] * slots
        + [
            tile,
            pl.BlockSpec((1, 1, rows, 1), lambda s, h: (s, h, 0, 0)),
            pl.BlockSpec((rows, 1), lambda s, h: (0, 0)),
            pl.BlockSpec((pieces, 1, rows), lambda s, h: (0, 0, 0)),
        ],
        out_specs=[tile] * (1 + 2 * pieces),
        out_shape=[wide] + [low] * (2 * pieces),
        compiler_params=pltpu.CompilerParams(vmem_limit_bytes=VMEM_LIMIT),
        name=name,
    )(*queries, *every, *every, *grads, out, logs, query_places, key_places)
    return found[0], found[1 : 1 + pieces], found[1 + pieces :]


def feed_up_kernel(steps, blocks, passed, *refs):
    in_refs, refs = refs[:blocks], refs[blocks:]
    heat_ref, forced_ref, route_in_ref, route_out_ref, up_ref = refs[:5]
    all_in_ref, gated_ref, scale_ref, rectified_ref = refs[5 + passed :]
    block = in_refs[0][...]
    for k in range(1, blocks):
        block = jnp.where(pl.program_id(0) < k * steps, block, in_refs[k][...])
    all_in_ref[...] = block
    units = up_ref.shape[1]
    band = units // 4

    squashed = jnp.tanh(dot(block, route_in_ref[...])).astype(bf16)
    logits = dot(squashed, route_out_ref[...]) / heat_ref[0]
    lane = lax.broadcasted_iota(jnp.int32, logits.shape, 1)
    logits = jnp.where(lane < 4, logits, neg_large)
    weights = jnp.exp(logits - jnp.max(logits, axis=1, keepdims=True))
    routed = weights / jnp.sum(weights, axis=1, keepdims=True)
    forced = forced_ref[...]
    chosen = jnp.where(lane.astype(f32) == forced - 1.0, 1.0, 0.0)
    mix = jnp.where(forced > 0.0, chosen, routed)
    scales = [mix[:, 3:4]]
    for k in (2, 1, 0):
        scales.insert(0, scales[0] + mix[:, k : k + 1])
    scale_ref[...] = by_lane(scales, scale_ref.shape)

    rectified = jnp.maximum(dot(block, up_ref[...]), 0.0)
    rectified_ref[...] = rectified
    gated_ref[...] = (rectified * rectified * by_band(scales, band, units)).astype(bf16)


def by_lane(columns, shape):
    lane = lax.broadcasted_iota(jnp.int32, shape, 1)
    found = jnp.zeros(shape, f32)
    for k, column in enumerate(columns):
        found = jnp.where(lane == k, column, found)
    return found


def by_band(columns, band, units):
    rows = columns[0].shape[0]
    if band % LANES == 0:
        return jnp.concatenate(
            [jnp.broadcast_to(column, (rows, band)) for column in columns], axis=1
        )
    at = lax.broadcasted_iota(jnp.int32, (rows, units), 1) // band
    found = jnp.broadcast_to(columns[3], (rows, units))
    for k in range(3):
        found = jnp.where(at == k, columns[k], found)
    return found


def band_sums(array, band):
    if band % LANES == 0:
        parts = [array[:, k * band : (k + 1) * band] for k in range(4)]
    else:
        at = lax.broadcasted_iota(jnp.int32, array.shape, 1) // band
        parts = [jnp.where(at == k, array, 0.0) for k in range(4)]
    return [jnp.sum(part, axis=1, keepdims=True) for part in parts]


def feed_down_kernel(count, steps, passed, *refs):
    adjoint_ref, scale_ref, rectified_ref, gated_ref, up_ref, down_ref = refs[:6]
    grad_up_ref, split_refs = refs[6 + passed], refs[7 + passed :]
    units = up_ref.shape[1]
    band = units // 4
    down = down_ref[...]
    rectified = rectified_ref[...]
    grad_gated = dot_cols(adjoint_ref[...], down)
    scales = [scale_ref[:, k : k + 1] for k in range(4)]
    twice = grad_gated * rectified
    grad_up = (twice * by_band(scales, band, units) * 2.0).astype(bf16)
    grad_up_ref[...] = grad_up
    sums = by_lane(band_sums(twice * rectified, band), split_refs[0].shape)
    grad_in = dot_cols(grad_up, up_ref[...]).astype(bf16)
    out = dot(gated_ref[...], down).astype(bf16)
    for k in range(count):

        @pl.when(pl.program_id(0) // steps == k)
        def _():
            for kind, value in enumerate((sums, grad_in, out)):
                split_refs[kind * count + k][...] = value


def tiles(width, at=0):
    return pl.BlockSpec((TILE, width), lambda i: (at + i, 0))


def fixed(array):
    return pl.BlockSpec(array.shape, lambda i: (0, 0), pipeline_mode=pl.Buffered(1))


def feed_up(blocks, heat, first, total, forced, route_in, route_out, up, passed):
    rows, width = blocks[0].shape
    tokens, count = rows * len(blocks), len(blocks)
    units = up.shape[1]
    at, steps = first // TILE, rows // TILE
    share = lambda k: pl.BlockSpec(
        (TILE, width), lambda i: (jnp.clip(i - k * steps, 0, steps - 1), 0)
    )
    before = count + 5
    return pl.pallas_call(
        functools.partial(feed_up_kernel, steps, count, len(passed)),
        grid=(tokens // TILE,),
        in_specs=[share(k) for k in range(count)]
        + [
            pl.BlockSpec(memory_space=pltpu.SMEM),
            tiles(1, at),
            fixed(route_in),
            fixed(route_out),
            fixed(up),
        ]
        + [pl.BlockSpec(memory_space=pl.ANY)] * len(passed),
        out_specs=[tiles(width, at), tiles(units, at), tiles(4), tiles(units)],
        out_shape=[
            jax.ShapeDtypeStruct((total, width), bf16),
            jax.ShapeDtypeStruct((total, units), bf16),
            jax.ShapeDtypeStruct((tokens, 4), f32),
            jax.ShapeDtypeStruct((tokens, units), f32),
        ],
        input_output_aliases={before + i: i for i in range(len(passed))},
        compiler_params=pltpu.CompilerParams(vmem_limit_bytes=VMEM_LIMIT),
        cost_estimate=pl.CostEstimate(
            flops=2 * tokens * width * units,
            bytes_accessed=2 * width * units + 6 * tokens * width,
            transcendentals=0,
        ),
        name="feed_up",
    )(*blocks, heat, forced, route_in, route_out, up, *passed)


def feed_down(adjoint, first, count, scale, rectified, gated, up, down, passed):
    total, width = adjoint.shape
    tokens, units = rectified.shape
    rows = tokens // count
    at, steps = first // TILE, rows // TILE
    share = lambda k, cols: pl.BlockSpec(
        (TILE, cols), lambda i: (jnp.clip(i - k * steps, 0, steps - 1), 0)
    )
    kinds = ((4, f32), (width, bf16), (width, bf16))
    found = pl.pallas_call(
        functools.partial(feed_down_kernel, count, steps, len(passed)),
        grid=(tokens // TILE,),
        in_specs=[
            tiles(width, at),
            tiles(4),
            tiles(units),
            tiles(units, at),
            fixed(up),
            fixed(down),
        ]
        + [pl.BlockSpec(memory_space=pl.ANY)] * len(passed),
        out_specs=[tiles(units, at)]
        + [share(k, cols) for cols, _ in kinds for k in range(count)],
        out_shape=[jax.ShapeDtypeStruct((total, units), bf16)]
        + [
            jax.ShapeDtypeStruct((rows, cols), dtype)
            for cols, dtype in kinds
            for _ in range(count)
        ],
        input_output_aliases={6 + i: i for i in range(len(passed))},
        compiler_params=pltpu.CompilerParams(vmem_limit_bytes=VMEM_LIMIT),
        cost_estimate=pl.CostEstimate(
            flops=6 * tokens * width * units,
            bytes_accessed=4 * width * units + 8 * tokens * width,
            transcendentals=0,
        ),
        name="feed_down",
    )(adjoint, scale, rectified, gated, up, down, *passed)
    return found[:1], *[found[1 + k * count : 1 + (k + 1) * count] for k in range(3)]


def per_device(
    layer_entries,
    incoming_adjoint,
    mixing_rescale_scalers,
    triple_projector_matrix,
    context_exit_matrix,
    dense_center_scaler,
    dense_center_offset,
    expand_matrix,
    shrink_matrix,
    span_chooser_initial,
    span_chooser_final,
    heat_divisor,
    sample_channel_fourths,
    element_preset_span,
    spot_group_table,
):
    block_len, seqs, width = layer_entries.shape
    tokens = block_len * seqs
    ring, plane = lax.axis_size("za"), lax.axis_size("yb")
    cores = lax.axis_size("bc")
    group = plane * lax.axis_size("bx") * cores
    devices = ring * group
    paired = plane == 2 and lax.axis_size("bx") == 2 and cores == 2
    za, yb = lax.axis_index("za"), lax.axis_index("yb")
    bx, bc = lax.axis_index("bx"), lax.axis_index("bc")
    rows = width // devices
    hidden_rows = FF // devices

    def home(array):
        return jnp.transpose(array, (1, 0, 2)).reshape(tokens, width)

    def back(array):
        return jnp.transpose(array.reshape(seqs, block_len, width), (1, 0, 2))

    entries, adjoint = home(layer_entries), home(incoming_adjoint)

    forced_home = jnp.transpose(element_preset_span, (1, 0)).reshape(tokens)
    forced_lanes = tokens // rows
    route_out_rows = span_chooser_final.shape[0]
    small_lanes = jnp.concatenate(
        [
            mixing_rescale_scalers[:, None],
            dense_center_scaler[:, None],
            dense_center_offset[:, None],
            jnp.pad(span_chooser_final, ((0, rows - route_out_rows), (0, 0))),
            forced_home.astype(bf16).reshape(rows, forced_lanes),
            jnp.zeros((rows, LANES - 7 - forced_lanes), bf16),
        ],
        axis=1,
    )
    qkv_cut = jnp.concatenate(
        [
            jnp.transpose(
                triple_projector_matrix.reshape(rows, 3, ring, GROUP_WIDTH),
                (2, 0, 1, 3),
            ).reshape(ring, rows, 3 * GROUP_WIDTH),
            jnp.broadcast_to(small_lanes, (ring, rows, LANES)),
            jnp.broadcast_to(span_chooser_initial, (ring, rows, RH)),
        ],
        axis=2,
    )
    units = ring * hidden_rows
    up_cut = jnp.transpose(
        expand_matrix.reshape(rows, ring, group, hidden_rows), (2, 0, 1, 3)
    ).reshape(group, rows, units)
    up_cut = lax.all_to_all(up_cut, PLANE, 0, 0, tiled=True).reshape(group * rows, units)
    qkv_cut = after(exchange(qkv_cut, "za"), up_cut)
    qkv_own = lax.all_gather(qkv_cut, PLANE, axis=1, tiled=False).reshape(width, 3 * GROUP_WIDTH + LANES + RH)
    small_lanes = qkv_own[:, 3 * GROUP_WIDTH : 3 * GROUP_WIDTH + LANES]
    route_in = qkv_own[:, 3 * GROUP_WIDTH + LANES :]
    gain_one, gain_two, bias_two = jnp.split(
        dot_cols(jnp.eye(8, LANES, dtype=bf16), small_lanes)[:3], 3, axis=0
    )
    by_device = small_lanes.reshape(devices, rows, LANES)
    route_out = by_device[:, :route_out_rows, 3:7].reshape(RH, 4)
    forced_all = by_device[:, :, 7 : 7 + forced_lanes].reshape(devices, tokens)
    out_own = lax.all_gather(context_exit_matrix, PLANE, axis=0, tiled=True)
    units = ring * hidden_rows
    entry_slots = ring_gather(entries, "za")
    up_own = lax.all_gather(
        after(up_cut, out_own, entry_slots[-1]), "za", axis=0, tiled=True
    )

    slot_ids = jnp.arange(ring, dtype=jnp.int32)
    table_ids = jnp.arange(spot_group_table.shape[0], dtype=jnp.int32)

    def places_of(piece):
        index = ((za - slot_ids) % ring) * plane + (yb - piece) % plane
        spots = jnp.sum(
            jnp.where(index[:, None] == table_ids[None, :], spot_group_table, 0), axis=1
        )
        return spots[:, None] * block_len + jnp.arange(block_len, dtype=jnp.int32)

    all_places = [places_of(piece) for piece in range(plane)]
    query_places = all_places[0].reshape(ring * block_len, 1)
    key_places = jnp.stack(all_places).reshape(plane, 1, ring * block_len)
    half = HD // 2
    inverse = theta_base ** (-(jnp.arange(half, dtype=f32) * (2.0 / HD)))
    angles = all_places[0].astype(f32)[:, :, None] * inverse
    cosine = jnp.concatenate([jnp.cos(angles), jnp.cos(angles)], axis=-1)
    sine = jnp.concatenate([-jnp.sin(angles), jnp.sin(angles)], axis=-1)
    active = (za < sample_channel_fourths).astype(f32)
    active_rows = jnp.broadcast_to(
        active[:, None, None], (seqs, block_len, 1)
    ).reshape(tokens, 1)

    if paired:
        spread = plane_gather
        at = jnp.stack(
            [
                (
                    (za * group + ((yb ^ y) * 2 + (bx ^ x)) * 2 + (bc ^ c)) * seqs + h
                ).astype(jnp.int32)
                for h, x, y, c in CHUNKS
            ]
        )
    else:
        spread = lambda block, between=None: [
            (lax.all_gather(block, PLANE, axis=0, tiled=True),)
        ]
        at = za * group * seqs + jnp.arange(group * seqs, dtype=jnp.int32)
    wide_adjoint = jnp.concatenate(sum(spread(adjoint), ()), axis=0)

    normed_slots, queries, boths = [], [], []
    for slot in range(ring):
        held = after(entry_slots[slot], entry_slots[min(slot + 2, ring - 1)])
        if slot > 0:
            held = after(held, boths[-1][0])
        held = held.astype(f32)
        inv_rms = lax.rsqrt(jnp.mean(held * held, axis=1, keepdims=True) + epsilon)
        normed_slots.append((held * inv_rms * gain_one).astype(bf16))
        joint = dot(normed_slots[slot], qkv_own)
        query, both = rope(
            joint.reshape(seqs, block_len, joint.shape[1]), cosine[slot], sine[slot]
        )
        queries.append(query)
        boths.append(ring_gather(both, "yb"))
    boths = [[slot[piece] for slot in boths] for piece in range(plane)]
    heads_out, attended, logs = attend(active, queries, boths, query_places, key_places)
    attended = after(attended, up_own).reshape(ring * tokens, GROUP_WIDTH)
    inputs = entries.astype(f32)
    hops = []
    parts = [
        lambda s=s: dot(attended[s * tokens : (s + 1) * tokens], out_own).astype(bf16)
        for s in range(ring)
    ]
    parts[0] = lambda: dot(after(attended[:tokens], wide_adjoint), out_own).astype(bf16)
    hidden = inputs + ring_scatter(parts, "za", hops)
    down_own = lax.all_gather(after(shrink_matrix, hops), "za", axis=0, tiled=True)

    centre = jnp.mean(hidden, axis=1, keepdims=True)
    centered = hidden - centre
    variance = jnp.mean(centered * centered, axis=1, keepdims=True)
    inv_std = lax.rsqrt(variance + epsilon)
    normal = centered * inv_std
    ffn_in = (normal * gain_two + bias_two).astype(bf16)

    picks = (at[:, None] == jnp.arange(devices * seqs)[None, :]).astype(bf16)
    wide_forced = dot(picks, forced_all.reshape(devices * seqs, block_len)).reshape(
        -1, 1
    )
    route_out_lanes = jnp.pad(route_out, ((0, 0), (0, LANES - 4)))

    def gather_back(groups, came=None):
        if paired:
            return plane_scatter(groups[0], came or plane_scatter_late(groups[1]))
        return lax.psum_scatter(
            groups[0][0], PLANE, scatter_dimension=0, tiled=True
        ).astype(f32)

    total = wide_adjoint.shape[0]
    kept, firsts, passed = [], [], ()

    def up_part(blocks):
        nonlocal passed
        firsts.append(sum(scale.shape[0] for scale, _ in kept))
        found = feed_up(
            blocks,
            heat_divisor,
            firsts[-1],
            total,
            wide_forced,
            route_in,
            route_out_lanes,
            up_own,
            passed,
        )
        passed = found[:2]
        kept.append(found[2:])
        return found[2]

    groups = spread(ffn_in, up_part)
    up_part(groups[-1])
    wide_in, gated = passed
    down_terms = dot_rows(gated, after(wide_adjoint, down_own)).astype(bf16)
    grad_down = lax.psum_scatter(down_terms, "za", scatter_dimension=0, tiled=True)
    late_adjoint = after(wide_adjoint, down_terms)
    count = len(groups)
    grad_bands, grad_ins, outs = [[None] * count for _ in range(3)]
    passed, came, band_came = (), None, None
    for turn in range(count)[::-1]:
        passed, grad_bands[turn], grad_ins[turn], outs[turn] = feed_down(
            late_adjoint,
            firsts[turn],
            len(groups[turn]),
            *kept[turn],
            gated,
            up_own,
            down_own,
            passed,
        )
        if paired and turn == 1:
            band_came = plane_scatter_late(grad_bands[1])
            came = plane_scatter_late(grad_ins[1])
            passed = after(passed, came[0], band_came)
    (grad_up,) = passed
    if paired:
        grad_ins[0] = after(grad_ins[0], came)
    grad_band_home = gather_back(grad_bands, band_came)
    grad_ffn_in = gather_back(grad_ins, came)

    temperature = heat_divisor[0]
    squashed = jnp.tanh(dot(ffn_in, route_in))
    routed = jax.nn.softmax(dot(squashed.astype(bf16), route_out) / temperature, axis=1)
    is_forced = (forced_home > 0)[:, None]
    grad_mix = jnp.cumsum(grad_band_home, axis=1)
    grad_logits = jnp.where(
        is_forced,
        0.0,
        routed
        * (grad_mix - jnp.sum(routed * grad_mix, axis=1, keepdims=True))
        / temperature,
    ).astype(bf16)
    grad_route_out = dot_rows(squashed.astype(bf16), grad_logits)
    grad_pre = (dot_cols(grad_logits, route_out) * (1.0 - squashed * squashed)).astype(
        bf16
    )
    grad_route_in = dot_rows(ffn_in, grad_pre)
    grad_ffn_in = grad_ffn_in + dot_cols(grad_pre, route_in)
    grad_gain_two = jnp.sum(grad_ffn_in * normal, axis=0)
    grad_bias_two = jnp.sum(grad_ffn_in, axis=0)
    grad_normal = grad_ffn_in * gain_two
    grad_hidden = adjoint.astype(f32) + inv_std * (
        grad_normal
        - jnp.mean(grad_normal, axis=1, keepdims=True)
        - normal * jnp.mean(grad_normal * normal, axis=1, keepdims=True)
    )
    small_terms = jnp.concatenate(
        [
            grad_route_in.reshape(devices, rows, RH),
            grad_gain_two.reshape(devices, rows, 1),
            grad_bias_two.reshape(devices, rows, 1),
            jnp.pad(
                grad_route_out.reshape(devices, route_out_rows, 4),
                ((0, 0), (0, rows - route_out_rows), (0, LANES - 6)),
            ),
        ],
        axis=2,
    ).astype(bf16)
    grad_low = after(grad_hidden.astype(bf16), grad_down)
    outs = after(outs, grad_low)
    came, steps = None, []
    if paired:
        came = plane_scatter_late(outs[1])
    out_sum = None
    if paired:
        early_outs = add_low(outs[0][0], swap(outs[0][1], "bc"))
        half_rows = early_outs.shape[0] // 2
        steps.append(add_low(early_outs[:half_rows], came[1]))
        steps.append(add_low(early_outs[half_rows:], came[2]))
    else:
        out_sum = gather_back(outs)
    grad_attn = [grad_low, onward(grad_low, "za")]
    up_terms = dot_rows(wide_in, after(grad_up, grad_low)).astype(bf16)
    grad_attn.append(onward(after(grad_attn[1], came, up_terms), "za"))
    grad_attn.append(onward(after(grad_attn[2], steps), "za"))
    up_terms = after(up_terms, grad_attn[3])
    up_terms = lax.psum_scatter(up_terms, "za", scatter_dimension=0, tiled=True)
    up_sums = up_terms
    up_terms = lax.all_to_all(
        up_terms.reshape(group, rows, units), PLANE, 0, 0, tiled=True
    )
    grad_wup = (
        jnp.transpose(up_terms.reshape(group, rows, ring, hidden_rows), (1, 2, 0, 3))
        .reshape(rows, FF)
        .astype(f32)
    )

    grad_heads = [
        (dot_cols(block, out_own) * active_rows)
        .astype(bf16)
        .reshape(seqs, block_len, GROUP_WIDTH)
        for block in grad_attn
    ]
    grad_queries, grad_keys, grad_values = [], [], []
    for name, chosen in (
        ("attend_back_far", range(1, plane)),
        ("attend_back", range(1)),
    ):
        if len(chosen) == 0:
            continue
        found = attend_back(
            queries,
            [boths[piece] for piece in chosen],
            grad_heads,
            heads_out,
            logs,
            query_places,
            key_places[jnp.array(chosen)],
            name,
        )
        if name == "attend_back_far":
            found, grad_heads = lax.optimization_barrier((found, grad_heads))
            steps, small_terms = after((steps, small_terms), found)

            def from_others(grads):
                running = grads[0]
                for term in grads[1:]:
                    running = add_low(term, onward(running, "yb"))
                return onward(running, "yb")

            grad_keys.append(from_others(found[1]))
            grad_values.append(from_others(found[2]))
        else:
            grad_keys.append(found[1][0])
            grad_values.append(found[2][0])
        grad_queries.append(found[0])
    if paired:
        half_rows = steps[0].shape[0] // 2
        out_sum = jnp.concatenate(
            [
                part[:half_rows].astype(f32) + swap(part[half_rows:], axis).astype(f32)
                for part, axis in zip(steps, ("bx", "yb"))
            ],
            axis=0,
        )
        small_terms = plane_reduce(
            small_terms.reshape(ring, plane, 2, cores, rows, RH + LANES)
        )
    else:
        small_terms = lax.psum_scatter(
            small_terms.reshape(ring, group, rows, RH + LANES),
            PLANE,
            scatter_dimension=1,
            tiled=False,
        )
    small_sum = sum(
        part.astype(f32)
        for part in rotate(
            lambda i: lax.dynamic_index_in_dim(small_terms, i, 0, keepdims=False), "za"
        )
    )
    result = back((hidden + out_sum).astype(bf16))
    joint = query_back(grad_queries, cosine, sine)
    attn_wide = jnp.concatenate(grad_attn, axis=0)
    normed_wide = jnp.concatenate(normed_slots, axis=0)

    def to_rows(terms, steps=None):
        cols = terms.shape[-1]
        if paired:
            terms = plane_reduce(
                terms.reshape(ring, plane, 2, cores, rows, cols), steps
            )
        else:
            terms = lax.psum_scatter(
                terms.reshape(ring, group, rows, cols),
                PLANE,
                scatter_dimension=1,
                tiled=False,
            )
        return exchange(terms, "za").astype(f32)

    flat_joint = lambda array: array.reshape(ring * tokens, 3 * GROUP_WIDTH)
    query_terms = dot_cols(
        flat_joint(after(joint, grad_keys, grad_values, result, small_sum))[:, :GROUP_WIDTH],
        qkv_own[:, :GROUP_WIDTH],
    )
    grad_out_terms = dot_rows(attended, attn_wide).astype(bf16)
    grad_wout = lax.psum_scatter(
        grad_out_terms, PLANE, scatter_dimension=0, tiled=True
    ).astype(f32)
    grad_keys = after(grad_keys, query_terms, grad_out_terms)
    joint = flat_joint(both_back(grad_keys, grad_values, cosine, sine, joint))
    both_own = qkv_own[:, GROUP_WIDTH : 3 * GROUP_WIDTH]
    low_terms = []
    for s in range(ring):
        at = slice(s * tokens, (s + 1) * tokens)
        terms = query_terms[at] + dot_cols(joint[at, GROUP_WIDTH:], both_own)
        low_terms.append(terms.astype(bf16))
    low_terms[1] = after(low_terms[1], up_sums)
    weight_terms = dot_rows(normed_wide, after(joint, low_terms[1])).astype(bf16)
    steps = []
    qkv_rows = to_rows(weight_terms, steps)
    low_terms[2] = after(low_terms[2], weight_terms)
    if steps:
        low_terms[2] = after(low_terms[2], steps[0])
        low_terms[3] = after(low_terms[3], steps[1], up_terms)
        low_terms[0] = after(low_terms[0], steps[2])
    grad_normed = ring_scatter([lambda s=s: low_terms[s] for s in range(ring)], "za")
    grad_wqkv = jnp.transpose(
        qkv_rows.reshape(ring, rows, 3, GROUP_WIDTH), (1, 2, 0, 3)
    ).reshape(rows, 3 * width)
    weight_rows = triple_projector_matrix.astype(f32)
    grad_gain_one = jnp.sum(grad_wqkv * weight_rows, axis=1) / (
        mixing_rescale_scalers.astype(f32)
    )
    inv_home = lax.rsqrt(jnp.mean(inputs * inputs, axis=1, keepdims=True) + epsilon)
    scaled = inputs * inv_home
    grad_scaled = grad_normed * gain_one
    grad_inputs = grad_hidden + inv_home * (
        grad_scaled - scaled * jnp.mean(grad_scaled * scaled, axis=1, keepdims=True)
    )
    grad_tokens = back(grad_inputs.astype(bf16))
    return (
        result,
        grad_tokens,
        grad_gain_one,
        grad_wqkv,
        grad_wout,
        small_sum[:, RH],
        small_sum[:, RH + 1],
        grad_wup,
        grad_down.astype(f32),
        small_sum[:, :RH],
        small_sum[:route_out_rows, RH + 2 : RH + 6],
    )


def solution(mesh):
    seq, batch = mesh.shape["seq"], mesh.shape["batch"]
    inner = Mesh(
        mesh.devices.reshape(RING, seq // RING, batch // 2, 2),
        ("za", "yb", "bx", "bc"),
    )
    along, across = ("za", "yb"), ("bx", "bc")
    tokens = P(along, across, None)
    vector = P(along + across)
    matrix = P(along + across, None)
    return jax.shard_map(
        per_device,
        mesh=inner,
        in_specs=(
            tokens,
            tokens,
            vector,
            matrix,
            matrix,
            vector,
            vector,
            matrix,
            matrix,
            matrix,
            matrix,
            P(),
            P(across),
            P(along, across),
            P(),
        ),
        out_specs=(
            tokens,
            tokens,
            vector,
            matrix,
            matrix,
            vector,
            vector,
            matrix,
            matrix,
            matrix,
            matrix,
        ),
        check_vma=False,
    )
```

```python
import functools
import math

import jax
import jax.numpy as jnp
from jax import lax
from jax.experimental import pallas as pl
from jax.experimental.pallas import tpu as pltpu
from jax.sharding import Mesh, PartitionSpec as P

H = 16
HD = 128
FF = 8192
RH = 256
RING = 4
SEQS = 2
GROUP_HEADS = H // RING
GROUP_WIDTH = GROUP_HEADS * HD
SCALE = 1.0 / math.sqrt(HD)
VMEM_LIMIT = 48 * 1024 * 1024
TILE = 256
LANES = 128

epsilon = 1e-05
theta_base = 10000.0
neg_large = -1e30
bf16 = jnp.bfloat16
f32 = jnp.float32
PLANE = ("yb", "bx", "bc")
EVERY = ("za",) + PLANE
SWAP = [(0, 1), (1, 0)]


def dot(left_mat, right_mat):
    return lax.dot_general(
        left_mat, right_mat, (((1,), (0,)), ((), ())), preferred_element_type=f32
    )


def dot_rows(left_mat, right_mat):
    return lax.dot_general(
        left_mat, right_mat, (((0,), (0,)), ((), ())), preferred_element_type=f32
    )


def dot_cols(left_mat, right_mat):
    return lax.dot_general(
        left_mat, right_mat, (((1,), (1,)), ((), ())), preferred_element_type=f32
    )


def onward(block, axis):
    size = lax.axis_size(axis)
    return lax.ppermute(block, axis, [(i, (i + 1) % size) for i in range(size)])


def after(value, *others):
    return lax.optimization_barrier((value, others))[0]


def add_low(left, right):
    return (left.astype(f32) + right.astype(f32)).astype(left.dtype)


def ring_gather(block, axis):
    slots = [block]
    for _ in range(1, lax.axis_size(axis)):
        slots.append(onward(slots[-1], axis))
    return slots


def ring_scatter(parts, axis, hops=None):
    running = parts[1]()
    for slot in range(2, lax.axis_size(axis)):
        moved = onward(running, axis)
        if hops is not None:
            hops.append(moved)
        running = add_low(parts[slot](), moved)
    moved = onward(running, axis)
    return parts[0]().astype(f32) + moved.astype(f32)


def in_order(slots, axis):
    size, me = lax.axis_size(axis), lax.axis_index(axis)
    rows = slots[0].shape[0]
    placed = jnp.zeros((size * rows,) + slots[0].shape[1:], slots[0].dtype)
    for far, slot in enumerate(slots):
        placed = lax.dynamic_update_slice_in_dim(
            placed, slot, (me - far) % size * rows, axis=0
        )
    return placed


def rotate(pieces, axis):
    size, me = lax.axis_size(axis), lax.axis_index(axis)
    came = [pieces(me)]
    for far in range(1, size):
        route = [(i, (i + far) % size) for i in range(size)]
        came.append(lax.ppermute(pieces((me + far) % size), axis, route))
    return came


def exchange(pieces, axis):
    return in_order(
        rotate(lambda i: lax.dynamic_index_in_dim(pieces, i, 0), axis), axis
    )


EARLY = [(0, 0, 0), (0, 1, 0), (1, 0, 0), (1, 0, 1)]
LATE = [(0, 0, 1), (0, 1, 1), (1, 1, 0), (1, 1, 1)]
CHUNKS = [(h, x, y, c) for part in (EARLY, LATE) for c in (0, 1) for h, x, y in part]


def swap(block, axis):
    return lax.ppermute(block, axis, SWAP)


def plane_gather(block, between=lambda early: ()):
    half = block.shape[0] // 2
    first, second = block[:half], block[half:]
    early = jnp.concatenate(
        [first, swap(first, "bx"), second, swap(second, "yb")], axis=0
    )
    late = swap(early[: 2 * half], "yb"), swap(early[2 * half :], "bx")
    groups = [(early, swap(early, "bc"))]
    late = jnp.concatenate(after(late, between(groups[0])), axis=0)
    return groups + [(late, swap(late, "bc"))]


def plane_scatter_late(terms):
    late = add_low(terms[0], swap(terms[1], "bc"))
    half = late.shape[0] // 2
    return late, swap(late[:half], "yb"), swap(late[half:], "bx")


def plane_scatter(terms, came, sums=None):
    rows = terms[0].shape[0] // 4
    early = add_low(terms[0], swap(terms[1], "bc"))
    first = add_low(early[: 2 * rows], came[1])
    second = add_low(early[2 * rows :], came[2])
    if sums is not None:
        sums.extend([first, second])
    first_sum = first[:rows].astype(f32) + swap(first[rows:], "bx").astype(f32)
    second_sum = second[:rows].astype(f32) + swap(second[rows:], "yb").astype(f32)
    return jnp.concatenate([first_sum, second_sum], axis=0)


def keep_and_swap(blocks, axis, dim, ready=()):
    me = lax.axis_index(axis)
    kept = lax.dynamic_index_in_dim(after(blocks, ready), me, dim, keepdims=False)
    sent = lax.dynamic_index_in_dim(blocks, 1 - me, dim, keepdims=False)
    return add_low(kept, swap(sent, axis))


def plane_reduce(blocks, stages=None, ready=((), ())):
    both = keep_and_swap(blocks, "bc", 3, ready[0])
    middle = blocks.shape[-1] // 2
    first = keep_and_swap(both[..., :middle], "yb", 1, ready[1])
    second = keep_and_swap(both[..., middle:], "bx", 2, ready[1])
    if stages is not None:
        stages.extend([both, (first, second)])
    first = keep_and_swap(first, "bx", 1)
    second = keep_and_swap(second, "yb", 1)
    if stages is not None:
        stages.append((first, second))
    return jnp.concatenate([first, second], axis=-1)


def rope_kernel(joint_ref, cos_ref, sin_ref, query_ref, both_ref):
    cosine, sine = cos_ref[...], sin_ref[...]
    for head in range(GROUP_HEADS):
        for part, out_ref in ((0, query_ref), (1, both_ref)):
            at = part * GROUP_WIDTH + head * HD
            raw = joint_ref[0, :, at : at + HD]
            turned = raw * cosine + pltpu.roll(raw, HD // 2, 1) * sine
            out_ref[0, :, head * HD : (head + 1) * HD] = turned.astype(bf16)
    both_ref[0, :, GROUP_WIDTH:] = joint_ref[0, :, 2 * GROUP_WIDTH :].astype(bf16)


def rope(joint, cosine, sine):
    seqs, block_len, width = joint.shape
    rows = lambda w: pl.BlockSpec((1, block_len, w), lambda b: (b, 0, 0))
    table = pl.BlockSpec((block_len, HD), lambda b: (0, 0))
    return pl.pallas_call(
        rope_kernel,
        grid=(seqs,),
        in_specs=[rows(3 * GROUP_WIDTH), table, table],
        out_specs=[rows(GROUP_WIDTH), rows(2 * GROUP_WIDTH)],
        out_shape=[
            jax.ShapeDtypeStruct((seqs, block_len, GROUP_WIDTH), bf16),
            jax.ShapeDtypeStruct((seqs, block_len, 2 * GROUP_WIDTH), bf16),
        ],
        compiler_params=pltpu.CompilerParams(vmem_limit_bytes=VMEM_LIMIT),
        name="rope",
    )(joint, cosine, sine)


def turn_back(grad, cosine, sine):
    return (grad * cosine - pltpu.roll(grad, HD // 2, 1) * sine).astype(bf16)


def query_back_kernel(terms, *refs):
    cos_ref, sin_ref, out_ref = refs[terms:]
    cosine, sine = cos_ref[0], sin_ref[0]
    for seq in range(out_ref.shape[1]):
        for head in range(GROUP_HEADS):
            at = slice(head * HD, (head + 1) * HD)
            grad = sum(ref[0, seq, :, at].astype(f32) for ref in refs[:terms])
            out_ref[0, seq, :, at] = turn_back(grad, cosine, sine)


def both_back_kernel(terms, *refs):
    key_refs, value_refs = refs[:terms], refs[terms : 2 * terms]
    cos_ref, sin_ref, _, out_ref = refs[2 * terms :]

    @pl.when(pl.program_id(1) == 0)
    def _():
        cosine, sine = cos_ref[0], sin_ref[0]
        for seq in range(out_ref.shape[1]):
            for head in range(GROUP_HEADS):
                at = slice(head * HD, (head + 1) * HD)
                grad = sum(ref[0, seq, :, at].astype(f32) for ref in key_refs)
                out_ref[0, seq, :, at] = turn_back(grad, cosine, sine)

    @pl.when(pl.program_id(1) == 1)
    def _():
        total = sum(ref[0].astype(f32) for ref in value_refs)
        out_ref[0] = total.astype(bf16)


def joint_shape(grad):
    return jax.ShapeDtypeStruct(grad.shape[:3] + (3 * GROUP_WIDTH,), bf16)


def query_back(grads, cosine, sine):
    slots, seqs, block_len, width = grads[0].shape
    rows = pl.BlockSpec((1, seqs, block_len, width), lambda s: (s, 0, 0, 0))
    table = pl.BlockSpec((1, block_len, HD), lambda s: (s, 0, 0))
    return pl.pallas_call(
        functools.partial(query_back_kernel, len(grads)),
        grid=(slots,),
        in_specs=[rows] * len(grads) + [table, table],
        out_specs=rows,
        out_shape=joint_shape(grads[0]),
        compiler_params=pltpu.CompilerParams(vmem_limit_bytes=VMEM_LIMIT),
        name="query_back",
    )(*grads, cosine, sine)


def both_back(keys, values, cosine, sine, joint):
    slots, seqs, block_len, width = keys[0].shape
    rows = pl.BlockSpec((1, seqs, block_len, width), lambda s, j: (s, 0, 0, 0))
    table = pl.BlockSpec((1, block_len, HD), lambda s, j: (s, 0, 0))
    terms = len(keys)
    return pl.pallas_call(
        functools.partial(both_back_kernel, terms),
        grid=(slots, 2),
        in_specs=[rows] * (2 * terms)
        + [table, table, pl.BlockSpec(memory_space=pl.ANY)],
        out_specs=pl.BlockSpec(
            (1, seqs, block_len, width), lambda s, j: (s, 0, 0, 1 + j)
        ),
        out_shape=joint_shape(keys[0]),
        input_output_aliases={2 * terms + 2: 0},
        compiler_params=pltpu.CompilerParams(vmem_limit_bytes=VMEM_LIMIT),
        name="both_back",
    )(*keys, *values, cosine, sine, joint)


def flat(ref):
    slots, _, block_len, width = ref.shape
    return ref[:, 0].reshape(slots * block_len, width)


def end_to_end(refs):
    return jnp.concatenate([ref[0] for ref in refs], axis=0)


def by_piece(refs, slots):
    return [refs[i : i + slots] for i in range(0, len(refs), slots)]


def attend_kernel(slots, pieces, *refs):
    active_ref, query_refs = refs[0], refs[1 : 1 + slots]
    rest = refs[1 + slots :]
    key_refs = by_piece(rest[: pieces * slots], slots)
    value_refs = by_piece(rest[pieces * slots : 2 * pieces * slots], slots)
    qplace_ref, kplace_ref, out_ref, low_ref, log_ref = rest[2 * pieces * slots :]
    queries = end_to_end(query_refs)
    query_places = qplace_ref[...]
    masked = []
    for piece in range(pieces):
        scores = dot_cols(queries, end_to_end(key_refs[piece])) * SCALE
        allowed = kplace_ref[piece] <= query_places
        masked.append(jnp.where(allowed, scores, neg_large))
    top = functools.reduce(
        jnp.maximum, [jnp.max(m, axis=1, keepdims=True) for m in masked]
    )
    total, gathered = 0.0, 0.0
    for piece in range(pieces):
        weights = jnp.exp(masked[piece] - top)
        total = total + jnp.sum(weights, axis=1, keepdims=True)
        gathered = gathered + dot(weights.astype(bf16), end_to_end(value_refs[piece]))
    result = gathered / total
    out_ref[:, 0] = result.reshape(out_ref.shape[0], out_ref.shape[2], HD)
    kept = active_ref[pl.program_id(0)]
    low_ref[:, 0] = (
        (result * kept).astype(bf16).reshape(out_ref.shape[0], out_ref.shape[2], HD)
    )
    log_ref[0, 0] = top + jnp.log(total)


def attend(active, queries, boths, query_places, key_places):
    slots, pieces = len(queries), len(boths)
    seqs, block_len, width = queries[0].shape
    rows = slots * block_len
    heads = width // HD
    own = pl.BlockSpec((1, block_len, HD), lambda s, h: (s, 0, h))
    value = pl.BlockSpec((1, block_len, HD), lambda s, h: (s, 0, heads + h))
    tile = pl.BlockSpec((slots, 1, block_len, HD), lambda s, h: (0, s, 0, h))
    every = [both for piece in boths for both in piece]
    shape = (slots, seqs, block_len, width)
    return pl.pallas_call(
        functools.partial(attend_kernel, slots, pieces),
        grid=(seqs, heads),
        in_specs=[pl.BlockSpec(memory_space=pltpu.SMEM)]
        + [own] * slots
        + [own] * len(every)
        + [value] * len(every)
        + [
            pl.BlockSpec((rows, 1), lambda s, h: (0, 0)),
            pl.BlockSpec((pieces, 1, rows), lambda s, h: (0, 0, 0)),
        ],
        out_specs=[
            tile,
            tile,
            pl.BlockSpec((1, 1, rows, 1), lambda s, h: (s, h, 0, 0)),
        ],
        out_shape=[
            jax.ShapeDtypeStruct(shape, f32),
            jax.ShapeDtypeStruct(shape, bf16),
            jax.ShapeDtypeStruct((seqs, heads, rows, 1), f32),
        ],
        compiler_params=pltpu.CompilerParams(vmem_limit_bytes=VMEM_LIMIT),
        name="attend",
    )(active, *queries, *every, *every, query_places, key_places)


def attend_back_kernel(slots, pieces, *refs):
    query_refs, rest = refs[:slots], refs[slots:]
    key_refs = by_piece(rest[: pieces * slots], slots)
    value_refs = by_piece(rest[pieces * slots : 2 * pieces * slots], slots)
    rest = rest[2 * pieces * slots :]
    grad_refs, rest = rest[:slots], rest[slots:]
    out_ref, log_ref, qplace_ref, kplace_ref, dq_ref = rest[:5]
    dk_refs, dv_refs = rest[5 : 5 + pieces], rest[5 + pieces :]
    queries, grads = end_to_end(query_refs), end_to_end(grad_refs)
    query_places = qplace_ref[...]
    dots = jnp.sum(grads.astype(f32) * flat(out_ref), axis=1, keepdims=True)
    log_norm = log_ref[0, 0]
    grad_query = 0.0
    shape = (slots, query_refs[0].shape[1], HD)
    for piece in range(pieces):
        keys, values = end_to_end(key_refs[piece]), end_to_end(value_refs[piece])
        scores = dot_cols(queries, keys) * SCALE
        allowed = kplace_ref[piece] <= query_places
        probs = jnp.exp(jnp.where(allowed, scores - log_norm, neg_large))
        grad_probs = dot_cols(grads, values)
        dv_refs[piece][:, 0] = (
            dot_rows(probs.astype(bf16), grads)
            .astype(dv_refs[piece].dtype)
            .reshape(shape)
        )
        grad_scores = (probs * (grad_probs - dots)).astype(bf16)
        dk_refs[piece][:, 0] = (
            (dot_rows(grad_scores, queries) * SCALE)
            .astype(dk_refs[piece].dtype)
            .reshape(shape)
        )
        grad_query = grad_query + dot(grad_scores, keys)
    dq_ref[:, 0] = (grad_query * SCALE).reshape(shape)


def attend_back(queries, boths, grads, out, logs, query_places, key_places, name):
    slots, pieces = len(queries), len(boths)
    seqs, block_len, width = queries[0].shape
    rows = slots * block_len
    heads = width // HD
    own = pl.BlockSpec((1, block_len, HD), lambda s, h: (s, 0, h))
    value = pl.BlockSpec((1, block_len, HD), lambda s, h: (s, 0, heads + h))
    tile = pl.BlockSpec((slots, 1, block_len, HD), lambda s, h: (0, s, 0, h))
    every = [both for piece in boths for both in piece]
    shape = (slots, seqs, block_len, width)
    wide = jax.ShapeDtypeStruct(shape, f32)
    low = jax.ShapeDtypeStruct(shape, bf16)
    found = pl.pallas_call(
        functools.partial(attend_back_kernel, slots, pieces),
        grid=(seqs, heads),
        in_specs=[own] * slots
        + [own] * len(every)
        + [value] * len(every)
        + [own] * slots
        + [
            tile,
            pl.BlockSpec((1, 1, rows, 1), lambda s, h: (s, h, 0, 0)),
            pl.BlockSpec((rows, 1), lambda s, h: (0, 0)),
            pl.BlockSpec((pieces, 1, rows), lambda s, h: (0, 0, 0)),
        ],
        out_specs=[tile] * (1 + 2 * pieces),
        out_shape=[wide] + [low] * (2 * pieces),
        compiler_params=pltpu.CompilerParams(vmem_limit_bytes=VMEM_LIMIT),
        name=name,
    )(*queries, *every, *every, *grads, out, logs, query_places, key_places)
    return found[0], found[1 : 1 + pieces], found[1 + pieces :]


def feed_up_kernel(steps, blocks, passed, *refs):
    in_refs, refs = refs[:blocks], refs[blocks:]
    heat_ref, forced_ref, route_in_ref, route_out_ref, up_ref = refs[:5]
    all_in_ref, gated_ref, scale_ref, rectified_ref = refs[5 + passed :]
    block = in_refs[0][...]
    for k in range(1, blocks):
        block = jnp.where(pl.program_id(0) < k * steps, block, in_refs[k][...])
    all_in_ref[...] = block
    units = up_ref.shape[1]
    band = units // 4

    squashed = jnp.tanh(dot(block, route_in_ref[...])).astype(bf16)
    logits = dot(squashed, route_out_ref[...]) / heat_ref[0]
    lane = lax.broadcasted_iota(jnp.int32, logits.shape, 1)
    logits = jnp.where(lane < 4, logits, neg_large)
    weights = jnp.exp(logits - jnp.max(logits, axis=1, keepdims=True))
    routed = weights / jnp.sum(weights, axis=1, keepdims=True)
    forced = forced_ref[...]
    chosen = jnp.where(lane.astype(f32) == forced - 1.0, 1.0, 0.0)
    mix = jnp.where(forced > 0.0, chosen, routed)
    scales = [mix[:, 3:4]]
    for k in (2, 1, 0):
        scales.insert(0, scales[0] + mix[:, k : k + 1])
    scale_ref[...] = by_lane(scales, scale_ref.shape)

    rectified = jnp.maximum(dot(block, up_ref[...]), 0.0)
    rectified_ref[...] = rectified
    gated_ref[...] = (rectified * rectified * by_band(scales, band, units)).astype(bf16)


def by_lane(columns, shape):
    lane = lax.broadcasted_iota(jnp.int32, shape, 1)
    found = jnp.zeros(shape, f32)
    for k, column in enumerate(columns):
        found = jnp.where(lane == k, column, found)
    return found


def by_band(columns, band, units):
    rows = columns[0].shape[0]
    if band % LANES == 0:
        return jnp.concatenate(
            [jnp.broadcast_to(column, (rows, band)) for column in columns], axis=1
        )
    at = lax.broadcasted_iota(jnp.int32, (rows, units), 1) // band
    found = jnp.broadcast_to(columns[3], (rows, units))
    for k in range(3):
        found = jnp.where(at == k, columns[k], found)
    return found


def band_sums(array, band):
    if band % LANES == 0:
        parts = [array[:, k * band : (k + 1) * band] for k in range(4)]
    else:
        at = lax.broadcasted_iota(jnp.int32, array.shape, 1) // band
        parts = [jnp.where(at == k, array, 0.0) for k in range(4)]
    return [jnp.sum(part, axis=1, keepdims=True) for part in parts]


def feed_down_kernel(count, steps, passed, *refs):
    adjoint_ref, scale_ref, rectified_ref, gated_ref, up_ref, down_ref = refs[:6]
    grad_up_ref, split_refs = refs[6 + passed], refs[7 + passed :]
    units = up_ref.shape[1]
    band = units // 4
    down = down_ref[...]
    rectified = rectified_ref[...]
    grad_gated = dot_cols(adjoint_ref[...], down)
    scales = [scale_ref[:, k : k + 1] for k in range(4)]
    twice = grad_gated * rectified
    grad_up = (twice * by_band(scales, band, units) * 2.0).astype(bf16)
    grad_up_ref[...] = grad_up
    sums = by_lane(band_sums(twice * rectified, band), split_refs[0].shape)
    grad_in = dot_cols(grad_up, up_ref[...]).astype(bf16)
    out = dot(gated_ref[...], down).astype(bf16)
    for k in range(count):

        @pl.when(pl.program_id(0) // steps == k)
        def _():
            for kind, value in enumerate((sums, grad_in, out)):
                split_refs[kind * count + k][...] = value


def tiles(width, at=0):
    return pl.BlockSpec((TILE, width), lambda i: (at + i, 0))


def fixed(array):
    return pl.BlockSpec(array.shape, lambda i: (0, 0), pipeline_mode=pl.Buffered(1))


def feed_up(blocks, heat, first, total, forced, route_in, route_out, up, passed):
    rows, width = blocks[0].shape
    tokens, count = rows * len(blocks), len(blocks)
    units = up.shape[1]
    at, steps = first // TILE, rows // TILE
    share = lambda k: pl.BlockSpec(
        (TILE, width), lambda i: (jnp.clip(i - k * steps, 0, steps - 1), 0)
    )
    before = count + 5
    return pl.pallas_call(
        functools.partial(feed_up_kernel, steps, count, len(passed)),
        grid=(tokens // TILE,),
        in_specs=[share(k) for k in range(count)]
        + [
            pl.BlockSpec(memory_space=pltpu.SMEM),
            tiles(1, at),
            fixed(route_in),
            fixed(route_out),
            fixed(up),
        ]
        + [pl.BlockSpec(memory_space=pl.ANY)] * len(passed),
        out_specs=[tiles(width, at), tiles(units, at), tiles(4), tiles(units)],
        out_shape=[
            jax.ShapeDtypeStruct((total, width), bf16),
            jax.ShapeDtypeStruct((total, units), bf16),
            jax.ShapeDtypeStruct((tokens, 4), f32),
            jax.ShapeDtypeStruct((tokens, units), f32),
        ],
        input_output_aliases={before + i: i for i in range(len(passed))},
        compiler_params=pltpu.CompilerParams(vmem_limit_bytes=VMEM_LIMIT),
        cost_estimate=pl.CostEstimate(
            flops=2 * tokens * width * units,
            bytes_accessed=2 * width * units + 6 * tokens * width,
            transcendentals=0,
        ),
        name="feed_up",
    )(*blocks, heat, forced, route_in, route_out, up, *passed)


def feed_down(adjoint, first, count, scale, rectified, gated, up, down, passed):
    total, width = adjoint.shape
    tokens, units = rectified.shape
    rows = tokens // count
    at, steps = first // TILE, rows // TILE
    share = lambda k, cols: pl.BlockSpec(
        (TILE, cols), lambda i: (jnp.clip(i - k * steps, 0, steps - 1), 0)
    )
    kinds = ((4, f32), (width, bf16), (width, bf16))
    found = pl.pallas_call(
        functools.partial(feed_down_kernel, count, steps, len(passed)),
        grid=(tokens // TILE,),
        in_specs=[
            tiles(width, at),
            tiles(4),
            tiles(units),
            tiles(units, at),
            fixed(up),
            fixed(down),
        ]
        + [pl.BlockSpec(memory_space=pl.ANY)] * len(passed),
        out_specs=[tiles(units, at)]
        + [share(k, cols) for cols, _ in kinds for k in range(count)],
        out_shape=[jax.ShapeDtypeStruct((total, units), bf16)]
        + [
            jax.ShapeDtypeStruct((rows, cols), dtype)
            for cols, dtype in kinds
            for _ in range(count)
        ],
        input_output_aliases={6 + i: i for i in range(len(passed))},
        compiler_params=pltpu.CompilerParams(vmem_limit_bytes=VMEM_LIMIT),
        cost_estimate=pl.CostEstimate(
            flops=6 * tokens * width * units,
            bytes_accessed=4 * width * units + 8 * tokens * width,
            transcendentals=0,
        ),
        name="feed_down",
    )(adjoint, scale, rectified, gated, up, down, *passed)
    return found[:1], *[found[1 + k * count : 1 + (k + 1) * count] for k in range(3)]


def columns_kernel(parts, *refs):
    place_ref, piece_refs, out_ref = refs[0], refs[1:-1], refs[-1]
    places = out_ref.shape[1] // piece_refs[0].shape[2]
    cols = piece_refs[0].shape[2] // parts
    place = 0
    for ref in piece_refs:
        for i in range(ref.shape[0]):
            for part in range(parts):
                at = pl.multiple_of((part * places + place_ref[place]) * cols, cols)
                block = ref[i, :, part * cols : (part + 1) * cols]
                out_ref[:, pl.ds(at, cols)] = block.astype(f32)
            place += 1


def columns(pieces, places, parts):
    count = sum(piece.shape[0] for piece in pieces)
    _, rows, cols = pieces[0].shape
    if cols // parts % LANES:
        every = jnp.concatenate(pieces, axis=0)[jnp.argsort(places)]
        every = every.reshape(count, rows, parts, cols // parts)
        return jnp.transpose(every, (1, 2, 0, 3)).reshape(rows, -1).astype(f32)
    return pl.pallas_call(
        functools.partial(columns_kernel, parts),
        in_specs=[pl.BlockSpec(memory_space=pltpu.SMEM)]
        + [pl.BlockSpec(memory_space=pltpu.VMEM)] * len(pieces),
        out_specs=pl.BlockSpec(memory_space=pltpu.VMEM),
        out_shape=jax.ShapeDtypeStruct((rows, count * cols), f32),
        compiler_params=pltpu.CompilerParams(vmem_limit_bytes=VMEM_LIMIT),
        name="columns",
    )(places, *pieces)


def per_device(
    layer_entries,
    incoming_adjoint,
    mixing_rescale_scalers,
    triple_projector_matrix,
    context_exit_matrix,
    dense_center_scaler,
    dense_center_offset,
    expand_matrix,
    shrink_matrix,
    span_chooser_initial,
    span_chooser_final,
    heat_divisor,
    sample_channel_fourths,
    element_preset_span,
    spot_group_table,
):
    block_len, seqs, width = layer_entries.shape
    tokens = block_len * seqs
    ring, plane = lax.axis_size("za"), lax.axis_size("yb")
    cores = lax.axis_size("bc")
    group = plane * lax.axis_size("bx") * cores
    devices = ring * group
    paired = plane == 2 and lax.axis_size("bx") == 2 and cores == 2
    za, yb = lax.axis_index("za"), lax.axis_index("yb")
    bx, bc = lax.axis_index("bx"), lax.axis_index("bc")
    rows = width // devices
    hidden_rows = FF // devices

    def home(array):
        return jnp.transpose(array, (1, 0, 2)).reshape(tokens, width)

    def back(array):
        return jnp.transpose(array.reshape(seqs, block_len, width), (1, 0, 2))

    entries, adjoint = home(layer_entries), home(incoming_adjoint)

    forced_home = jnp.transpose(element_preset_span, (1, 0)).reshape(tokens)
    forced_lanes = tokens // rows
    route_out_rows = span_chooser_final.shape[0]
    small_lanes = jnp.concatenate(
        [
            mixing_rescale_scalers[:, None],
            dense_center_scaler[:, None],
            dense_center_offset[:, None],
            jnp.pad(span_chooser_final, ((0, rows - route_out_rows), (0, 0))),
            forced_home.astype(bf16).reshape(rows, forced_lanes),
            jnp.zeros((rows, LANES - 7 - forced_lanes), bf16),
        ],
        axis=1,
    )
    qkv_cut = jnp.concatenate(
        [
            jnp.transpose(
                triple_projector_matrix.reshape(rows, 3, ring, GROUP_WIDTH),
                (2, 0, 1, 3),
            ).reshape(ring, rows, 3 * GROUP_WIDTH),
            jnp.broadcast_to(small_lanes, (ring, rows, LANES)),
            jnp.broadcast_to(span_chooser_initial, (ring, rows, RH)),
        ],
        axis=2,
    )
    units = ring * hidden_rows
    up_cut = jnp.transpose(
        expand_matrix.reshape(rows, ring, group, hidden_rows), (2, 0, 1, 3)
    ).reshape(group, rows, units)
    up_cut = lax.all_to_all(up_cut, PLANE, 0, 0, tiled=True).reshape(group * rows, units)
    qkv_cut = after(exchange(qkv_cut, "za"), up_cut)
    qkv_own = lax.all_gather(qkv_cut, PLANE, axis=1, tiled=False).reshape(width, 3 * GROUP_WIDTH + LANES + RH)
    small_lanes = qkv_own[:, 3 * GROUP_WIDTH : 3 * GROUP_WIDTH + LANES]
    route_in = qkv_own[:, 3 * GROUP_WIDTH + LANES :]
    gain_one, gain_two, bias_two = jnp.split(
        dot_cols(jnp.eye(8, LANES, dtype=bf16), small_lanes)[:3], 3, axis=0
    )
    by_device = small_lanes.reshape(devices, rows, LANES)
    route_out = by_device[:, :route_out_rows, 3:7].reshape(RH, 4)
    forced_all = by_device[:, :, 7 : 7 + forced_lanes].reshape(devices, tokens)
    out_own = lax.all_gather(context_exit_matrix, PLANE, axis=0, tiled=True)
    units = ring * hidden_rows
    entry_slots = ring_gather(entries, "za")
    up_own = lax.all_gather(
        after(up_cut, out_own, entry_slots[-1]), "za", axis=0, tiled=True
    )
    slot_ids = jnp.arange(ring, dtype=jnp.int32)
    table_ids = jnp.arange(spot_group_table.shape[0], dtype=jnp.int32)

    def places_of(piece):
        index = ((za - slot_ids) % ring) * plane + (yb - piece) % plane
        spots = jnp.sum(
            jnp.where(index[:, None] == table_ids[None, :], spot_group_table, 0), axis=1
        )
        return spots[:, None] * block_len + jnp.arange(block_len, dtype=jnp.int32)

    all_places = [places_of(piece) for piece in range(plane)]
    query_places = all_places[0].reshape(ring * block_len, 1)
    key_places = jnp.stack(all_places).reshape(plane, 1, ring * block_len)
    half = HD // 2
    inverse = theta_base ** (-(jnp.arange(half, dtype=f32) * (2.0 / HD)))
    angles = all_places[0].astype(f32)[:, :, None] * inverse
    cosine = jnp.concatenate([jnp.cos(angles), jnp.cos(angles)], axis=-1)
    sine = jnp.concatenate([-jnp.sin(angles), jnp.sin(angles)], axis=-1)
    active = (za < sample_channel_fourths).astype(f32)
    active_rows = jnp.broadcast_to(
        active[:, None, None], (seqs, block_len, 1)
    ).reshape(tokens, 1)

    if paired:
        spread = plane_gather
        at = jnp.stack(
            [
                (
                    (za * group + ((yb ^ y) * 2 + (bx ^ x)) * 2 + (bc ^ c)) * seqs + h
                ).astype(jnp.int32)
                for h, x, y, c in CHUNKS
            ]
        )
    else:
        spread = lambda block, between=None: [
            (lax.all_gather(block, PLANE, axis=0, tiled=True),)
        ]
        at = za * group * seqs + jnp.arange(group * seqs, dtype=jnp.int32)
    wide_adjoint = jnp.concatenate(sum(spread(adjoint), ()), axis=0)

    normed_slots, queries, boths = [], [], []
    for slot in range(ring):
        held = after(entry_slots[slot], entry_slots[2 if slot < 2 else ring - 1])
        if slot > 0:
            held = after(held, boths[-1][0])
        held = held.astype(f32)
        inv_rms = lax.rsqrt(jnp.mean(held * held, axis=1, keepdims=True) + epsilon)
        normed_slots.append((held * inv_rms * gain_one).astype(bf16))
        joint = dot(normed_slots[slot], qkv_own)
        query, both = rope(
            joint.reshape(seqs, block_len, joint.shape[1]), cosine[slot], sine[slot]
        )
        queries.append(query)
        boths.append(ring_gather(both, "yb"))
    boths = [[slot[piece] for slot in boths] for piece in range(plane)]
    heads_out, attended, logs = attend(active, queries, boths, query_places, key_places)
    attended = attended.reshape(ring * tokens, GROUP_WIDTH)
    inputs = entries.astype(f32)
    hops = []
    parts = [
        lambda s=s: dot(attended[s * tokens : (s + 1) * tokens], out_own).astype(bf16)
        for s in range(ring)
    ]
    for slot, needed in ((0, wide_adjoint), (2, up_own)):
        block = after(attended[slot * tokens : (slot + 1) * tokens], needed)
        parts[slot] = lambda block=block: dot(block, out_own).astype(bf16)
    hidden = inputs + ring_scatter(parts, "za", hops)
    down_own = lax.all_gather(after(shrink_matrix, hidden), "za", axis=0, tiled=True)

    centre = jnp.mean(hidden, axis=1, keepdims=True)
    centered = hidden - centre
    variance = jnp.mean(centered * centered, axis=1, keepdims=True)
    inv_std = lax.rsqrt(variance + epsilon)
    normal = centered * inv_std
    ffn_in = (normal * gain_two + bias_two).astype(bf16)

    picks = (at[:, None] == jnp.arange(devices * seqs)[None, :]).astype(bf16)
    wide_forced = dot(picks, forced_all.reshape(devices * seqs, block_len)).reshape(
        -1, 1
    )
    route_out_lanes = jnp.pad(route_out, ((0, 0), (0, LANES - 4)))

    def gather_back(groups, came=None, sums=None):
        if paired:
            came = came or plane_scatter_late(groups[1])
            return plane_scatter(groups[0], came, sums)
        return lax.psum_scatter(
            groups[0][0], PLANE, scatter_dimension=0, tiled=True
        ).astype(f32)

    total = wide_adjoint.shape[0]
    kept, firsts, passed = [], [], ()

    def up_part(blocks):
        nonlocal passed
        firsts.append(sum(scale.shape[0] for scale, _ in kept))
        found = feed_up(
            blocks,
            heat_divisor,
            firsts[-1],
            total,
            wide_forced,
            route_in,
            route_out_lanes,
            up_own,
            passed,
        )
        passed = found[:2]
        kept.append(found[2:])
        return found[2]

    groups = spread(ffn_in, up_part)
    up_part(groups[-1])
    wide_in, gated = passed
    down_terms = dot_rows(gated, after(wide_adjoint, down_own)).astype(bf16)
    grad_down = lax.psum_scatter(down_terms, "za", scatter_dimension=0, tiled=True)
    late_adjoint = after(wide_adjoint, down_terms)
    count = len(groups)
    grad_bands, grad_ins, outs = [[None] * count for _ in range(3)]
    passed, came, band_came = (), None, None
    for turn in range(count)[::-1]:
        passed, grad_bands[turn], grad_ins[turn], outs[turn] = feed_down(
            late_adjoint,
            firsts[turn],
            len(groups[turn]),
            *kept[turn],
            gated,
            up_own,
            down_own,
            passed,
        )
        if paired and turn == 1:
            band_came = plane_scatter_late(grad_bands[1])
            came = plane_scatter_late(grad_ins[1])
            passed = after(passed, came[0])
    (grad_up,) = passed
    if paired:
        grad_ins[0] = after(grad_ins[0], came)
    sums = []
    grad_ffn_in = gather_back(grad_ins, came, sums)
    grad_bands[0] = after(grad_bands[0], sums)
    grad_band_home = gather_back(grad_bands, band_came)

    temperature = heat_divisor[0]
    squashed = jnp.tanh(dot(ffn_in, route_in))
    routed = jax.nn.softmax(dot(squashed.astype(bf16), route_out) / temperature, axis=1)
    is_forced = (forced_home > 0)[:, None]
    grad_mix = jnp.cumsum(grad_band_home, axis=1)
    grad_logits = jnp.where(
        is_forced,
        0.0,
        routed
        * (grad_mix - jnp.sum(routed * grad_mix, axis=1, keepdims=True))
        / temperature,
    ).astype(bf16)
    grad_pre = (dot_cols(grad_logits, route_out) * (1.0 - squashed * squashed)).astype(
        bf16
    )
    grad_ffn_in = grad_ffn_in + dot_cols(grad_pre, route_in)
    grad_gain_two = jnp.sum(grad_ffn_in * normal, axis=0)
    grad_bias_two = jnp.sum(grad_ffn_in, axis=0)
    grad_normal = grad_ffn_in * gain_two
    grad_hidden = adjoint.astype(f32) + inv_std * (
        grad_normal
        - jnp.mean(grad_normal, axis=1, keepdims=True)
        - normal * jnp.mean(grad_normal * normal, axis=1, keepdims=True)
    )
    grad_low = after(grad_hidden.astype(bf16), grad_down)
    outs = after(outs, grad_low)
    came, steps = None, []
    if paired:
        came = plane_scatter_late(outs[1])
    out_sum = None
    if paired:
        early_outs = add_low(outs[0][0], swap(outs[0][1], "bc"))
        half_rows = early_outs.shape[0] // 2
        steps.append(add_low(early_outs[:half_rows], came[1]))
        steps.append(add_low(early_outs[half_rows:], came[2]))
    else:
        out_sum = gather_back(outs)
    grad_attn = [grad_low, onward(grad_low, "za")]
    up_terms = dot_rows(wide_in, after(grad_up, grad_low)).astype(bf16)
    grad_attn.append(onward(after(grad_attn[1], came[0] if came else (), up_terms), "za"))
    grad_attn.append(onward(after(grad_attn[2], steps), "za"))
    router_parts = after(
        (ffn_in, grad_pre, squashed, grad_logits), grad_attn[2]
    )
    grad_route_in = dot_rows(router_parts[0], router_parts[1]).astype(bf16)
    grad_route_out = dot_rows(router_parts[2].astype(bf16), router_parts[3])
    others = jnp.concatenate(
        [
            grad_gain_two.reshape(devices, rows),
            grad_bias_two.reshape(devices, rows),
            grad_route_out.reshape(devices, 4 * route_out_rows),
            jnp.zeros((devices, RH - 2 * rows - 4 * route_out_rows), f32),
        ],
        axis=1,
    ).astype(bf16)
    small_rows = rows + 16
    small_terms = jnp.concatenate(
        [
            grad_route_in.reshape(devices, rows, RH),
            others[:, None],
            jnp.zeros((devices, 15, RH), bf16),
        ],
        axis=1,
    )
    if paired:
        half_rows = steps[0].shape[0] // 2
        out_sum = jnp.concatenate(
            [
                part[:half_rows].astype(f32) + swap(part[half_rows:], axis).astype(f32)
                for part, axis in zip(steps, ("bx", "yb"))
            ],
            axis=0,
        )
        small_terms = keep_and_swap(
            small_terms.reshape(ring, plane, 2, cores, small_rows, RH), "bc", 3
        )
    else:
        small_terms = lax.psum_scatter(
            small_terms.reshape(ring, group, small_rows, RH),
            PLANE,
            scatter_dimension=1,
            tiled=False,
        )
    result = back((hidden + out_sum).astype(bf16))
    grad_attn[3] = after(grad_attn[3], result, small_terms)
    up_terms = after(up_terms, grad_attn[3])
    up_terms = lax.psum_scatter(up_terms, "za", scatter_dimension=0, tiled=True)
    up_terms = lax.all_to_all(
        up_terms.reshape(group, rows, units), PLANE, 0, 0, tiled=True
    )
    grad_heads = [
        (dot_cols(block, out_own) * active_rows)
        .astype(bf16)
        .reshape(seqs, block_len, GROUP_WIDTH)
        for block in grad_attn
    ]
    grad_queries, grad_keys, grad_values = [], [], []
    for name, chosen in (
        ("attend_back_far", range(1, plane)),
        ("attend_back", range(1)),
    ):
        if len(chosen) == 0:
            continue
        found = attend_back(
            queries,
            [boths[piece] for piece in chosen],
            grad_heads,
            heads_out,
            logs,
            query_places,
            key_places[jnp.array(chosen)],
            name,
        )
        if name == "attend_back_far":
            found, grad_heads = lax.optimization_barrier((found, grad_heads))

            def from_others(grads):
                running = grads[0]
                for term in grads[1:]:
                    running = add_low(term, onward(running, "yb"))
                return onward(running, "yb")

            grad_keys.append(from_others(found[1]))
            grad_values.append(from_others(found[2]))
        else:
            grad_keys.append(found[1][0])
            grad_values.append(found[2][0])
        grad_queries.append(found[0])
    if paired:
        small_terms = keep_and_swap(after(small_terms, grad_queries[0]), "bx", 2)
    joint = query_back(grad_queries, cosine, sine)
    attn_wide = jnp.concatenate(grad_attn, axis=0)
    normed_wide = jnp.concatenate(normed_slots, axis=0)

    def to_rows(terms, stages, ready):
        cols = terms.shape[-1]
        if paired:
            terms = plane_reduce(
                terms.reshape(ring, plane, 2, cores, rows, cols), stages, ready
            )
        else:
            terms = lax.psum_scatter(
                terms.reshape(ring, group, rows, cols),
                PLANE,
                scatter_dimension=1,
                tiled=False,
            )
        return rotate(lambda i: lax.dynamic_index_in_dim(terms, i, 0), "za")

    flat_joint = lambda array: array.reshape(ring * tokens, 3 * GROUP_WIDTH)
    query_terms = dot_cols(
        flat_joint(after(joint, grad_keys, grad_values, small_terms))[:, :GROUP_WIDTH],
        qkv_own[:, :GROUP_WIDTH],
    )
    grad_out_terms = dot_rows(after(attended, grad_keys, grad_values), attn_wide).astype(bf16)
    grad_wout = lax.psum_scatter(
        grad_out_terms, PLANE, scatter_dimension=0, tiled=True
    ).astype(f32)
    grad_keys = after(grad_keys, query_terms, grad_out_terms)
    joint = flat_joint(both_back(grad_keys, grad_values, cosine, sine, joint))
    both_own = qkv_own[:, GROUP_WIDTH : 3 * GROUP_WIDTH]
    def low_term(s, ready):
        rows_of = after(joint, ready)[s * tokens : (s + 1) * tokens, GROUP_WIDTH:]
        terms = query_terms[s * tokens : (s + 1) * tokens] + dot_cols(rows_of, both_own)
        return terms.astype(bf16)

    running = after(low_term(1, ()), up_terms)
    moved_once = onward(running, "za")
    weight_terms = dot_rows(normed_wide, after(joint, running)).astype(bf16)
    running = add_low(after(low_term(2, ()), weight_terms), moved_once)
    moved_twice = onward(running, "za")
    stages = []
    qkv_rows = to_rows(weight_terms, stages, (moved_once, ()))
    if paired:
        small_terms = keep_and_swap(after(small_terms, stages[1]), "yb", 1)
    grad_wup = columns([after(up_terms, running)], jnp.arange(group, dtype=jnp.int32), ring)
    running = add_low(after(low_term(3, (running, stages[:1])), stages[:2]), moved_twice)
    moved = onward(running, "za")
    small_sum = sum(
        part.astype(f32)
        for part in rotate(
            lambda i: lax.dynamic_index_in_dim(
                after(small_terms, running, stages[2:]), i, 0, keepdims=False
            ),
            "za",
        )
    )
    last = after(low_term(0, running), stages[2:], grad_wup, result, small_sum)
    grad_normed = last.astype(f32) + moved.astype(f32)
    grad_wqkv = columns(qkv_rows, ((za - slot_ids) % ring).astype(jnp.int32), 3)
    weight_rows = triple_projector_matrix.astype(f32)
    grad_gain_one = jnp.sum(grad_wqkv * weight_rows, axis=1) / (
        mixing_rescale_scalers.astype(f32)
    )
    inv_home = lax.rsqrt(jnp.mean(inputs * inputs, axis=1, keepdims=True) + epsilon)
    scaled = inputs * inv_home
    grad_scaled = grad_normed * gain_one
    grad_inputs = grad_hidden + inv_home * (
        grad_scaled - scaled * jnp.mean(grad_scaled * scaled, axis=1, keepdims=True)
    )
    grad_tokens = back(grad_inputs.astype(bf16))
    return (
        result,
        grad_tokens,
        grad_gain_one,
        grad_wqkv,
        grad_wout,
        small_sum[rows, :rows],
        small_sum[rows, rows : 2 * rows],
        grad_wup,
        grad_down.astype(f32),
        small_sum[:rows],
        small_sum[rows, 2 * rows : 2 * rows + 4 * route_out_rows].reshape(-1, 4),
    )


def solution(mesh):
    seq, batch = mesh.shape["seq"], mesh.shape["batch"]
    inner = Mesh(
        mesh.devices.reshape(RING, seq // RING, batch // 2, 2),
        ("za", "yb", "bx", "bc"),
    )
    along, across = ("za", "yb"), ("bx", "bc")
    tokens = P(along, across, None)
    vector = P(along + across)
    matrix = P(along + across, None)
    return jax.shard_map(
        per_device,
        mesh=inner,
        in_specs=(
            tokens,
            tokens,
            vector,
            matrix,
            matrix,
            vector,
            vector,
            matrix,
            matrix,
            matrix,
            matrix,
            P(),
            P(across),
            P(along, across),
            P(),
        ),
        out_specs=(
            tokens,
            tokens,
            vector,
            matrix,
            matrix,
            vector,
            vector,
            matrix,
            matrix,
            matrix,
            matrix,
        ),
        check_vma=False,
    )
```

```python
import functools
import math

import jax
import jax.numpy as jnp
from jax import lax
from jax.experimental import pallas as pl
from jax.experimental.pallas import tpu as pltpu
from jax.sharding import Mesh, PartitionSpec as P

H = 16
HD = 128
FF = 8192
RH = 256
RING = 4
SEQS = 2
GROUP_HEADS = H // RING
GROUP_WIDTH = GROUP_HEADS * HD
SCALE = 1.0 / math.sqrt(HD)
VMEM_LIMIT = 48 * 1024 * 1024
TILE = 256
LANES = 128

epsilon = 1e-05
theta_base = 10000.0
neg_large = -1e30
bf16 = jnp.bfloat16
f32 = jnp.float32
PLANE = ("yb", "bx", "bc")
EVERY = ("za",) + PLANE
SWAP = [(0, 1), (1, 0)]


def dot(left_mat, right_mat):
    return lax.dot_general(
        left_mat, right_mat, (((1,), (0,)), ((), ())), preferred_element_type=f32
    )


def dot_rows(left_mat, right_mat):
    return lax.dot_general(
        left_mat, right_mat, (((0,), (0,)), ((), ())), preferred_element_type=f32
    )


def dot_cols(left_mat, right_mat):
    return lax.dot_general(
        left_mat, right_mat, (((1,), (1,)), ((), ())), preferred_element_type=f32
    )


def onward(block, axis):
    size = lax.axis_size(axis)
    return lax.ppermute(block, axis, [(i, (i + 1) % size) for i in range(size)])


def after(value, *others):
    return lax.optimization_barrier((value, others))[0]


def add_low(left, right):
    return (left.astype(f32) + right.astype(f32)).astype(left.dtype)


def ring_gather(block, axis):
    slots = [block]
    for _ in range(1, lax.axis_size(axis)):
        slots.append(onward(slots[-1], axis))
    return slots


def ring_scatter(parts, axis, hops=None):
    running = parts[1]()
    for slot in range(2, lax.axis_size(axis)):
        moved = onward(running, axis)
        if hops is not None:
            hops.append(moved)
        running = add_low(parts[slot](), moved)
    moved = onward(running, axis)
    return parts[0]().astype(f32) + moved.astype(f32)


def in_order(slots, axis):
    size, me = lax.axis_size(axis), lax.axis_index(axis)
    rows = slots[0].shape[0]
    placed = jnp.zeros((size * rows,) + slots[0].shape[1:], slots[0].dtype)
    for far, slot in enumerate(slots):
        placed = lax.dynamic_update_slice_in_dim(
            placed, slot, (me - far) % size * rows, axis=0
        )
    return placed


def rotate(pieces, axis):
    size, me = lax.axis_size(axis), lax.axis_index(axis)
    came = [pieces(me)]
    for far in range(1, size):
        route = [(i, (i + far) % size) for i in range(size)]
        came.append(lax.ppermute(pieces((me + far) % size), axis, route))
    return came


def exchange(pieces, axis):
    return in_order(
        rotate(lambda i: lax.dynamic_index_in_dim(pieces, i, 0), axis), axis
    )


EARLY = [(0, 0, 0), (0, 1, 0), (1, 0, 0), (1, 0, 1)]
LATE = [(0, 0, 1), (0, 1, 1), (1, 1, 0), (1, 1, 1)]
CHUNKS = [(h, x, y, c) for part in (EARLY, LATE) for c in (0, 1) for h, x, y in part]


def swap(block, axis):
    return lax.ppermute(block, axis, SWAP)


def plane_gather(block, between=lambda early: ()):
    half = block.shape[0] // 2
    first, second = block[:half], block[half:]
    early = jnp.concatenate(
        [first, swap(first, "bx"), second, swap(second, "yb")], axis=0
    )
    late = swap(early[: 2 * half], "yb"), swap(early[2 * half :], "bx")
    groups = [(early, swap(early, "bc"))]
    late = jnp.concatenate(after(late, between(groups[0])), axis=0)
    return groups + [(late, swap(late, "bc"))]


def plane_scatter_late(terms):
    late = add_low(terms[0], swap(terms[1], "bc"))
    half = late.shape[0] // 2
    return late, swap(late[:half], "yb"), swap(late[half:], "bx")


def plane_scatter(terms, came, sums=None):
    rows = terms[0].shape[0] // 4
    early = add_low(terms[0], swap(terms[1], "bc"))
    first = add_low(early[: 2 * rows], came[1])
    second = add_low(early[2 * rows :], came[2])
    if sums is not None:
        sums.extend([first, second])
    first_sum = first[:rows].astype(f32) + swap(first[rows:], "bx").astype(f32)
    second_sum = second[:rows].astype(f32) + swap(second[rows:], "yb").astype(f32)
    return jnp.concatenate([first_sum, second_sum], axis=0)


def keep_and_swap(blocks, axis, dim, ready=()):
    me = lax.axis_index(axis)
    kept = lax.dynamic_index_in_dim(after(blocks, ready), me, dim, keepdims=False)
    sent = lax.dynamic_index_in_dim(blocks, 1 - me, dim, keepdims=False)
    return add_low(kept, swap(sent, axis))


def plane_reduce(blocks, stages=None, ready=((), ())):
    both = keep_and_swap(blocks, "bc", 3, ready[0])
    middle = blocks.shape[-1] // 2
    first = keep_and_swap(both[..., :middle], "yb", 1, ready[1])
    second = keep_and_swap(both[..., middle:], "bx", 2, ready[1])
    if stages is not None:
        stages.extend([both, (first, second)])
    first = keep_and_swap(first, "bx", 1)
    second = keep_and_swap(second, "yb", 1)
    if stages is not None:
        stages.append((first, second))
    return jnp.concatenate([first, second], axis=-1)


def rope_kernel(joint_ref, cos_ref, sin_ref, query_ref, both_ref):
    cosine, sine = cos_ref[...], sin_ref[...]
    for head in range(GROUP_HEADS):
        for part, out_ref in ((0, query_ref), (1, both_ref)):
            at = part * GROUP_WIDTH + head * HD
            raw = joint_ref[0, :, at : at + HD]
            turned = raw * cosine + pltpu.roll(raw, HD // 2, 1) * sine
            out_ref[0, :, head * HD : (head + 1) * HD] = turned.astype(bf16)
    both_ref[0, :, GROUP_WIDTH:] = joint_ref[0, :, 2 * GROUP_WIDTH :].astype(bf16)


def rope(joint, cosine, sine):
    seqs, block_len, width = joint.shape
    rows = lambda w: pl.BlockSpec((1, block_len, w), lambda b: (b, 0, 0))
    table = pl.BlockSpec((block_len, HD), lambda b: (0, 0))
    return pl.pallas_call(
        rope_kernel,
        grid=(seqs,),
        in_specs=[rows(3 * GROUP_WIDTH), table, table],
        out_specs=[rows(GROUP_WIDTH), rows(2 * GROUP_WIDTH)],
        out_shape=[
            jax.ShapeDtypeStruct((seqs, block_len, GROUP_WIDTH), bf16),
            jax.ShapeDtypeStruct((seqs, block_len, 2 * GROUP_WIDTH), bf16),
        ],
        compiler_params=pltpu.CompilerParams(vmem_limit_bytes=VMEM_LIMIT),
        name="rope",
    )(joint, cosine, sine)


def turn_back(grad, cosine, sine):
    return (grad * cosine - pltpu.roll(grad, HD // 2, 1) * sine).astype(bf16)


def query_back_kernel(terms, *refs):
    cos_ref, sin_ref, out_ref = refs[terms:]
    cosine, sine = cos_ref[0], sin_ref[0]
    for seq in range(out_ref.shape[1]):
        for head in range(GROUP_HEADS):
            at = slice(head * HD, (head + 1) * HD)
            grad = sum(ref[0, seq, :, at].astype(f32) for ref in refs[:terms])
            out_ref[0, seq, :, at] = turn_back(grad, cosine, sine)


def both_back_kernel(terms, *refs):
    key_refs, value_refs = refs[:terms], refs[terms : 2 * terms]
    cos_ref, sin_ref, _, out_ref = refs[2 * terms :]

    @pl.when(pl.program_id(1) == 0)
    def _():
        cosine, sine = cos_ref[0], sin_ref[0]
        for seq in range(out_ref.shape[1]):
            for head in range(GROUP_HEADS):
                at = slice(head * HD, (head + 1) * HD)
                grad = sum(ref[0, seq, :, at].astype(f32) for ref in key_refs)
                out_ref[0, seq, :, at] = turn_back(grad, cosine, sine)

    @pl.when(pl.program_id(1) == 1)
    def _():
        total = sum(ref[0].astype(f32) for ref in value_refs)
        out_ref[0] = total.astype(bf16)


def joint_shape(grad):
    return jax.ShapeDtypeStruct(grad.shape[:3] + (3 * GROUP_WIDTH,), bf16)


def query_back(grads, cosine, sine):
    slots, seqs, block_len, width = grads[0].shape
    rows = pl.BlockSpec((1, seqs, block_len, width), lambda s: (s, 0, 0, 0))
    table = pl.BlockSpec((1, block_len, HD), lambda s: (s, 0, 0))
    return pl.pallas_call(
        functools.partial(query_back_kernel, len(grads)),
        grid=(slots,),
        in_specs=[rows] * len(grads) + [table, table],
        out_specs=rows,
        out_shape=joint_shape(grads[0]),
        compiler_params=pltpu.CompilerParams(vmem_limit_bytes=VMEM_LIMIT),
        name="query_back",
    )(*grads, cosine, sine)


def both_back(keys, values, cosine, sine, joint):
    slots, seqs, block_len, width = keys[0].shape
    rows = pl.BlockSpec((1, seqs, block_len, width), lambda s, j: (s, 0, 0, 0))
    table = pl.BlockSpec((1, block_len, HD), lambda s, j: (s, 0, 0))
    terms = len(keys)
    return pl.pallas_call(
        functools.partial(both_back_kernel, terms),
        grid=(slots, 2),
        in_specs=[rows] * (2 * terms)
        + [table, table, pl.BlockSpec(memory_space=pl.ANY)],
        out_specs=pl.BlockSpec(
            (1, seqs, block_len, width), lambda s, j: (s, 0, 0, 1 + j)
        ),
        out_shape=joint_shape(keys[0]),
        input_output_aliases={2 * terms + 2: 0},
        compiler_params=pltpu.CompilerParams(vmem_limit_bytes=VMEM_LIMIT),
        name="both_back",
    )(*keys, *values, cosine, sine, joint)


def flat(ref):
    slots, _, block_len, width = ref.shape
    return ref[:, 0].reshape(slots * block_len, width)


def end_to_end(refs):
    return jnp.concatenate([ref[0] for ref in refs], axis=0)


def by_piece(refs, slots):
    return [refs[i : i + slots] for i in range(0, len(refs), slots)]


def attend_kernel(slots, pieces, *refs):
    active_ref, query_refs = refs[0], refs[1 : 1 + slots]
    rest = refs[1 + slots :]
    key_refs = by_piece(rest[: pieces * slots], slots)
    value_refs = by_piece(rest[pieces * slots : 2 * pieces * slots], slots)
    qplace_ref, kplace_ref, out_ref, low_ref, log_ref = rest[2 * pieces * slots :]
    queries = end_to_end(query_refs)
    query_places = qplace_ref[...]
    masked = []
    for piece in range(pieces):
        scores = dot_cols(queries, end_to_end(key_refs[piece])) * SCALE
        allowed = kplace_ref[piece] <= query_places
        masked.append(jnp.where(allowed, scores, neg_large))
    top = functools.reduce(
        jnp.maximum, [jnp.max(m, axis=1, keepdims=True) for m in masked]
    )
    total, gathered = 0.0, 0.0
    for piece in range(pieces):
        weights = jnp.exp(masked[piece] - top)
        total = total + jnp.sum(weights, axis=1, keepdims=True)
        gathered = gathered + dot(weights.astype(bf16), end_to_end(value_refs[piece]))
    result = gathered / total
    out_ref[:, 0] = result.reshape(out_ref.shape[0], out_ref.shape[2], HD)
    kept = active_ref[pl.program_id(0)]
    low_ref[:, 0] = (
        (result * kept).astype(bf16).reshape(out_ref.shape[0], out_ref.shape[2], HD)
    )
    log_ref[0, 0] = top + jnp.log(total)


def attend(active, queries, boths, query_places, key_places):
    slots, pieces = len(queries), len(boths)
    seqs, block_len, width = queries[0].shape
    rows = slots * block_len
    heads = width // HD
    own = pl.BlockSpec((1, block_len, HD), lambda s, h: (s, 0, h))
    value = pl.BlockSpec((1, block_len, HD), lambda s, h: (s, 0, heads + h))
    tile = pl.BlockSpec((slots, 1, block_len, HD), lambda s, h: (0, s, 0, h))
    every = [both for piece in boths for both in piece]
    shape = (slots, seqs, block_len, width)
    return pl.pallas_call(
        functools.partial(attend_kernel, slots, pieces),
        grid=(seqs, heads),
        in_specs=[pl.BlockSpec(memory_space=pltpu.SMEM)]
        + [own] * slots
        + [own] * len(every)
        + [value] * len(every)
        + [
            pl.BlockSpec((rows, 1), lambda s, h: (0, 0)),
            pl.BlockSpec((pieces, 1, rows), lambda s, h: (0, 0, 0)),
        ],
        out_specs=[
            tile,
            tile,
            pl.BlockSpec((1, 1, rows, 1), lambda s, h: (s, h, 0, 0)),
        ],
        out_shape=[
            jax.ShapeDtypeStruct(shape, f32),
            jax.ShapeDtypeStruct(shape, bf16),
            jax.ShapeDtypeStruct((seqs, heads, rows, 1), f32),
        ],
        compiler_params=pltpu.CompilerParams(vmem_limit_bytes=VMEM_LIMIT),
        name="attend",
    )(active, *queries, *every, *every, query_places, key_places)


def attend_back_kernel(slots, pieces, *refs):
    query_refs, rest = refs[:slots], refs[slots:]
    key_refs = by_piece(rest[: pieces * slots], slots)
    value_refs = by_piece(rest[pieces * slots : 2 * pieces * slots], slots)
    rest = rest[2 * pieces * slots :]
    grad_refs, rest = rest[:slots], rest[slots:]
    out_ref, log_ref, qplace_ref, kplace_ref, dq_ref = rest[:5]
    dk_refs, dv_refs = rest[5 : 5 + pieces], rest[5 + pieces :]
    queries, grads = end_to_end(query_refs), end_to_end(grad_refs)
    query_places = qplace_ref[...]
    dots = jnp.sum(grads.astype(f32) * flat(out_ref), axis=1, keepdims=True)
    log_norm = log_ref[0, 0]
    grad_query = 0.0
    shape = (slots, query_refs[0].shape[1], HD)
    for piece in range(pieces):
        keys, values = end_to_end(key_refs[piece]), end_to_end(value_refs[piece])
        scores = dot_cols(queries, keys) * SCALE
        allowed = kplace_ref[piece] <= query_places
        probs = jnp.exp(jnp.where(allowed, scores - log_norm, neg_large))
        grad_probs = dot_cols(grads, values)
        dv_refs[piece][:, 0] = (
            dot_rows(probs.astype(bf16), grads)
            .astype(dv_refs[piece].dtype)
            .reshape(shape)
        )
        grad_scores = (probs * (grad_probs - dots)).astype(bf16)
        dk_refs[piece][:, 0] = (
            (dot_rows(grad_scores, queries) * SCALE)
            .astype(dk_refs[piece].dtype)
            .reshape(shape)
        )
        grad_query = grad_query + dot(grad_scores, keys)
    dq_ref[:, 0] = (grad_query * SCALE).reshape(shape)


def attend_back(queries, boths, grads, out, logs, query_places, key_places, name):
    slots, pieces = len(queries), len(boths)
    seqs, block_len, width = queries[0].shape
    rows = slots * block_len
    heads = width // HD
    own = pl.BlockSpec((1, block_len, HD), lambda s, h: (s, 0, h))
    value = pl.BlockSpec((1, block_len, HD), lambda s, h: (s, 0, heads + h))
    tile = pl.BlockSpec((slots, 1, block_len, HD), lambda s, h: (0, s, 0, h))
    every = [both for piece in boths for both in piece]
    shape = (slots, seqs, block_len, width)
    wide = jax.ShapeDtypeStruct(shape, f32)
    low = jax.ShapeDtypeStruct(shape, bf16)
    found = pl.pallas_call(
        functools.partial(attend_back_kernel, slots, pieces),
        grid=(seqs, heads),
        in_specs=[own] * slots
        + [own] * len(every)
        + [value] * len(every)
        + [own] * slots
        + [
            tile,
            pl.BlockSpec((1, 1, rows, 1), lambda s, h: (s, h, 0, 0)),
            pl.BlockSpec((rows, 1), lambda s, h: (0, 0)),
            pl.BlockSpec((pieces, 1, rows), lambda s, h: (0, 0, 0)),
        ],
        out_specs=[tile] * (1 + 2 * pieces),
        out_shape=[wide] + [low] * (2 * pieces),
        compiler_params=pltpu.CompilerParams(vmem_limit_bytes=VMEM_LIMIT),
        name=name,
    )(*queries, *every, *every, *grads, out, logs, query_places, key_places)
    return found[0], found[1 : 1 + pieces], found[1 + pieces :]


def feed_up_kernel(steps, blocks, passed, *refs):
    in_refs, refs = refs[:blocks], refs[blocks:]
    heat_ref, forced_ref, route_in_ref, route_out_ref, up_ref = refs[:5]
    all_in_ref, gated_ref, scale_ref, rectified_ref = refs[5 + passed :]
    block = in_refs[0][...]
    for k in range(1, blocks):
        block = jnp.where(pl.program_id(0) < k * steps, block, in_refs[k][...])
    all_in_ref[...] = block
    units = up_ref.shape[1]
    band = units // 4

    squashed = jnp.tanh(dot(block, route_in_ref[...])).astype(bf16)
    logits = dot(squashed, route_out_ref[...]) / heat_ref[0]
    lane = lax.broadcasted_iota(jnp.int32, logits.shape, 1)
    logits = jnp.where(lane < 4, logits, neg_large)
    weights = jnp.exp(logits - jnp.max(logits, axis=1, keepdims=True))
    routed = weights / jnp.sum(weights, axis=1, keepdims=True)
    forced = forced_ref[...]
    chosen = jnp.where(lane.astype(f32) == forced - 1.0, 1.0, 0.0)
    mix = jnp.where(forced > 0.0, chosen, routed)
    scales = [mix[:, 3:4]]
    for k in (2, 1, 0):
        scales.insert(0, scales[0] + mix[:, k : k + 1])
    scale_ref[...] = by_lane(scales, scale_ref.shape)

    rectified = jnp.maximum(dot(block, up_ref[...]), 0.0)
    rectified_ref[...] = rectified
    gated_ref[...] = (rectified * rectified * by_band(scales, band, units)).astype(bf16)


def by_lane(columns, shape):
    lane = lax.broadcasted_iota(jnp.int32, shape, 1)
    found = jnp.zeros(shape, f32)
    for k, column in enumerate(columns):
        found = jnp.where(lane == k, column, found)
    return found


def by_band(columns, band, units):
    rows = columns[0].shape[0]
    if band % LANES == 0:
        return jnp.concatenate(
            [jnp.broadcast_to(column, (rows, band)) for column in columns], axis=1
        )
    at = lax.broadcasted_iota(jnp.int32, (rows, units), 1) // band
    found = jnp.broadcast_to(columns[3], (rows, units))
    for k in range(3):
        found = jnp.where(at == k, columns[k], found)
    return found


def band_sums(array, band):
    if band % LANES == 0:
        parts = [array[:, k * band : (k + 1) * band] for k in range(4)]
    else:
        at = lax.broadcasted_iota(jnp.int32, array.shape, 1) // band
        parts = [jnp.where(at == k, array, 0.0) for k in range(4)]
    return [jnp.sum(part, axis=1, keepdims=True) for part in parts]


def feed_down_kernel(count, steps, passed, *refs):
    adjoint_ref, scale_ref, rectified_ref, gated_ref, up_ref, down_ref = refs[:6]
    grad_up_ref, split_refs = refs[6 + passed], refs[7 + passed :]
    units = up_ref.shape[1]
    band = units // 4
    down = down_ref[...]
    rectified = rectified_ref[...]
    grad_gated = dot_cols(adjoint_ref[...], down)
    scales = [scale_ref[:, k : k + 1] for k in range(4)]
    twice = grad_gated * rectified
    grad_up = (twice * by_band(scales, band, units) * 2.0).astype(bf16)
    grad_up_ref[...] = grad_up
    sums = by_lane(band_sums(twice * rectified, band), split_refs[0].shape)
    grad_in = dot_cols(grad_up, up_ref[...]).astype(bf16)
    out = dot(gated_ref[...], down).astype(bf16)
    for k in range(count):

        @pl.when(pl.program_id(0) // steps == k)
        def _():
            for kind, value in enumerate((sums, grad_in, out)):
                split_refs[kind * count + k][...] = value


def tiles(width, at=0):
    return pl.BlockSpec((TILE, width), lambda i: (at + i, 0))


def fixed(array):
    return pl.BlockSpec(array.shape, lambda i: (0, 0), pipeline_mode=pl.Buffered(1))


def feed_up(blocks, heat, first, total, forced, route_in, route_out, up, passed):
    rows, width = blocks[0].shape
    tokens, count = rows * len(blocks), len(blocks)
    units = up.shape[1]
    at, steps = first // TILE, rows // TILE
    share = lambda k: pl.BlockSpec(
        (TILE, width), lambda i: (jnp.clip(i - k * steps, 0, steps - 1), 0)
    )
    before = count + 5
    return pl.pallas_call(
        functools.partial(feed_up_kernel, steps, count, len(passed)),
        grid=(tokens // TILE,),
        in_specs=[share(k) for k in range(count)]
        + [
            pl.BlockSpec(memory_space=pltpu.SMEM),
            tiles(1, at),
            fixed(route_in),
            fixed(route_out),
            fixed(up),
        ]
        + [pl.BlockSpec(memory_space=pl.ANY)] * len(passed),
        out_specs=[tiles(width, at), tiles(units, at), tiles(4), tiles(units)],
        out_shape=[
            jax.ShapeDtypeStruct((total, width), bf16),
            jax.ShapeDtypeStruct((total, units), bf16),
            jax.ShapeDtypeStruct((tokens, 4), f32),
            jax.ShapeDtypeStruct((tokens, units), f32),
        ],
        input_output_aliases={before + i: i for i in range(len(passed))},
        compiler_params=pltpu.CompilerParams(vmem_limit_bytes=VMEM_LIMIT),
        cost_estimate=pl.CostEstimate(
            flops=2 * tokens * width * units,
            bytes_accessed=2 * width * units + 6 * tokens * width,
            transcendentals=0,
        ),
        name="feed_up",
    )(*blocks, heat, forced, route_in, route_out, up, *passed)


def feed_down(adjoint, first, count, scale, rectified, gated, up, down, passed):
    total, width = adjoint.shape
    tokens, units = rectified.shape
    rows = tokens // count
    at, steps = first // TILE, rows // TILE
    share = lambda k, cols: pl.BlockSpec(
        (TILE, cols), lambda i: (jnp.clip(i - k * steps, 0, steps - 1), 0)
    )
    kinds = ((4, f32), (width, bf16), (width, bf16))
    found = pl.pallas_call(
        functools.partial(feed_down_kernel, count, steps, len(passed)),
        grid=(tokens // TILE,),
        in_specs=[
            tiles(width, at),
            tiles(4),
            tiles(units),
            tiles(units, at),
            fixed(up),
            fixed(down),
        ]
        + [pl.BlockSpec(memory_space=pl.ANY)] * len(passed),
        out_specs=[tiles(units, at)]
        + [share(k, cols) for cols, _ in kinds for k in range(count)],
        out_shape=[jax.ShapeDtypeStruct((total, units), bf16)]
        + [
            jax.ShapeDtypeStruct((rows, cols), dtype)
            for cols, dtype in kinds
            for _ in range(count)
        ],
        input_output_aliases={6 + i: i for i in range(len(passed))},
        compiler_params=pltpu.CompilerParams(vmem_limit_bytes=VMEM_LIMIT),
        cost_estimate=pl.CostEstimate(
            flops=6 * tokens * width * units,
            bytes_accessed=4 * width * units + 8 * tokens * width,
            transcendentals=0,
        ),
        name="feed_down",
    )(adjoint, scale, rectified, gated, up, down, *passed)
    return found[:1], *[found[1 + k * count : 1 + (k + 1) * count] for k in range(3)]


def columns_kernel(parts, *refs):
    place_ref, piece_refs, out_ref = refs[0], refs[1:-1], refs[-1]
    places = out_ref.shape[1] // piece_refs[0].shape[2]
    cols = piece_refs[0].shape[2] // parts
    place = 0
    for ref in piece_refs:
        for i in range(ref.shape[0]):
            for part in range(parts):
                at = pl.multiple_of((part * places + place_ref[place]) * cols, cols)
                block = ref[i, :, part * cols : (part + 1) * cols]
                out_ref[:, pl.ds(at, cols)] = block.astype(f32)
            place += 1


def columns(pieces, places, parts):
    count = sum(piece.shape[0] for piece in pieces)
    _, rows, cols = pieces[0].shape
    if cols // parts % LANES:
        every = jnp.concatenate(pieces, axis=0)[jnp.argsort(places)]
        every = every.reshape(count, rows, parts, cols // parts)
        return jnp.transpose(every, (1, 2, 0, 3)).reshape(rows, -1).astype(f32)
    return pl.pallas_call(
        functools.partial(columns_kernel, parts),
        in_specs=[pl.BlockSpec(memory_space=pltpu.SMEM)]
        + [pl.BlockSpec(memory_space=pltpu.VMEM)] * len(pieces),
        out_specs=pl.BlockSpec(memory_space=pltpu.VMEM),
        out_shape=jax.ShapeDtypeStruct((rows, count * cols), f32),
        compiler_params=pltpu.CompilerParams(vmem_limit_bytes=VMEM_LIMIT),
        name="columns",
    )(places, *pieces)


def per_device(
    layer_entries,
    incoming_adjoint,
    mixing_rescale_scalers,
    triple_projector_matrix,
    context_exit_matrix,
    dense_center_scaler,
    dense_center_offset,
    expand_matrix,
    shrink_matrix,
    span_chooser_initial,
    span_chooser_final,
    heat_divisor,
    sample_channel_fourths,
    element_preset_span,
    spot_group_table,
):
    block_len, seqs, width = layer_entries.shape
    tokens = block_len * seqs
    ring, plane = lax.axis_size("za"), lax.axis_size("yb")
    cores = lax.axis_size("bc")
    group = plane * lax.axis_size("bx") * cores
    devices = ring * group
    paired = plane == 2 and lax.axis_size("bx") == 2 and cores == 2
    za, yb = lax.axis_index("za"), lax.axis_index("yb")
    bx, bc = lax.axis_index("bx"), lax.axis_index("bc")
    rows = width // devices
    hidden_rows = FF // devices

    def home(array):
        return jnp.transpose(array, (1, 0, 2)).reshape(tokens, width)

    def back(array):
        return jnp.transpose(array.reshape(seqs, block_len, width), (1, 0, 2))

    entries, adjoint = home(layer_entries), home(incoming_adjoint)

    forced_home = jnp.transpose(element_preset_span, (1, 0)).reshape(tokens)
    forced_lanes = tokens // rows
    route_out_rows = span_chooser_final.shape[0]
    small_lanes = jnp.concatenate(
        [
            mixing_rescale_scalers[:, None],
            dense_center_scaler[:, None],
            dense_center_offset[:, None],
            jnp.pad(span_chooser_final, ((0, rows - route_out_rows), (0, 0))),
            forced_home.astype(bf16).reshape(rows, forced_lanes),
            jnp.zeros((rows, LANES - 7 - forced_lanes), bf16),
        ],
        axis=1,
    )
    qkv_cut = jnp.concatenate(
        [
            jnp.transpose(
                triple_projector_matrix.reshape(rows, 3, ring, GROUP_WIDTH),
                (2, 0, 1, 3),
            ).reshape(ring, rows, 3 * GROUP_WIDTH),
            jnp.broadcast_to(small_lanes, (ring, rows, LANES)),
            jnp.broadcast_to(span_chooser_initial, (ring, rows, RH)),
        ],
        axis=2,
    )
    units = ring * hidden_rows
    up_cut = jnp.transpose(
        expand_matrix.reshape(rows, ring, group, hidden_rows), (2, 0, 1, 3)
    ).reshape(group, rows, units)
    up_cut = lax.all_to_all(up_cut, PLANE, 0, 0, tiled=True).reshape(group * rows, units)
    qkv_cut = after(exchange(qkv_cut, "za"), up_cut)
    qkv_own = lax.all_gather(qkv_cut, PLANE, axis=1, tiled=False).reshape(width, 3 * GROUP_WIDTH + LANES + RH)
    small_lanes = qkv_own[:, 3 * GROUP_WIDTH : 3 * GROUP_WIDTH + LANES]
    route_in = qkv_own[:, 3 * GROUP_WIDTH + LANES :]
    gain_one, gain_two, bias_two = jnp.split(
        dot_cols(jnp.eye(8, LANES, dtype=bf16), small_lanes)[:3], 3, axis=0
    )
    by_device = small_lanes.reshape(devices, rows, LANES)
    route_out = by_device[:, :route_out_rows, 3:7].reshape(RH, 4)
    forced_all = by_device[:, :, 7 : 7 + forced_lanes].reshape(devices, tokens)
    out_own = lax.all_gather(context_exit_matrix, PLANE, axis=0, tiled=True)
    units = ring * hidden_rows
    entry_slots = ring_gather(entries, "za")
    up_own = lax.all_gather(
        after(up_cut, out_own, entry_slots[-1]), "za", axis=0, tiled=True
    )
    slot_ids = jnp.arange(ring, dtype=jnp.int32)
    table_ids = jnp.arange(spot_group_table.shape[0], dtype=jnp.int32)

    def places_of(piece):
        index = ((za - slot_ids) % ring) * plane + (yb - piece) % plane
        spots = jnp.sum(
            jnp.where(index[:, None] == table_ids[None, :], spot_group_table, 0), axis=1
        )
        return spots[:, None] * block_len + jnp.arange(block_len, dtype=jnp.int32)

    all_places = [places_of(piece) for piece in range(plane)]
    query_places = all_places[0].reshape(ring * block_len, 1)
    key_places = jnp.stack(all_places).reshape(plane, 1, ring * block_len)
    half = HD // 2
    inverse = theta_base ** (-(jnp.arange(half, dtype=f32) * (2.0 / HD)))
    angles = all_places[0].astype(f32)[:, :, None] * inverse
    cosine = jnp.concatenate([jnp.cos(angles), jnp.cos(angles)], axis=-1)
    sine = jnp.concatenate([-jnp.sin(angles), jnp.sin(angles)], axis=-1)
    active = (za < sample_channel_fourths).astype(f32)
    active_rows = jnp.broadcast_to(
        active[:, None, None], (seqs, block_len, 1)
    ).reshape(tokens, 1)

    if paired:
        spread = plane_gather
        at = jnp.stack(
            [
                (
                    (za * group + ((yb ^ y) * 2 + (bx ^ x)) * 2 + (bc ^ c)) * seqs + h
                ).astype(jnp.int32)
                for h, x, y, c in CHUNKS
            ]
        )
    else:
        spread = lambda block, between=None: [
            (lax.all_gather(block, PLANE, axis=0, tiled=True),)
        ]
        at = za * group * seqs + jnp.arange(group * seqs, dtype=jnp.int32)
    wide_adjoint = jnp.concatenate(sum(spread(adjoint), ()), axis=0)

    normed_slots, queries, boths = [], [], []
    for slot in range(ring):
        held = after(entry_slots[slot], entry_slots[2 if slot < 2 else ring - 1])
        if slot > 0:
            held = after(held, boths[-1][0])
        held = held.astype(f32)
        inv_rms = lax.rsqrt(jnp.mean(held * held, axis=1, keepdims=True) + epsilon)
        normed_slots.append((held * inv_rms * gain_one).astype(bf16))
        joint = dot(normed_slots[slot], qkv_own)
        query, both = rope(
            joint.reshape(seqs, block_len, joint.shape[1]), cosine[slot], sine[slot]
        )
        queries.append(query)
        boths.append(ring_gather(both, "yb"))
    boths = [[slot[piece] for slot in boths] for piece in range(plane)]
    heads_out, attended, logs = attend(active, queries, boths, query_places, key_places)
    attended = attended.reshape(ring * tokens, GROUP_WIDTH)
    inputs = entries.astype(f32)
    hops = []
    parts = [
        lambda s=s: dot(attended[s * tokens : (s + 1) * tokens], out_own).astype(bf16)
        for s in range(ring)
    ]
    for slot, needed in ((0, wide_adjoint), (2, up_own)):
        block = after(attended[slot * tokens : (slot + 1) * tokens], needed)
        parts[slot] = lambda block=block: dot(block, out_own).astype(bf16)
    hidden = inputs + ring_scatter(parts, "za", hops)
    down_own = lax.all_gather(after(shrink_matrix, hidden), "za", axis=0, tiled=True)

    centre = jnp.mean(hidden, axis=1, keepdims=True)
    centered = hidden - centre
    variance = jnp.mean(centered * centered, axis=1, keepdims=True)
    inv_std = lax.rsqrt(variance + epsilon)
    normal = centered * inv_std
    ffn_in = (normal * gain_two + bias_two).astype(bf16)

    picks = (at[:, None] == jnp.arange(devices * seqs)[None, :]).astype(bf16)
    wide_forced = dot(picks, forced_all.reshape(devices * seqs, block_len)).reshape(
        -1, 1
    )
    route_out_lanes = jnp.pad(route_out, ((0, 0), (0, LANES - 4)))

    def gather_back(groups, came=None, sums=None):
        if paired:
            came = came or plane_scatter_late(groups[1])
            return plane_scatter(groups[0], came, sums)
        return lax.psum_scatter(
            groups[0][0], PLANE, scatter_dimension=0, tiled=True
        ).astype(f32)

    total = wide_adjoint.shape[0]
    kept, firsts, passed = [], [], ()

    def up_part(blocks):
        nonlocal passed
        firsts.append(sum(scale.shape[0] for scale, _ in kept))
        found = feed_up(
            blocks,
            heat_divisor,
            firsts[-1],
            total,
            wide_forced,
            route_in,
            route_out_lanes,
            up_own,
            passed,
        )
        passed = found[:2]
        kept.append(found[2:])
        return found[2]

    groups = spread(ffn_in, up_part)
    up_part(groups[-1])
    wide_in, gated = passed
    down_terms = dot_rows(gated, after(wide_adjoint, down_own)).astype(bf16)
    grad_down = lax.psum_scatter(down_terms, "za", scatter_dimension=0, tiled=True)
    late_adjoint = after(wide_adjoint, down_terms)
    count = len(groups)
    grad_bands, grad_ins, outs = [[None] * count for _ in range(3)]
    passed, came, band_came = (), None, None
    for turn in range(count)[::-1]:
        passed, grad_bands[turn], grad_ins[turn], outs[turn] = feed_down(
            late_adjoint,
            firsts[turn],
            len(groups[turn]),
            *kept[turn],
            gated,
            up_own,
            down_own,
            passed,
        )
        if paired and turn == 1:
            band_came = plane_scatter_late(grad_bands[1])
            came = plane_scatter_late(grad_ins[1])
            passed = after(passed, came[0])
    (grad_up,) = passed
    if paired:
        grad_ins[0] = after(grad_ins[0], came)
    sums = []
    grad_ffn_in = gather_back(grad_ins, came, sums)
    grad_bands[0] = after(grad_bands[0], sums)
    grad_band_home = gather_back(grad_bands, band_came)

    temperature = heat_divisor[0]
    squashed = jnp.tanh(dot(ffn_in, route_in))
    routed = jax.nn.softmax(dot(squashed.astype(bf16), route_out) / temperature, axis=1)
    is_forced = (forced_home > 0)[:, None]
    grad_mix = jnp.cumsum(grad_band_home, axis=1)
    grad_logits = jnp.where(
        is_forced,
        0.0,
        routed
        * (grad_mix - jnp.sum(routed * grad_mix, axis=1, keepdims=True))
        / temperature,
    ).astype(bf16)
    grad_pre = (dot_cols(grad_logits, route_out) * (1.0 - squashed * squashed)).astype(
        bf16
    )
    grad_ffn_in = grad_ffn_in + dot_cols(grad_pre, route_in)
    grad_gain_two = jnp.sum(grad_ffn_in * normal, axis=0)
    grad_bias_two = jnp.sum(grad_ffn_in, axis=0)
    grad_normal = grad_ffn_in * gain_two
    grad_hidden = adjoint.astype(f32) + inv_std * (
        grad_normal
        - jnp.mean(grad_normal, axis=1, keepdims=True)
        - normal * jnp.mean(grad_normal * normal, axis=1, keepdims=True)
    )
    grad_low = after(grad_hidden.astype(bf16), grad_down)
    outs = after(outs, grad_low)
    came, steps = None, []
    if paired:
        came = plane_scatter_late(outs[1])
    out_sum = None
    if paired:
        early_outs = add_low(outs[0][0], swap(outs[0][1], "bc"))
        half_rows = early_outs.shape[0] // 2
        steps.append(add_low(early_outs[:half_rows], came[1]))
        steps.append(add_low(early_outs[half_rows:], came[2]))
    else:
        out_sum = gather_back(outs)
    grad_attn = [grad_low, onward(grad_low, "za")]
    up_terms = dot_rows(wide_in, after(grad_up, grad_low)).astype(bf16)

    def head_grads(block):
        heads = (dot_cols(block, out_own) * active_rows).astype(bf16)
        return heads.reshape(seqs, block_len, GROUP_WIDTH)

    grad_heads = [head_grads(grad_attn[0])]
    beside = (came[0] if came else (), up_terms, grad_heads[0])
    grad_attn.append(onward(after(grad_attn[1], beside), "za"))
    grad_heads.append(head_grads(grad_attn[1]))
    grad_attn.append(onward(after(grad_attn[2], grad_heads[1], steps), "za"))
    grad_heads.append(head_grads(grad_attn[2]))
    router_parts = after(
        (ffn_in, grad_pre, squashed, grad_logits, grad_gain_two, grad_bias_two),
        grad_attn[2],
    )
    grad_route_in = dot_rows(router_parts[0], router_parts[1]).astype(bf16)
    grad_route_out = dot_rows(router_parts[2].astype(bf16), router_parts[3])
    others = jnp.concatenate(
        [
            router_parts[4].reshape(devices, rows),
            router_parts[5].reshape(devices, rows),
            grad_route_out.reshape(devices, 4 * route_out_rows),
            jnp.zeros((devices, RH - 2 * rows - 4 * route_out_rows), f32),
        ],
        axis=1,
    ).astype(bf16)
    small_rows = rows + 16
    small_terms = jnp.concatenate(
        [
            grad_route_in.reshape(devices, rows, RH),
            others[:, None],
            jnp.zeros((devices, 15, RH), bf16),
        ],
        axis=1,
    )
    if paired:
        half_rows = steps[0].shape[0] // 2
        out_sum = jnp.concatenate(
            [
                part[:half_rows].astype(f32) + swap(part[half_rows:], axis).astype(f32)
                for part, axis in zip(steps, ("bx", "yb"))
            ],
            axis=0,
        )
        small_terms = keep_and_swap(
            small_terms.reshape(ring, plane, 2, cores, small_rows, RH), "bc", 3
        )
    else:
        small_terms = lax.psum_scatter(
            small_terms.reshape(ring, group, small_rows, RH),
            PLANE,
            scatter_dimension=1,
            tiled=False,
        )
    result = back((hidden + out_sum).astype(bf16))
    grad_attn[3] = after(grad_attn[3], result, small_terms, grad_heads[2])
    grad_heads.append(head_grads(grad_attn[3]))
    up_terms = after(up_terms, grad_attn[3])
    up_terms = lax.psum_scatter(up_terms, "za", scatter_dimension=0, tiled=True)
    up_terms = lax.all_to_all(
        up_terms.reshape(group, rows, units), PLANE, 0, 0, tiled=True
    )
    grad_queries, grad_keys, grad_values = [], [], []
    for name, chosen in (
        ("attend_back_far", range(1, plane)),
        ("attend_back", range(1)),
    ):
        if len(chosen) == 0:
            continue
        found = attend_back(
            queries,
            [boths[piece] for piece in chosen],
            grad_heads,
            heads_out,
            logs,
            query_places,
            key_places[jnp.array(chosen)],
            name,
        )
        if name == "attend_back_far":
            found, grad_heads = lax.optimization_barrier((found, grad_heads))

            def from_others(grads):
                running = grads[0]
                for term in grads[1:]:
                    running = add_low(term, onward(running, "yb"))
                return onward(running, "yb")

            grad_keys.append(from_others(found[1]))
            grad_values.append(from_others(found[2]))
        else:
            grad_keys.append(found[1][0])
            grad_values.append(found[2][0])
        grad_queries.append(found[0])
    if paired:
        small_terms = keep_and_swap(after(small_terms, grad_queries[0]), "bx", 2)
    joint = query_back(grad_queries, cosine, sine)
    attn_wide = jnp.concatenate(grad_attn, axis=0)
    normed_wide = jnp.concatenate(normed_slots, axis=0)

    def to_rows(terms, stages, ready):
        cols = terms.shape[-1]
        if paired:
            terms = plane_reduce(
                terms.reshape(ring, plane, 2, cores, rows, cols), stages, ready
            )
        else:
            terms = lax.psum_scatter(
                terms.reshape(ring, group, rows, cols),
                PLANE,
                scatter_dimension=1,
                tiled=False,
            )
        return rotate(lambda i: lax.dynamic_index_in_dim(terms, i, 0), "za")

    flat_joint = lambda array: array.reshape(ring * tokens, 3 * GROUP_WIDTH)
    query_terms = dot_cols(
        flat_joint(after(joint, grad_keys, grad_values, small_terms))[:, :GROUP_WIDTH],
        qkv_own[:, :GROUP_WIDTH],
    )
    grad_out_terms = dot_rows(after(attended, grad_keys, grad_values), attn_wide).astype(bf16)
    grad_wout = lax.psum_scatter(
        grad_out_terms, PLANE, scatter_dimension=0, tiled=True
    ).astype(f32)
    grad_keys = after(grad_keys, query_terms, grad_out_terms)
    joint = flat_joint(both_back(grad_keys, grad_values, cosine, sine, joint))
    both_own = qkv_own[:, GROUP_WIDTH : 3 * GROUP_WIDTH]
    def low_term(s, ready):
        rows_of = after(joint, ready)[s * tokens : (s + 1) * tokens, GROUP_WIDTH:]
        terms = query_terms[s * tokens : (s + 1) * tokens] + dot_cols(rows_of, both_own)
        return terms.astype(bf16)

    running = after(low_term(1, ()), up_terms)
    moved_once = onward(running, "za")
    weight_terms = dot_rows(normed_wide, after(joint, running)).astype(bf16)
    running = add_low(after(low_term(2, ()), weight_terms), moved_once)
    moved_twice = onward(running, "za")
    stages = []
    qkv_rows = to_rows(weight_terms, stages, (moved_once, ()))
    if paired:
        small_terms = keep_and_swap(after(small_terms, stages[1]), "yb", 1)
    grad_wup = columns([after(up_terms, running)], jnp.arange(group, dtype=jnp.int32), ring)
    running = add_low(after(low_term(3, (running, stages[:1])), stages[:2]), moved_twice)
    moved = onward(running, "za")
    small_sum = sum(
        part.astype(f32)
        for part in rotate(
            lambda i: lax.dynamic_index_in_dim(
                after(small_terms, qkv_rows[1:]), i, 0, keepdims=False
            ),
            "za",
        )
    )
    last = after(low_term(0, running), stages[2:], grad_wup, result)
    grad_normed = last.astype(f32) + moved.astype(f32)
    inv_home = lax.rsqrt(jnp.mean(inputs * inputs, axis=1, keepdims=True) + epsilon)
    scaled = inputs * inv_home
    grad_scaled = grad_normed * gain_one
    grad_inputs = grad_hidden + inv_home * (
        grad_scaled - scaled * jnp.mean(grad_scaled * scaled, axis=1, keepdims=True)
    )
    grad_tokens = back(grad_inputs.astype(bf16))
    grad_wqkv = columns(after(qkv_rows, grad_tokens), ((za - slot_ids) % ring).astype(jnp.int32), 3)
    weight_rows = triple_projector_matrix.astype(f32)
    grad_gain_one = jnp.sum(grad_wqkv * weight_rows, axis=1) / (
        mixing_rescale_scalers.astype(f32)
    )
    return (
        result,
        grad_tokens,
        grad_gain_one,
        grad_wqkv,
        grad_wout,
        small_sum[rows, :rows],
        small_sum[rows, rows : 2 * rows],
        grad_wup,
        grad_down.astype(f32),
        small_sum[:rows],
        small_sum[rows, 2 * rows : 2 * rows + 4 * route_out_rows].reshape(-1, 4),
    )


def solution(mesh):
    seq, batch = mesh.shape["seq"], mesh.shape["batch"]
    inner = Mesh(
        mesh.devices.reshape(RING, seq // RING, batch // 2, 2),
        ("za", "yb", "bx", "bc"),
    )
    along, across = ("za", "yb"), ("bx", "bc")
    tokens = P(along, across, None)
    vector = P(along + across)
    matrix = P(along + across, None)
    return jax.shard_map(
        per_device,
        mesh=inner,
        in_specs=(
            tokens,
            tokens,
            vector,
            matrix,
            matrix,
            vector,
            vector,
            matrix,
            matrix,
            matrix,
            matrix,
            P(),
            P(across),
            P(along, across),
            P(),
        ),
        out_specs=(
            tokens,
            tokens,
            vector,
            matrix,
            matrix,
            vector,
            vector,
            matrix,
            matrix,
            matrix,
            matrix,
        ),
        check_vma=False,
    )
```

```python
import functools
import math

import jax
import jax.numpy as jnp
from jax import lax
from jax.experimental import pallas as pl
from jax.experimental.pallas import tpu as pltpu
from jax.sharding import Mesh, PartitionSpec as P

H = 16
HD = 128
FF = 8192
RH = 256
RING = 4
SEQS = 2
GROUP_HEADS = H // RING
GROUP_WIDTH = GROUP_HEADS * HD
SCALE = 1.0 / math.sqrt(HD)
VMEM_LIMIT = 48 * 1024 * 1024
TILE = 256
LANES = 128

epsilon = 1e-05
theta_base = 10000.0
neg_large = -1e30
bf16 = jnp.bfloat16
f32 = jnp.float32
PLANE = ("yb", "bx", "bc")
EVERY = ("za",) + PLANE
SWAP = [(0, 1), (1, 0)]


def dot(left_mat, right_mat):
    return lax.dot_general(
        left_mat, right_mat, (((1,), (0,)), ((), ())), preferred_element_type=f32
    )


def dot_rows(left_mat, right_mat):
    return lax.dot_general(
        left_mat, right_mat, (((0,), (0,)), ((), ())), preferred_element_type=f32
    )


def dot_cols(left_mat, right_mat):
    return lax.dot_general(
        left_mat, right_mat, (((1,), (1,)), ((), ())), preferred_element_type=f32
    )


def onward(block, axis):
    size = lax.axis_size(axis)
    return lax.ppermute(block, axis, [(i, (i + 1) % size) for i in range(size)])


def after(value, *others):
    return lax.optimization_barrier((value, others))[0]


def add_low(left, right):
    return (left.astype(f32) + right.astype(f32)).astype(left.dtype)


def ring_gather(block, axis):
    slots = [block]
    for _ in range(1, lax.axis_size(axis)):
        slots.append(onward(slots[-1], axis))
    return slots


def ring_scatter(parts, axis, hops=None):
    running = parts[1]()
    for slot in range(2, lax.axis_size(axis)):
        moved = onward(running, axis)
        if hops is not None:
            hops.append(moved)
        running = add_low(parts[slot](), moved)
    moved = onward(running, axis)
    return parts[0]().astype(f32) + moved.astype(f32)


def in_order(slots, axis):
    size, me = lax.axis_size(axis), lax.axis_index(axis)
    rows = slots[0].shape[0]
    placed = jnp.zeros((size * rows,) + slots[0].shape[1:], slots[0].dtype)
    for far, slot in enumerate(slots):
        placed = lax.dynamic_update_slice_in_dim(
            placed, slot, (me - far) % size * rows, axis=0
        )
    return placed


def rotate(pieces, axis):
    size, me = lax.axis_size(axis), lax.axis_index(axis)
    came = [pieces(me)]
    for far in range(1, size):
        route = [(i, (i + far) % size) for i in range(size)]
        came.append(lax.ppermute(pieces((me + far) % size), axis, route))
    return came


def exchange(pieces, axis):
    return in_order(
        rotate(lambda i: lax.dynamic_index_in_dim(pieces, i, 0), axis), axis
    )


EARLY = [(0, 0, 0), (0, 1, 0), (1, 0, 0), (1, 0, 1)]
LATE = [(0, 0, 1), (0, 1, 1), (1, 1, 0), (1, 1, 1)]
CHUNKS = [(h, x, y, c) for part in (EARLY, LATE) for c in (0, 1) for h, x, y in part]


def swap(block, axis):
    return lax.ppermute(block, axis, SWAP)


def plane_gather(block, between=lambda early: ()):
    half = block.shape[0] // 2
    first, second = block[:half], block[half:]
    early = jnp.concatenate(
        [first, swap(first, "bx"), second, swap(second, "yb")], axis=0
    )
    late = swap(early[: 2 * half], "yb"), swap(early[2 * half :], "bx")
    groups = [(early, swap(early, "bc"))]
    late = jnp.concatenate(after(late, between(groups[0])), axis=0)
    return groups + [(late, swap(late, "bc"))]


def plane_scatter_late(terms):
    late = add_low(terms[0], swap(terms[1], "bc"))
    half = late.shape[0] // 2
    return late, swap(late[:half], "yb"), swap(late[half:], "bx")


def plane_scatter(terms, came, sums=None):
    rows = terms[0].shape[0] // 4
    early = add_low(terms[0], swap(terms[1], "bc"))
    first = add_low(early[: 2 * rows], came[1])
    second = add_low(early[2 * rows :], came[2])
    if sums is not None:
        sums.extend([first, second])
    first_sum = first[:rows].astype(f32) + swap(first[rows:], "bx").astype(f32)
    second_sum = second[:rows].astype(f32) + swap(second[rows:], "yb").astype(f32)
    return jnp.concatenate([first_sum, second_sum], axis=0)


def keep_and_swap(blocks, axis, dim, ready=()):
    me = lax.axis_index(axis)
    kept = lax.dynamic_index_in_dim(after(blocks, ready), me, dim, keepdims=False)
    sent = lax.dynamic_index_in_dim(blocks, 1 - me, dim, keepdims=False)
    return add_low(kept, swap(sent, axis))


def plane_reduce(blocks, stages=None, ready=((), ())):
    both = keep_and_swap(blocks, "bc", 3, ready[0])
    middle = blocks.shape[-1] // 2
    first = keep_and_swap(both[..., :middle], "yb", 1, ready[1])
    second = keep_and_swap(both[..., middle:], "bx", 2, ready[1])
    if stages is not None:
        stages.extend([both, (first, second)])
    first = keep_and_swap(first, "bx", 1)
    second = keep_and_swap(second, "yb", 1)
    if stages is not None:
        stages.append((first, second))
    return jnp.concatenate([first, second], axis=-1)


def rope_kernel(joint_ref, cos_ref, sin_ref, query_ref, both_ref):
    cosine, sine = cos_ref[...], sin_ref[...]
    for head in range(GROUP_HEADS):
        for part, out_ref in ((0, query_ref), (1, both_ref)):
            at = part * GROUP_WIDTH + head * HD
            raw = joint_ref[0, :, at : at + HD]
            turned = raw * cosine + pltpu.roll(raw, HD // 2, 1) * sine
            out_ref[0, :, head * HD : (head + 1) * HD] = turned.astype(bf16)
    both_ref[0, :, GROUP_WIDTH:] = joint_ref[0, :, 2 * GROUP_WIDTH :].astype(bf16)


def rope(joint, cosine, sine):
    seqs, block_len, width = joint.shape
    rows = lambda w: pl.BlockSpec((1, block_len, w), lambda b: (b, 0, 0))
    table = pl.BlockSpec((block_len, HD), lambda b: (0, 0))
    return pl.pallas_call(
        rope_kernel,
        grid=(seqs,),
        in_specs=[rows(3 * GROUP_WIDTH), table, table],
        out_specs=[rows(GROUP_WIDTH), rows(2 * GROUP_WIDTH)],
        out_shape=[
            jax.ShapeDtypeStruct((seqs, block_len, GROUP_WIDTH), bf16),
            jax.ShapeDtypeStruct((seqs, block_len, 2 * GROUP_WIDTH), bf16),
        ],
        compiler_params=pltpu.CompilerParams(vmem_limit_bytes=VMEM_LIMIT),
        name="rope",
    )(joint, cosine, sine)


def turn_back(grad, cosine, sine):
    return (grad * cosine - pltpu.roll(grad, HD // 2, 1) * sine).astype(bf16)


def query_back_kernel(terms, *refs):
    cos_ref, sin_ref, out_ref = refs[terms:]
    cosine, sine = cos_ref[0], sin_ref[0]
    for seq in range(out_ref.shape[1]):
        for head in range(GROUP_HEADS):
            at = slice(head * HD, (head + 1) * HD)
            grad = sum(ref[0, seq, :, at].astype(f32) for ref in refs[:terms])
            out_ref[0, seq, :, at] = turn_back(grad, cosine, sine)


def both_back_kernel(terms, *refs):
    key_refs, value_refs = refs[:terms], refs[terms : 2 * terms]
    cos_ref, sin_ref, _, out_ref = refs[2 * terms :]

    @pl.when(pl.program_id(1) == 0)
    def _():
        cosine, sine = cos_ref[0], sin_ref[0]
        for seq in range(out_ref.shape[1]):
            for head in range(GROUP_HEADS):
                at = slice(head * HD, (head + 1) * HD)
                grad = sum(ref[0, seq, :, at].astype(f32) for ref in key_refs)
                out_ref[0, seq, :, at] = turn_back(grad, cosine, sine)

    @pl.when(pl.program_id(1) == 1)
    def _():
        total = sum(ref[0].astype(f32) for ref in value_refs)
        out_ref[0] = total.astype(bf16)


def joint_shape(grad):
    return jax.ShapeDtypeStruct(grad.shape[:3] + (3 * GROUP_WIDTH,), bf16)


def query_back(grads, cosine, sine):
    slots, seqs, block_len, width = grads[0].shape
    rows = pl.BlockSpec((1, seqs, block_len, width), lambda s: (s, 0, 0, 0))
    table = pl.BlockSpec((1, block_len, HD), lambda s: (s, 0, 0))
    return pl.pallas_call(
        functools.partial(query_back_kernel, len(grads)),
        grid=(slots,),
        in_specs=[rows] * len(grads) + [table, table],
        out_specs=rows,
        out_shape=joint_shape(grads[0]),
        compiler_params=pltpu.CompilerParams(vmem_limit_bytes=VMEM_LIMIT),
        name="query_back",
    )(*grads, cosine, sine)


def both_back(keys, values, cosine, sine, joint):
    slots, seqs, block_len, width = keys[0].shape
    rows = pl.BlockSpec((1, seqs, block_len, width), lambda s, j: (s, 0, 0, 0))
    table = pl.BlockSpec((1, block_len, HD), lambda s, j: (s, 0, 0))
    terms = len(keys)
    return pl.pallas_call(
        functools.partial(both_back_kernel, terms),
        grid=(slots, 2),
        in_specs=[rows] * (2 * terms)
        + [table, table, pl.BlockSpec(memory_space=pl.ANY)],
        out_specs=pl.BlockSpec(
            (1, seqs, block_len, width), lambda s, j: (s, 0, 0, 1 + j)
        ),
        out_shape=joint_shape(keys[0]),
        input_output_aliases={2 * terms + 2: 0},
        compiler_params=pltpu.CompilerParams(vmem_limit_bytes=VMEM_LIMIT),
        name="both_back",
    )(*keys, *values, cosine, sine, joint)


def flat(ref):
    slots, _, block_len, width = ref.shape
    return ref[:, 0].reshape(slots * block_len, width)


def end_to_end(refs):
    return jnp.concatenate([ref[0] for ref in refs], axis=0)


def by_piece(refs, slots):
    return [refs[i : i + slots] for i in range(0, len(refs), slots)]


def attend_kernel(slots, pieces, *refs):
    active_ref, query_refs = refs[0], refs[1 : 1 + slots]
    rest = refs[1 + slots :]
    key_refs = by_piece(rest[: pieces * slots], slots)
    value_refs = by_piece(rest[pieces * slots : 2 * pieces * slots], slots)
    qplace_ref, kplace_ref, out_ref, low_ref, log_ref = rest[2 * pieces * slots :]
    queries = end_to_end(query_refs)
    query_places = qplace_ref[...]
    masked = []
    for piece in range(pieces):
        scores = dot_cols(queries, end_to_end(key_refs[piece])) * SCALE
        allowed = kplace_ref[piece] <= query_places
        masked.append(jnp.where(allowed, scores, neg_large))
    top = functools.reduce(
        jnp.maximum, [jnp.max(m, axis=1, keepdims=True) for m in masked]
    )
    total, gathered = 0.0, 0.0
    for piece in range(pieces):
        weights = jnp.exp(masked[piece] - top)
        total = total + jnp.sum(weights, axis=1, keepdims=True)
        gathered = gathered + dot(weights.astype(bf16), end_to_end(value_refs[piece]))
    result = gathered / total
    out_ref[:, 0] = result.reshape(out_ref.shape[0], out_ref.shape[2], HD)
    kept = active_ref[pl.program_id(0)]
    low_ref[:, 0] = (
        (result * kept).astype(bf16).reshape(out_ref.shape[0], out_ref.shape[2], HD)
    )
    log_ref[0, 0] = top + jnp.log(total)


def attend(active, queries, boths, query_places, key_places):
    slots, pieces = len(queries), len(boths)
    seqs, block_len, width = queries[0].shape
    rows = slots * block_len
    heads = width // HD
    own = pl.BlockSpec((1, block_len, HD), lambda s, h: (s, 0, h))
    value = pl.BlockSpec((1, block_len, HD), lambda s, h: (s, 0, heads + h))
    tile = pl.BlockSpec((slots, 1, block_len, HD), lambda s, h: (0, s, 0, h))
    every = [both for piece in boths for both in piece]
    shape = (slots, seqs, block_len, width)
    return pl.pallas_call(
        functools.partial(attend_kernel, slots, pieces),
        grid=(seqs, heads),
        in_specs=[pl.BlockSpec(memory_space=pltpu.SMEM)]
        + [own] * slots
        + [own] * len(every)
        + [value] * len(every)
        + [
            pl.BlockSpec((rows, 1), lambda s, h: (0, 0)),
            pl.BlockSpec((pieces, 1, rows), lambda s, h: (0, 0, 0)),
        ],
        out_specs=[
            tile,
            tile,
            pl.BlockSpec((1, 1, rows, 1), lambda s, h: (s, h, 0, 0)),
        ],
        out_shape=[
            jax.ShapeDtypeStruct(shape, f32),
            jax.ShapeDtypeStruct(shape, bf16),
            jax.ShapeDtypeStruct((seqs, heads, rows, 1), f32),
        ],
        compiler_params=pltpu.CompilerParams(vmem_limit_bytes=VMEM_LIMIT),
        name="attend",
    )(active, *queries, *every, *every, query_places, key_places)


def attend_back_kernel(slots, pieces, *refs):
    query_refs, rest = refs[:slots], refs[slots:]
    key_refs = by_piece(rest[: pieces * slots], slots)
    value_refs = by_piece(rest[pieces * slots : 2 * pieces * slots], slots)
    rest = rest[2 * pieces * slots :]
    grad_refs, rest = rest[:slots], rest[slots:]
    out_ref, log_ref, qplace_ref, kplace_ref, dq_ref = rest[:5]
    dk_refs, dv_refs = rest[5 : 5 + pieces], rest[5 + pieces :]
    queries, grads = end_to_end(query_refs), end_to_end(grad_refs)
    query_places = qplace_ref[...]
    dots = jnp.sum(grads.astype(f32) * flat(out_ref), axis=1, keepdims=True)
    log_norm = log_ref[0, 0]
    grad_query = 0.0
    shape = (slots, query_refs[0].shape[1], HD)
    for piece in range(pieces):
        keys, values = end_to_end(key_refs[piece]), end_to_end(value_refs[piece])
        scores = dot_cols(queries, keys) * SCALE
        allowed = kplace_ref[piece] <= query_places
        probs = jnp.exp(jnp.where(allowed, scores - log_norm, neg_large))
        grad_probs = dot_cols(grads, values)
        dv_refs[piece][:, 0] = (
            dot_rows(probs.astype(bf16), grads)
            .astype(dv_refs[piece].dtype)
            .reshape(shape)
        )
        grad_scores = (probs * (grad_probs - dots)).astype(bf16)
        dk_refs[piece][:, 0] = (
            (dot_rows(grad_scores, queries) * SCALE)
            .astype(dk_refs[piece].dtype)
            .reshape(shape)
        )
        grad_query = grad_query + dot(grad_scores, keys)
    dq_ref[:, 0] = (grad_query * SCALE).reshape(shape)


def attend_back(queries, boths, grads, out, logs, query_places, key_places, name):
    slots, pieces = len(queries), len(boths)
    seqs, block_len, width = queries[0].shape
    rows = slots * block_len
    heads = width // HD
    own = pl.BlockSpec((1, block_len, HD), lambda s, h: (s, 0, h))
    value = pl.BlockSpec((1, block_len, HD), lambda s, h: (s, 0, heads + h))
    tile = pl.BlockSpec((slots, 1, block_len, HD), lambda s, h: (0, s, 0, h))
    every = [both for piece in boths for both in piece]
    shape = (slots, seqs, block_len, width)
    wide = jax.ShapeDtypeStruct(shape, f32)
    low = jax.ShapeDtypeStruct(shape, bf16)
    found = pl.pallas_call(
        functools.partial(attend_back_kernel, slots, pieces),
        grid=(seqs, heads),
        in_specs=[own] * slots
        + [own] * len(every)
        + [value] * len(every)
        + [own] * slots
        + [
            tile,
            pl.BlockSpec((1, 1, rows, 1), lambda s, h: (s, h, 0, 0)),
            pl.BlockSpec((rows, 1), lambda s, h: (0, 0)),
            pl.BlockSpec((pieces, 1, rows), lambda s, h: (0, 0, 0)),
        ],
        out_specs=[tile] * (1 + 2 * pieces),
        out_shape=[wide] + [low] * (2 * pieces),
        compiler_params=pltpu.CompilerParams(vmem_limit_bytes=VMEM_LIMIT),
        name=name,
    )(*queries, *every, *every, *grads, out, logs, query_places, key_places)
    return found[0], found[1 : 1 + pieces], found[1 + pieces :]


def feed_up_kernel(steps, blocks, passed, *refs):
    in_refs, refs = refs[:blocks], refs[blocks:]
    heat_ref, forced_ref, route_in_ref, route_out_ref, up_ref = refs[:5]
    all_in_ref, gated_ref, scale_ref, rectified_ref = refs[5 + passed :]
    block = in_refs[0][...]
    for k in range(1, blocks):
        block = jnp.where(pl.program_id(0) < k * steps, block, in_refs[k][...])
    all_in_ref[...] = block
    units = up_ref.shape[1]
    band = units // 4

    squashed = jnp.tanh(dot(block, route_in_ref[...])).astype(bf16)
    logits = dot(squashed, route_out_ref[...]) / heat_ref[0]
    lane = lax.broadcasted_iota(jnp.int32, logits.shape, 1)
    logits = jnp.where(lane < 4, logits, neg_large)
    weights = jnp.exp(logits - jnp.max(logits, axis=1, keepdims=True))
    routed = weights / jnp.sum(weights, axis=1, keepdims=True)
    forced = forced_ref[...]
    chosen = jnp.where(lane.astype(f32) == forced - 1.0, 1.0, 0.0)
    mix = jnp.where(forced > 0.0, chosen, routed)
    scales = [mix[:, 3:4]]
    for k in (2, 1, 0):
        scales.insert(0, scales[0] + mix[:, k : k + 1])
    scale_ref[...] = by_lane(scales, scale_ref.shape)

    rectified = jnp.maximum(dot(block, up_ref[...]), 0.0)
    rectified_ref[...] = rectified
    gated_ref[...] = (rectified * rectified * by_band(scales, band, units)).astype(bf16)


def by_lane(columns, shape):
    lane = lax.broadcasted_iota(jnp.int32, shape, 1)
    found = jnp.zeros(shape, f32)
    for k, column in enumerate(columns):
        found = jnp.where(lane == k, column, found)
    return found


def by_band(columns, band, units):
    rows = columns[0].shape[0]
    if band % LANES == 0:
        return jnp.concatenate(
            [jnp.broadcast_to(column, (rows, band)) for column in columns], axis=1
        )
    at = lax.broadcasted_iota(jnp.int32, (rows, units), 1) // band
    found = jnp.broadcast_to(columns[3], (rows, units))
    for k in range(3):
        found = jnp.where(at == k, columns[k], found)
    return found


def band_sums(array, band):
    if band % LANES == 0:
        parts = [array[:, k * band : (k + 1) * band] for k in range(4)]
    else:
        at = lax.broadcasted_iota(jnp.int32, array.shape, 1) // band
        parts = [jnp.where(at == k, array, 0.0) for k in range(4)]
    return [jnp.sum(part, axis=1, keepdims=True) for part in parts]


def feed_down_kernel(count, steps, passed, *refs):
    adjoint_ref, scale_ref, rectified_ref, gated_ref, up_ref, down_ref = refs[:6]
    grad_up_ref, split_refs = refs[6 + passed], refs[7 + passed :]
    units = up_ref.shape[1]
    band = units // 4
    down = down_ref[...]
    rectified = rectified_ref[...]
    grad_gated = dot_cols(adjoint_ref[...], down)
    scales = [scale_ref[:, k : k + 1] for k in range(4)]
    twice = grad_gated * rectified
    grad_up = (twice * by_band(scales, band, units) * 2.0).astype(bf16)
    grad_up_ref[...] = grad_up
    sums = by_lane(band_sums(twice * rectified, band), split_refs[0].shape)
    grad_in = dot_cols(grad_up, up_ref[...]).astype(bf16)
    out = dot(gated_ref[...], down).astype(bf16)
    for k in range(count):

        @pl.when(pl.program_id(0) // steps == k)
        def _():
            for kind, value in enumerate((sums, grad_in, out)):
                split_refs[kind * count + k][...] = value


def tiles(width, at=0):
    return pl.BlockSpec((TILE, width), lambda i: (at + i, 0))


def fixed(array):
    return pl.BlockSpec(array.shape, lambda i: (0, 0), pipeline_mode=pl.Buffered(1))


def feed_up(blocks, heat, first, total, forced, route_in, route_out, up, passed):
    rows, width = blocks[0].shape
    tokens, count = rows * len(blocks), len(blocks)
    units = up.shape[1]
    at, steps = first // TILE, rows // TILE
    share = lambda k: pl.BlockSpec(
        (TILE, width), lambda i: (jnp.clip(i - k * steps, 0, steps - 1), 0)
    )
    before = count + 5
    return pl.pallas_call(
        functools.partial(feed_up_kernel, steps, count, len(passed)),
        grid=(tokens // TILE,),
        in_specs=[share(k) for k in range(count)]
        + [
            pl.BlockSpec(memory_space=pltpu.SMEM),
            tiles(1, at),
            fixed(route_in),
            fixed(route_out),
            fixed(up),
        ]
        + [pl.BlockSpec(memory_space=pl.ANY)] * len(passed),
        out_specs=[tiles(width, at), tiles(units, at), tiles(4), tiles(units)],
        out_shape=[
            jax.ShapeDtypeStruct((total, width), bf16),
            jax.ShapeDtypeStruct((total, units), bf16),
            jax.ShapeDtypeStruct((tokens, 4), f32),
            jax.ShapeDtypeStruct((tokens, units), f32),
        ],
        input_output_aliases={before + i: i for i in range(len(passed))},
        compiler_params=pltpu.CompilerParams(vmem_limit_bytes=VMEM_LIMIT),
        cost_estimate=pl.CostEstimate(
            flops=2 * tokens * width * units,
            bytes_accessed=2 * width * units + 6 * tokens * width,
            transcendentals=0,
        ),
        name="feed_up",
    )(*blocks, heat, forced, route_in, route_out, up, *passed)


def feed_down(adjoint, first, count, scale, rectified, gated, up, down, passed):
    total, width = adjoint.shape
    tokens, units = rectified.shape
    rows = tokens // count
    at, steps = first // TILE, rows // TILE
    share = lambda k, cols: pl.BlockSpec(
        (TILE, cols), lambda i: (jnp.clip(i - k * steps, 0, steps - 1), 0)
    )
    kinds = ((4, f32), (width, bf16), (width, bf16))
    found = pl.pallas_call(
        functools.partial(feed_down_kernel, count, steps, len(passed)),
        grid=(tokens // TILE,),
        in_specs=[
            tiles(width, at),
            tiles(4),
            tiles(units),
            tiles(units, at),
            fixed(up),
            fixed(down),
        ]
        + [pl.BlockSpec(memory_space=pl.ANY)] * len(passed),
        out_specs=[tiles(units, at)]
        + [share(k, cols) for cols, _ in kinds for k in range(count)],
        out_shape=[jax.ShapeDtypeStruct((total, units), bf16)]
        + [
            jax.ShapeDtypeStruct((rows, cols), dtype)
            for cols, dtype in kinds
            for _ in range(count)
        ],
        input_output_aliases={6 + i: i for i in range(len(passed))},
        compiler_params=pltpu.CompilerParams(vmem_limit_bytes=VMEM_LIMIT),
        cost_estimate=pl.CostEstimate(
            flops=6 * tokens * width * units,
            bytes_accessed=4 * width * units + 8 * tokens * width,
            transcendentals=0,
        ),
        name="feed_down",
    )(adjoint, scale, rectified, gated, up, down, *passed)
    return found[:1], *[found[1 + k * count : 1 + (k + 1) * count] for k in range(3)]


def columns_kernel(parts, *refs):
    place_ref, piece_refs, out_ref = refs[0], refs[1:-1], refs[-1]
    places = out_ref.shape[1] // piece_refs[0].shape[2]
    cols = piece_refs[0].shape[2] // parts
    place = 0
    for ref in piece_refs:
        for i in range(ref.shape[0]):
            for part in range(parts):
                at = pl.multiple_of((part * places + place_ref[place]) * cols, cols)
                block = ref[i, :, part * cols : (part + 1) * cols]
                out_ref[:, pl.ds(at, cols)] = block.astype(f32)
            place += 1


def columns(pieces, places, parts):
    count = sum(piece.shape[0] for piece in pieces)
    _, rows, cols = pieces[0].shape
    if cols // parts % LANES:
        every = jnp.concatenate(pieces, axis=0)[jnp.argsort(places)]
        every = every.reshape(count, rows, parts, cols // parts)
        return jnp.transpose(every, (1, 2, 0, 3)).reshape(rows, -1).astype(f32)
    return pl.pallas_call(
        functools.partial(columns_kernel, parts),
        in_specs=[pl.BlockSpec(memory_space=pltpu.SMEM)]
        + [pl.BlockSpec(memory_space=pltpu.VMEM)] * len(pieces),
        out_specs=pl.BlockSpec(memory_space=pltpu.VMEM),
        out_shape=jax.ShapeDtypeStruct((rows, count * cols), f32),
        compiler_params=pltpu.CompilerParams(vmem_limit_bytes=VMEM_LIMIT),
        name="columns",
    )(places, *pieces)


def per_device(
    layer_entries,
    incoming_adjoint,
    mixing_rescale_scalers,
    triple_projector_matrix,
    context_exit_matrix,
    dense_center_scaler,
    dense_center_offset,
    expand_matrix,
    shrink_matrix,
    span_chooser_initial,
    span_chooser_final,
    heat_divisor,
    sample_channel_fourths,
    element_preset_span,
    spot_group_table,
):
    block_len, seqs, width = layer_entries.shape
    tokens = block_len * seqs
    ring, plane = lax.axis_size("za"), lax.axis_size("yb")
    cores = lax.axis_size("bc")
    group = plane * lax.axis_size("bx") * cores
    devices = ring * group
    paired = plane == 2 and lax.axis_size("bx") == 2 and cores == 2
    za, yb = lax.axis_index("za"), lax.axis_index("yb")
    bx, bc = lax.axis_index("bx"), lax.axis_index("bc")
    rows = width // devices
    hidden_rows = FF // devices

    def home(array):
        return jnp.transpose(array, (1, 0, 2)).reshape(tokens, width)

    def back(array):
        return jnp.transpose(array.reshape(seqs, block_len, width), (1, 0, 2))

    entries, adjoint = home(layer_entries), home(incoming_adjoint)

    forced_home = jnp.transpose(element_preset_span, (1, 0)).reshape(tokens)
    forced_lanes = tokens // rows
    route_out_rows = span_chooser_final.shape[0]
    small_lanes = jnp.concatenate(
        [
            mixing_rescale_scalers[:, None],
            dense_center_scaler[:, None],
            dense_center_offset[:, None],
            jnp.pad(span_chooser_final, ((0, rows - route_out_rows), (0, 0))),
            forced_home.astype(bf16).reshape(rows, forced_lanes),
            jnp.zeros((rows, LANES - 7 - forced_lanes), bf16),
        ],
        axis=1,
    )
    qkv_cut = jnp.concatenate(
        [
            jnp.transpose(
                triple_projector_matrix.reshape(rows, 3, ring, GROUP_WIDTH),
                (2, 0, 1, 3),
            ).reshape(ring, rows, 3 * GROUP_WIDTH),
            jnp.broadcast_to(small_lanes, (ring, rows, LANES)),
            jnp.broadcast_to(span_chooser_initial, (ring, rows, RH)),
        ],
        axis=2,
    )
    units = ring * hidden_rows
    up_cut = jnp.transpose(
        expand_matrix.reshape(rows, ring, group, hidden_rows), (2, 0, 1, 3)
    ).reshape(group, rows, units)
    up_cut = lax.all_to_all(up_cut, PLANE, 0, 0, tiled=True).reshape(group * rows, units)
    qkv_cut = after(exchange(qkv_cut, "za"), up_cut)
    qkv_own = lax.all_gather(qkv_cut, PLANE, axis=1, tiled=False).reshape(width, 3 * GROUP_WIDTH + LANES + RH)
    small_lanes = qkv_own[:, 3 * GROUP_WIDTH : 3 * GROUP_WIDTH + LANES]
    route_in = qkv_own[:, 3 * GROUP_WIDTH + LANES :]
    gain_one, gain_two, bias_two = jnp.split(
        dot_cols(jnp.eye(8, LANES, dtype=bf16), small_lanes)[:3], 3, axis=0
    )
    by_device = small_lanes.reshape(devices, rows, LANES)
    route_out = by_device[:, :route_out_rows, 3:7].reshape(RH, 4)
    forced_all = by_device[:, :, 7 : 7 + forced_lanes].reshape(devices, tokens)
    out_own = lax.all_gather(context_exit_matrix, PLANE, axis=0, tiled=True)
    units = ring * hidden_rows
    entry_slots = ring_gather(entries, "za")
    up_own = lax.all_gather(
        after(up_cut, out_own, entry_slots[-1]), "za", axis=0, tiled=True
    )
    slot_ids = jnp.arange(ring, dtype=jnp.int32)
    table_ids = jnp.arange(spot_group_table.shape[0], dtype=jnp.int32)

    def places_of(piece):
        index = ((za - slot_ids) % ring) * plane + (yb - piece) % plane
        spots = jnp.sum(
            jnp.where(index[:, None] == table_ids[None, :], spot_group_table, 0), axis=1
        )
        return spots[:, None] * block_len + jnp.arange(block_len, dtype=jnp.int32)

    all_places = [places_of(piece) for piece in range(plane)]
    query_places = all_places[0].reshape(ring * block_len, 1)
    key_places = jnp.stack(all_places).reshape(plane, 1, ring * block_len)
    half = HD // 2
    inverse = theta_base ** (-(jnp.arange(half, dtype=f32) * (2.0 / HD)))
    angles = all_places[0].astype(f32)[:, :, None] * inverse
    cosine = jnp.concatenate([jnp.cos(angles), jnp.cos(angles)], axis=-1)
    sine = jnp.concatenate([-jnp.sin(angles), jnp.sin(angles)], axis=-1)
    active = (za < sample_channel_fourths).astype(f32)
    active_rows = jnp.broadcast_to(
        active[:, None, None], (seqs, block_len, 1)
    ).reshape(tokens, 1)

    if paired:
        spread = plane_gather
        at = jnp.stack(
            [
                (
                    (za * group + ((yb ^ y) * 2 + (bx ^ x)) * 2 + (bc ^ c)) * seqs + h
                ).astype(jnp.int32)
                for h, x, y, c in CHUNKS
            ]
        )
    else:
        spread = lambda block, between=None: [
            (lax.all_gather(block, PLANE, axis=0, tiled=True),)
        ]
        at = za * group * seqs + jnp.arange(group * seqs, dtype=jnp.int32)
    wide_adjoint = jnp.concatenate(sum(spread(adjoint), ()), axis=0)

    normed_slots, queries, boths = [], [], []
    for slot in range(ring):
        held = after(entry_slots[slot], entry_slots[2 if slot < 2 else ring - 1])
        if slot > 0:
            held = after(held, boths[-1][0])
        held = held.astype(f32)
        inv_rms = lax.rsqrt(jnp.mean(held * held, axis=1, keepdims=True) + epsilon)
        normed_slots.append((held * inv_rms * gain_one).astype(bf16))
        joint = dot(normed_slots[slot], qkv_own)
        query, both = rope(
            joint.reshape(seqs, block_len, joint.shape[1]), cosine[slot], sine[slot]
        )
        queries.append(query)
        boths.append(ring_gather(both, "yb"))
    boths = [[slot[piece] for slot in boths] for piece in range(plane)]
    heads_out, attended, logs = attend(active, queries, boths, query_places, key_places)
    attended = attended.reshape(ring * tokens, GROUP_WIDTH)
    inputs = entries.astype(f32)
    hops = []
    parts = [
        lambda s=s: dot(attended[s * tokens : (s + 1) * tokens], out_own).astype(bf16)
        for s in range(ring)
    ]
    for slot, needed in ((0, wide_adjoint), (2, up_own)):
        block = after(attended[slot * tokens : (slot + 1) * tokens], needed)
        parts[slot] = lambda block=block: dot(block, out_own).astype(bf16)
    hidden = inputs + ring_scatter(parts, "za", hops)
    down_own = lax.all_gather(after(shrink_matrix, hidden), "za", axis=0, tiled=True)

    centre = jnp.mean(hidden, axis=1, keepdims=True)
    centered = hidden - centre
    variance = jnp.mean(centered * centered, axis=1, keepdims=True)
    inv_std = lax.rsqrt(variance + epsilon)
    normal = centered * inv_std
    ffn_in = (normal * gain_two + bias_two).astype(bf16)

    picks = (at[:, None] == jnp.arange(devices * seqs)[None, :]).astype(bf16)
    wide_forced = dot(picks, forced_all.reshape(devices * seqs, block_len)).reshape(
        -1, 1
    )
    route_out_lanes = jnp.pad(route_out, ((0, 0), (0, LANES - 4)))

    def gather_back(groups, came=None, sums=None):
        if paired:
            came = came or plane_scatter_late(groups[1])
            return plane_scatter(groups[0], came, sums)
        return lax.psum_scatter(
            groups[0][0], PLANE, scatter_dimension=0, tiled=True
        ).astype(f32)

    total = wide_adjoint.shape[0]
    kept, firsts, passed = [], [], ()

    def up_part(blocks):
        nonlocal passed
        firsts.append(sum(scale.shape[0] for scale, _ in kept))
        found = feed_up(
            blocks,
            heat_divisor,
            firsts[-1],
            total,
            wide_forced,
            route_in,
            route_out_lanes,
            up_own,
            passed,
        )
        passed = found[:2]
        kept.append(found[2:])
        return found[2]

    groups = spread(ffn_in, up_part)
    up_part(groups[-1])
    wide_in, gated = passed
    down_terms = dot_rows(gated, after(wide_adjoint, down_own)).astype(bf16)
    grad_down = lax.psum_scatter(down_terms, "za", scatter_dimension=0, tiled=True)
    late_adjoint = after(wide_adjoint, down_terms)
    count = len(groups)
    grad_bands, grad_ins, outs = [[None] * count for _ in range(3)]
    passed, came, band_came = (), None, None
    for turn in range(count)[::-1]:
        passed, grad_bands[turn], grad_ins[turn], outs[turn] = feed_down(
            late_adjoint,
            firsts[turn],
            len(groups[turn]),
            *kept[turn],
            gated,
            up_own,
            down_own,
            passed,
        )
        if paired and turn == 1:
            band_came = plane_scatter_late(grad_bands[1])
            came = plane_scatter_late(grad_ins[1])
            passed = after(passed, came[0])
    (grad_up,) = passed
    if paired:
        grad_ins[0] = after(grad_ins[0], came)
    sums = []
    grad_ffn_in = gather_back(grad_ins, came, sums)
    grad_bands[0] = after(grad_bands[0], sums)
    grad_band_home = gather_back(grad_bands, band_came)

    temperature = heat_divisor[0]
    squashed = jnp.tanh(dot(ffn_in, route_in))
    routed = jax.nn.softmax(dot(squashed.astype(bf16), route_out) / temperature, axis=1)
    is_forced = (forced_home > 0)[:, None]
    grad_mix = jnp.cumsum(grad_band_home, axis=1)
    grad_logits = jnp.where(
        is_forced,
        0.0,
        routed
        * (grad_mix - jnp.sum(routed * grad_mix, axis=1, keepdims=True))
        / temperature,
    ).astype(bf16)
    grad_pre = (dot_cols(grad_logits, route_out) * (1.0 - squashed * squashed)).astype(
        bf16
    )
    grad_ffn_in = grad_ffn_in + dot_cols(grad_pre, route_in)
    grad_gain_two = jnp.sum(grad_ffn_in * normal, axis=0)
    grad_bias_two = jnp.sum(grad_ffn_in, axis=0)
    grad_normal = grad_ffn_in * gain_two
    grad_hidden = adjoint.astype(f32) + inv_std * (
        grad_normal
        - jnp.mean(grad_normal, axis=1, keepdims=True)
        - normal * jnp.mean(grad_normal * normal, axis=1, keepdims=True)
    )
    grad_low = after(grad_hidden.astype(bf16), grad_down)
    outs = after(outs, grad_low)
    came, steps = None, []
    if paired:
        came = plane_scatter_late(outs[1])
    out_sum = None
    if paired:
        early_outs = add_low(outs[0][0], swap(outs[0][1], "bc"))
        half_rows = early_outs.shape[0] // 2
        steps.append(add_low(early_outs[:half_rows], came[1]))
        steps.append(add_low(early_outs[half_rows:], came[2]))
    else:
        out_sum = gather_back(outs)
    grad_attn = [grad_low, onward(grad_low, "za")]
    up_terms = dot_rows(wide_in, after(grad_up, grad_low)).astype(bf16)
    grad_attn.append(onward(after(grad_attn[1], came[0] if came else (), up_terms), "za"))
    grad_attn.append(onward(after(grad_attn[2], steps), "za"))
    router_parts = after(
        (ffn_in, grad_pre, squashed, grad_logits), grad_attn[2]
    )
    grad_route_in = dot_rows(router_parts[0], router_parts[1]).astype(bf16)
    grad_route_out = dot_rows(router_parts[2].astype(bf16), router_parts[3])
    others = jnp.concatenate(
        [
            grad_gain_two.reshape(devices, rows),
            grad_bias_two.reshape(devices, rows),
            grad_route_out.reshape(devices, 4 * route_out_rows),
            jnp.zeros((devices, RH - 2 * rows - 4 * route_out_rows), f32),
        ],
        axis=1,
    ).astype(bf16)
    small_rows = rows + 16
    small_terms = jnp.concatenate(
        [
            grad_route_in.reshape(devices, rows, RH),
            others[:, None],
            jnp.zeros((devices, 15, RH), bf16),
        ],
        axis=1,
    )
    if paired:
        half_rows = steps[0].shape[0] // 2
        out_sum = jnp.concatenate(
            [
                part[:half_rows].astype(f32) + swap(part[half_rows:], axis).astype(f32)
                for part, axis in zip(steps, ("bx", "yb"))
            ],
            axis=0,
        )
        small_terms = keep_and_swap(
            small_terms.reshape(ring, plane, 2, cores, small_rows, RH), "bc", 3
        )
    else:
        small_terms = lax.psum_scatter(
            small_terms.reshape(ring, group, small_rows, RH),
            PLANE,
            scatter_dimension=1,
            tiled=False,
        )
    result = back((hidden + out_sum).astype(bf16))
    grad_attn[3] = after(grad_attn[3], result, small_terms)
    up_terms = after(up_terms, grad_attn[3])
    up_terms = lax.psum_scatter(up_terms, "za", scatter_dimension=0, tiled=True)
    up_terms = lax.all_to_all(
        up_terms.reshape(group, rows, units), PLANE, 0, 0, tiled=True
    )
    grad_heads = [
        (dot_cols(block, out_own) * active_rows)
        .astype(bf16)
        .reshape(seqs, block_len, GROUP_WIDTH)
        for block in grad_attn
    ]
    grad_queries, grad_keys, grad_values = [], [], []
    for name, chosen in (
        ("attend_back_far", range(1, plane)),
        ("attend_back", range(1)),
    ):
        if len(chosen) == 0:
            continue
        found = attend_back(
            queries,
            [boths[piece] for piece in chosen],
            grad_heads,
            heads_out,
            logs,
            query_places,
            key_places[jnp.array(chosen)],
            name,
        )
        if name == "attend_back_far":
            found, grad_heads = lax.optimization_barrier((found, grad_heads))

            def from_others(grads):
                running = grads[0]
                for term in grads[1:]:
                    running = add_low(term, onward(running, "yb"))
                return onward(running, "yb")

            grad_keys.append(from_others(found[1]))
            grad_values.append(from_others(found[2]))
        else:
            grad_keys.append(found[1][0])
            grad_values.append(found[2][0])
        grad_queries.append(found[0])
    small_terms = sum(
        part.astype(f32)
        for part in rotate(
            lambda i: lax.dynamic_index_in_dim(
                after(small_terms, grad_queries[0]), i, 0, keepdims=False
            ),
            "za",
        )
    ).astype(bf16)
    joint = query_back(grad_queries, cosine, sine)
    attn_wide = jnp.concatenate(grad_attn, axis=0)
    normed_wide = jnp.concatenate(normed_slots, axis=0)

    def to_rows(terms, stages, ready):
        cols = terms.shape[-1]
        if paired:
            terms = plane_reduce(
                terms.reshape(ring, plane, 2, cores, rows, cols), stages, ready
            )
        else:
            terms = lax.psum_scatter(
                terms.reshape(ring, group, rows, cols),
                PLANE,
                scatter_dimension=1,
                tiled=False,
            )
        return rotate(lambda i: lax.dynamic_index_in_dim(terms, i, 0), "za")

    flat_joint = lambda array: array.reshape(ring * tokens, 3 * GROUP_WIDTH)
    query_terms = dot_cols(
        flat_joint(after(joint, grad_keys, grad_values, small_terms))[:, :GROUP_WIDTH],
        qkv_own[:, :GROUP_WIDTH],
    )
    grad_out_terms = dot_rows(after(attended, grad_keys, grad_values), attn_wide).astype(bf16)
    grad_wout = lax.psum_scatter(
        grad_out_terms, PLANE, scatter_dimension=0, tiled=True
    ).astype(f32)
    grad_keys = after(grad_keys, query_terms, grad_out_terms)
    joint = flat_joint(both_back(grad_keys, grad_values, cosine, sine, joint))
    both_own = qkv_own[:, GROUP_WIDTH : 3 * GROUP_WIDTH]
    def low_term(s, ready):
        rows_of = after(joint, ready)[s * tokens : (s + 1) * tokens, GROUP_WIDTH:]
        terms = query_terms[s * tokens : (s + 1) * tokens] + dot_cols(rows_of, both_own)
        return terms.astype(bf16)

    running = after(low_term(1, ()), up_terms)
    moved_once = onward(running, "za")
    weight_terms = dot_rows(normed_wide, after(joint, running)).astype(bf16)
    small_sums = after(small_terms, running)
    if paired:
        small_sums = keep_and_swap(keep_and_swap(small_sums, "bx", 1), "yb", 0)
    small_sum = small_sums.astype(f32)
    running = add_low(after(low_term(2, ()), weight_terms, small_sums), moved_once)
    moved_twice = onward(running, "za")
    stages = []
    qkv_rows = to_rows(weight_terms, stages, (moved_once, ()))
    grad_wup = columns([after(up_terms, running)], jnp.arange(group, dtype=jnp.int32), ring)
    running = add_low(after(low_term(3, (running, stages[:1])), stages[:2]), moved_twice)
    moved = onward(running, "za")
    last = after(low_term(0, running), stages[2:], grad_wup, result)
    grad_normed = last.astype(f32) + moved.astype(f32)
    grad_wqkv = columns(qkv_rows, ((za - slot_ids) % ring).astype(jnp.int32), 3)
    weight_rows = triple_projector_matrix.astype(f32)
    grad_gain_one = jnp.sum(grad_wqkv * weight_rows, axis=1) / (
        mixing_rescale_scalers.astype(f32)
    )
    inv_home = lax.rsqrt(jnp.mean(inputs * inputs, axis=1, keepdims=True) + epsilon)
    scaled = inputs * inv_home
    grad_scaled = grad_normed * gain_one
    grad_inputs = grad_hidden + inv_home * (
        grad_scaled - scaled * jnp.mean(grad_scaled * scaled, axis=1, keepdims=True)
    )
    grad_tokens = back(grad_inputs.astype(bf16))
    return (
        result,
        grad_tokens,
        grad_gain_one,
        grad_wqkv,
        grad_wout,
        small_sum[rows, :rows],
        small_sum[rows, rows : 2 * rows],
        grad_wup,
        grad_down.astype(f32),
        small_sum[:rows],
        small_sum[rows, 2 * rows : 2 * rows + 4 * route_out_rows].reshape(-1, 4),
    )


def solution(mesh):
    seq, batch = mesh.shape["seq"], mesh.shape["batch"]
    inner = Mesh(
        mesh.devices.reshape(RING, seq // RING, batch // 2, 2),
        ("za", "yb", "bx", "bc"),
    )
    along, across = ("za", "yb"), ("bx", "bc")
    tokens = P(along, across, None)
    vector = P(along + across)
    matrix = P(along + across, None)
    return jax.shard_map(
        per_device,
        mesh=inner,
        in_specs=(
            tokens,
            tokens,
            vector,
            matrix,
            matrix,
            vector,
            vector,
            matrix,
            matrix,
            matrix,
            matrix,
            P(),
            P(across),
            P(along, across),
            P(),
        ),
        out_specs=(
            tokens,
            tokens,
            vector,
            matrix,
            matrix,
            vector,
            vector,
            matrix,
            matrix,
            matrix,
            matrix,
        ),
        check_vma=False,
    )
```

```python
import functools
import math

import jax
import jax.numpy as jnp
from jax import lax
from jax.experimental import pallas as pl
from jax.experimental.pallas import tpu as pltpu
from jax.sharding import Mesh, PartitionSpec as P

H = 16
HD = 128
FF = 8192
RH = 256
RING = 4
SEQS = 2
GROUP_HEADS = H // RING
GROUP_WIDTH = GROUP_HEADS * HD
SCALE = 1.0 / math.sqrt(HD)
VMEM_LIMIT = 48 * 1024 * 1024
TILE = 256
LANES = 128

epsilon = 1e-05
theta_base = 10000.0
neg_large = -1e30
bf16 = jnp.bfloat16
f32 = jnp.float32
PLANE = ("yb", "bx", "bc")
EVERY = ("za",) + PLANE
SWAP = [(0, 1), (1, 0)]


def dot(left_mat, right_mat):
    return lax.dot_general(
        left_mat, right_mat, (((1,), (0,)), ((), ())), preferred_element_type=f32
    )


def dot_rows(left_mat, right_mat):
    return lax.dot_general(
        left_mat, right_mat, (((0,), (0,)), ((), ())), preferred_element_type=f32
    )


def dot_cols(left_mat, right_mat):
    return lax.dot_general(
        left_mat, right_mat, (((1,), (1,)), ((), ())), preferred_element_type=f32
    )


def onward(block, axis):
    size = lax.axis_size(axis)
    return lax.ppermute(block, axis, [(i, (i + 1) % size) for i in range(size)])


def after(value, *others):
    return lax.optimization_barrier((value, others))[0]


def add_low(left, right):
    return (left.astype(f32) + right.astype(f32)).astype(left.dtype)


def ring_gather(block, axis):
    slots = [block]
    for _ in range(1, lax.axis_size(axis)):
        slots.append(onward(slots[-1], axis))
    return slots


def ring_scatter(parts, axis, hops=None):
    running = parts[1]()
    for slot in range(2, lax.axis_size(axis)):
        moved = onward(running, axis)
        if hops is not None:
            hops.append(moved)
        running = add_low(parts[slot](), moved)
    moved = onward(running, axis)
    return parts[0]().astype(f32) + moved.astype(f32)


def in_order(slots, axis):
    size, me = lax.axis_size(axis), lax.axis_index(axis)
    rows = slots[0].shape[0]
    placed = jnp.zeros((size * rows,) + slots[0].shape[1:], slots[0].dtype)
    for far, slot in enumerate(slots):
        placed = lax.dynamic_update_slice_in_dim(
            placed, slot, (me - far) % size * rows, axis=0
        )
    return placed


def rotate(pieces, axis):
    size, me = lax.axis_size(axis), lax.axis_index(axis)
    came = [pieces(me)]
    for far in range(1, size):
        route = [(i, (i + far) % size) for i in range(size)]
        came.append(lax.ppermute(pieces((me + far) % size), axis, route))
    return came


def exchange(pieces, axis):
    return in_order(
        rotate(lambda i: lax.dynamic_index_in_dim(pieces, i, 0), axis), axis
    )


EARLY = [(0, 0, 0), (0, 1, 0), (1, 0, 0), (1, 0, 1)]
LATE = [(0, 0, 1), (0, 1, 1), (1, 1, 0), (1, 1, 1)]
CHUNKS = [(h, x, y, c) for part in (EARLY, LATE) for c in (0, 1) for h, x, y in part]


def swap(block, axis):
    return lax.ppermute(block, axis, SWAP)


def plane_gather(block, between=lambda early: ()):
    half = block.shape[0] // 2
    first, second = block[:half], block[half:]
    early = jnp.concatenate(
        [first, swap(first, "bx"), second, swap(second, "yb")], axis=0
    )
    late = swap(early[: 2 * half], "yb"), swap(early[2 * half :], "bx")
    groups = [(early, swap(early, "bc"))]
    late = jnp.concatenate(after(late, between(groups[0])), axis=0)
    return groups + [(late, swap(late, "bc"))]


def plane_scatter_late(terms):
    late = add_low(terms[0], swap(terms[1], "bc"))
    half = late.shape[0] // 2
    return late, swap(late[:half], "yb"), swap(late[half:], "bx")


def plane_scatter(terms, came, sums=None):
    rows = terms[0].shape[0] // 4
    early = add_low(terms[0], swap(terms[1], "bc"))
    first = add_low(early[: 2 * rows], came[1])
    second = add_low(early[2 * rows :], came[2])
    if sums is not None:
        sums.extend([first, second])
    first_sum = first[:rows].astype(f32) + swap(first[rows:], "bx").astype(f32)
    second_sum = second[:rows].astype(f32) + swap(second[rows:], "yb").astype(f32)
    return jnp.concatenate([first_sum, second_sum], axis=0)


def keep_and_swap(blocks, axis, dim, ready=()):
    me = lax.axis_index(axis)
    kept = lax.dynamic_index_in_dim(after(blocks, ready), me, dim, keepdims=False)
    sent = lax.dynamic_index_in_dim(blocks, 1 - me, dim, keepdims=False)
    return add_low(kept, swap(sent, axis))


def plane_reduce(blocks, stages=None, ready=((), ())):
    both = keep_and_swap(blocks, "bc", 3, ready[0])
    middle = blocks.shape[-1] // 2
    first = keep_and_swap(both[..., :middle], "yb", 1, ready[1])
    second = keep_and_swap(both[..., middle:], "bx", 2, ready[1])
    if stages is not None:
        stages.extend([both, (first, second)])
    first = keep_and_swap(first, "bx", 1)
    second = keep_and_swap(second, "yb", 1)
    if stages is not None:
        stages.append((first, second))
    return jnp.concatenate([first, second], axis=-1)


def rope_kernel(joint_ref, cos_ref, sin_ref, query_ref, both_ref):
    cosine, sine = cos_ref[...], sin_ref[...]
    for head in range(GROUP_HEADS):
        for part, out_ref in ((0, query_ref), (1, both_ref)):
            at = part * GROUP_WIDTH + head * HD
            raw = joint_ref[0, :, at : at + HD]
            turned = raw * cosine + pltpu.roll(raw, HD // 2, 1) * sine
            out_ref[0, :, head * HD : (head + 1) * HD] = turned.astype(bf16)
    both_ref[0, :, GROUP_WIDTH:] = joint_ref[0, :, 2 * GROUP_WIDTH :].astype(bf16)


def rope(joint, cosine, sine):
    seqs, block_len, width = joint.shape
    rows = lambda w: pl.BlockSpec((1, block_len, w), lambda b: (b, 0, 0))
    table = pl.BlockSpec((block_len, HD), lambda b: (0, 0))
    return pl.pallas_call(
        rope_kernel,
        grid=(seqs,),
        in_specs=[rows(3 * GROUP_WIDTH), table, table],
        out_specs=[rows(GROUP_WIDTH), rows(2 * GROUP_WIDTH)],
        out_shape=[
            jax.ShapeDtypeStruct((seqs, block_len, GROUP_WIDTH), bf16),
            jax.ShapeDtypeStruct((seqs, block_len, 2 * GROUP_WIDTH), bf16),
        ],
        compiler_params=pltpu.CompilerParams(vmem_limit_bytes=VMEM_LIMIT),
        name="rope",
    )(joint, cosine, sine)


def turn_back(grad, cosine, sine):
    return (grad * cosine - pltpu.roll(grad, HD // 2, 1) * sine).astype(bf16)


def query_back_kernel(terms, *refs):
    cos_ref, sin_ref, out_ref = refs[terms:]
    cosine, sine = cos_ref[0], sin_ref[0]
    for seq in range(out_ref.shape[1]):
        for head in range(GROUP_HEADS):
            at = slice(head * HD, (head + 1) * HD)
            grad = sum(ref[0, seq, :, at].astype(f32) for ref in refs[:terms])
            out_ref[0, seq, :, at] = turn_back(grad, cosine, sine)


def both_back_kernel(terms, *refs):
    key_refs, value_refs = refs[:terms], refs[terms : 2 * terms]
    cos_ref, sin_ref, _, out_ref = refs[2 * terms :]

    @pl.when(pl.program_id(1) == 0)
    def _():
        cosine, sine = cos_ref[0], sin_ref[0]
        for seq in range(out_ref.shape[1]):
            for head in range(GROUP_HEADS):
                at = slice(head * HD, (head + 1) * HD)
                grad = sum(ref[0, seq, :, at].astype(f32) for ref in key_refs)
                out_ref[0, seq, :, at] = turn_back(grad, cosine, sine)

    @pl.when(pl.program_id(1) == 1)
    def _():
        total = sum(ref[0].astype(f32) for ref in value_refs)
        out_ref[0] = total.astype(bf16)


def joint_shape(grad):
    return jax.ShapeDtypeStruct(grad.shape[:3] + (3 * GROUP_WIDTH,), bf16)


def query_back(grads, cosine, sine):
    slots, seqs, block_len, width = grads[0].shape
    rows = pl.BlockSpec((1, seqs, block_len, width), lambda s: (s, 0, 0, 0))
    table = pl.BlockSpec((1, block_len, HD), lambda s: (s, 0, 0))
    return pl.pallas_call(
        functools.partial(query_back_kernel, len(grads)),
        grid=(slots,),
        in_specs=[rows] * len(grads) + [table, table],
        out_specs=rows,
        out_shape=joint_shape(grads[0]),
        compiler_params=pltpu.CompilerParams(vmem_limit_bytes=VMEM_LIMIT),
        name="query_back",
    )(*grads, cosine, sine)


def both_back(keys, values, cosine, sine, joint):
    slots, seqs, block_len, width = keys[0].shape
    rows = pl.BlockSpec((1, seqs, block_len, width), lambda s, j: (s, 0, 0, 0))
    table = pl.BlockSpec((1, block_len, HD), lambda s, j: (s, 0, 0))
    terms = len(keys)
    return pl.pallas_call(
        functools.partial(both_back_kernel, terms),
        grid=(slots, 2),
        in_specs=[rows] * (2 * terms)
        + [table, table, pl.BlockSpec(memory_space=pl.ANY)],
        out_specs=pl.BlockSpec(
            (1, seqs, block_len, width), lambda s, j: (s, 0, 0, 1 + j)
        ),
        out_shape=joint_shape(keys[0]),
        input_output_aliases={2 * terms + 2: 0},
        compiler_params=pltpu.CompilerParams(vmem_limit_bytes=VMEM_LIMIT),
        name="both_back",
    )(*keys, *values, cosine, sine, joint)


def flat(ref):
    slots, _, block_len, width = ref.shape
    return ref[:, 0].reshape(slots * block_len, width)


def end_to_end(refs):
    return jnp.concatenate([ref[0] for ref in refs], axis=0)


def by_piece(refs, slots):
    return [refs[i : i + slots] for i in range(0, len(refs), slots)]


def attend_kernel(slots, pieces, *refs):
    active_ref, query_refs = refs[0], refs[1 : 1 + slots]
    rest = refs[1 + slots :]
    key_refs = by_piece(rest[: pieces * slots], slots)
    value_refs = by_piece(rest[pieces * slots : 2 * pieces * slots], slots)
    qplace_ref, kplace_ref, out_ref, low_ref, log_ref = rest[2 * pieces * slots :]
    queries = end_to_end(query_refs)
    query_places = qplace_ref[...]
    masked = []
    for piece in range(pieces):
        scores = dot_cols(queries, end_to_end(key_refs[piece])) * SCALE
        allowed = kplace_ref[piece] <= query_places
        masked.append(jnp.where(allowed, scores, neg_large))
    top = functools.reduce(
        jnp.maximum, [jnp.max(m, axis=1, keepdims=True) for m in masked]
    )
    total, gathered = 0.0, 0.0
    for piece in range(pieces):
        weights = jnp.exp(masked[piece] - top)
        total = total + jnp.sum(weights, axis=1, keepdims=True)
        gathered = gathered + dot(weights.astype(bf16), end_to_end(value_refs[piece]))
    result = gathered / total
    out_ref[:, 0] = result.reshape(out_ref.shape[0], out_ref.shape[2], HD)
    kept = active_ref[pl.program_id(0)]
    low_ref[:, 0] = (
        (result * kept).astype(bf16).reshape(out_ref.shape[0], out_ref.shape[2], HD)
    )
    log_ref[0, 0] = top + jnp.log(total)


def attend(active, queries, boths, query_places, key_places):
    slots, pieces = len(queries), len(boths)
    seqs, block_len, width = queries[0].shape
    rows = slots * block_len
    heads = width // HD
    own = pl.BlockSpec((1, block_len, HD), lambda s, h: (s, 0, h))
    value = pl.BlockSpec((1, block_len, HD), lambda s, h: (s, 0, heads + h))
    tile = pl.BlockSpec((slots, 1, block_len, HD), lambda s, h: (0, s, 0, h))
    every = [both for piece in boths for both in piece]
    shape = (slots, seqs, block_len, width)
    return pl.pallas_call(
        functools.partial(attend_kernel, slots, pieces),
        grid=(seqs, heads),
        in_specs=[pl.BlockSpec(memory_space=pltpu.SMEM)]
        + [own] * slots
        + [own] * len(every)
        + [value] * len(every)
        + [
            pl.BlockSpec((rows, 1), lambda s, h: (0, 0)),
            pl.BlockSpec((pieces, 1, rows), lambda s, h: (0, 0, 0)),
        ],
        out_specs=[
            tile,
            tile,
            pl.BlockSpec((1, 1, rows, 1), lambda s, h: (s, h, 0, 0)),
        ],
        out_shape=[
            jax.ShapeDtypeStruct(shape, f32),
            jax.ShapeDtypeStruct(shape, bf16),
            jax.ShapeDtypeStruct((seqs, heads, rows, 1), f32),
        ],
        compiler_params=pltpu.CompilerParams(vmem_limit_bytes=VMEM_LIMIT),
        name="attend",
    )(active, *queries, *every, *every, query_places, key_places)


def attend_back_kernel(slots, pieces, *refs):
    query_refs, rest = refs[:slots], refs[slots:]
    key_refs = by_piece(rest[: pieces * slots], slots)
    value_refs = by_piece(rest[pieces * slots : 2 * pieces * slots], slots)
    rest = rest[2 * pieces * slots :]
    grad_refs, rest = rest[:slots], rest[slots:]
    out_ref, log_ref, qplace_ref, kplace_ref, dq_ref = rest[:5]
    dk_refs, dv_refs = rest[5 : 5 + pieces], rest[5 + pieces :]
    queries, grads = end_to_end(query_refs), end_to_end(grad_refs)
    query_places = qplace_ref[...]
    dots = jnp.sum(grads.astype(f32) * flat(out_ref), axis=1, keepdims=True)
    log_norm = log_ref[0, 0]
    grad_query = 0.0
    shape = (slots, query_refs[0].shape[1], HD)
    for piece in range(pieces):
        keys, values = end_to_end(key_refs[piece]), end_to_end(value_refs[piece])
        scores = dot_cols(queries, keys) * SCALE
        allowed = kplace_ref[piece] <= query_places
        probs = jnp.exp(jnp.where(allowed, scores - log_norm, neg_large))
        grad_probs = dot_cols(grads, values)
        dv_refs[piece][:, 0] = (
            dot_rows(probs.astype(bf16), grads)
            .astype(dv_refs[piece].dtype)
            .reshape(shape)
        )
        grad_scores = (probs * (grad_probs - dots)).astype(bf16)
        dk_refs[piece][:, 0] = (
            (dot_rows(grad_scores, queries) * SCALE)
            .astype(dk_refs[piece].dtype)
            .reshape(shape)
        )
        grad_query = grad_query + dot(grad_scores, keys)
    dq_ref[:, 0] = (grad_query * SCALE).reshape(shape)


def attend_back(queries, boths, grads, out, logs, query_places, key_places, name):
    slots, pieces = len(queries), len(boths)
    seqs, block_len, width = queries[0].shape
    rows = slots * block_len
    heads = width // HD
    own = pl.BlockSpec((1, block_len, HD), lambda s, h: (s, 0, h))
    value = pl.BlockSpec((1, block_len, HD), lambda s, h: (s, 0, heads + h))
    tile = pl.BlockSpec((slots, 1, block_len, HD), lambda s, h: (0, s, 0, h))
    every = [both for piece in boths for both in piece]
    shape = (slots, seqs, block_len, width)
    wide = jax.ShapeDtypeStruct(shape, f32)
    low = jax.ShapeDtypeStruct(shape, bf16)
    found = pl.pallas_call(
        functools.partial(attend_back_kernel, slots, pieces),
        grid=(seqs, heads),
        in_specs=[own] * slots
        + [own] * len(every)
        + [value] * len(every)
        + [own] * slots
        + [
            tile,
            pl.BlockSpec((1, 1, rows, 1), lambda s, h: (s, h, 0, 0)),
            pl.BlockSpec((rows, 1), lambda s, h: (0, 0)),
            pl.BlockSpec((pieces, 1, rows), lambda s, h: (0, 0, 0)),
        ],
        out_specs=[tile] * (1 + 2 * pieces),
        out_shape=[wide] + [low] * (2 * pieces),
        compiler_params=pltpu.CompilerParams(vmem_limit_bytes=VMEM_LIMIT),
        name=name,
    )(*queries, *every, *every, *grads, out, logs, query_places, key_places)
    return found[0], found[1 : 1 + pieces], found[1 + pieces :]


def feed_up_kernel(steps, blocks, passed, *refs):
    in_refs, refs = refs[:blocks], refs[blocks:]
    heat_ref, forced_ref, route_in_ref, route_out_ref, up_ref = refs[:5]
    all_in_ref, gated_ref, scale_ref, rectified_ref = refs[5 + passed :]
    block = in_refs[0][...]
    for k in range(1, blocks):
        block = jnp.where(pl.program_id(0) < k * steps, block, in_refs[k][...])
    all_in_ref[...] = block
    units = up_ref.shape[1]
    band = units // 4

    squashed = jnp.tanh(dot(block, route_in_ref[...])).astype(bf16)
    logits = dot(squashed, route_out_ref[...]) / heat_ref[0]
    lane = lax.broadcasted_iota(jnp.int32, logits.shape, 1)
    logits = jnp.where(lane < 4, logits, neg_large)
    weights = jnp.exp(logits - jnp.max(logits, axis=1, keepdims=True))
    routed = weights / jnp.sum(weights, axis=1, keepdims=True)
    forced = forced_ref[...]
    chosen = jnp.where(lane.astype(f32) == forced - 1.0, 1.0, 0.0)
    mix = jnp.where(forced > 0.0, chosen, routed)
    scales = [mix[:, 3:4]]
    for k in (2, 1, 0):
        scales.insert(0, scales[0] + mix[:, k : k + 1])
    scale_ref[...] = by_lane(scales, scale_ref.shape)

    rectified = jnp.maximum(dot(block, up_ref[...]), 0.0)
    rectified_ref[...] = rectified
    gated_ref[...] = (rectified * rectified * by_band(scales, band, units)).astype(bf16)


def by_lane(columns, shape):
    lane = lax.broadcasted_iota(jnp.int32, shape, 1)
    found = jnp.zeros(shape, f32)
    for k, column in enumerate(columns):
        found = jnp.where(lane == k, column, found)
    return found


def by_band(columns, band, units):
    rows = columns[0].shape[0]
    if band % LANES == 0:
        return jnp.concatenate(
            [jnp.broadcast_to(column, (rows, band)) for column in columns], axis=1
        )
    at = lax.broadcasted_iota(jnp.int32, (rows, units), 1) // band
    found = jnp.broadcast_to(columns[3], (rows, units))
    for k in range(3):
        found = jnp.where(at == k, columns[k], found)
    return found


def band_sums(array, band):
    if band % LANES == 0:
        parts = [array[:, k * band : (k + 1) * band] for k in range(4)]
    else:
        at = lax.broadcasted_iota(jnp.int32, array.shape, 1) // band
        parts = [jnp.where(at == k, array, 0.0) for k in range(4)]
    return [jnp.sum(part, axis=1, keepdims=True) for part in parts]


def feed_down_kernel(count, steps, passed, *refs):
    adjoint_ref, scale_ref, rectified_ref, gated_ref, up_ref, down_ref = refs[:6]
    grad_up_ref, split_refs = refs[6 + passed], refs[7 + passed :]
    units = up_ref.shape[1]
    band = units // 4
    down = down_ref[...]
    rectified = rectified_ref[...]
    grad_gated = dot_cols(adjoint_ref[...], down)
    scales = [scale_ref[:, k : k + 1] for k in range(4)]
    twice = grad_gated * rectified
    grad_up = (twice * by_band(scales, band, units) * 2.0).astype(bf16)
    grad_up_ref[...] = grad_up
    sums = by_lane(band_sums(twice * rectified, band), split_refs[0].shape)
    grad_in = dot_cols(grad_up, up_ref[...]).astype(bf16)
    out = dot(gated_ref[...], down).astype(bf16)
    for k in range(count):

        @pl.when(pl.program_id(0) // steps == k)
        def _():
            for kind, value in enumerate((sums, grad_in, out)):
                split_refs[kind * count + k][...] = value


def tiles(width, at=0):
    return pl.BlockSpec((TILE, width), lambda i: (at + i, 0))


def fixed(array):
    return pl.BlockSpec(array.shape, lambda i: (0, 0), pipeline_mode=pl.Buffered(1))


def feed_up(blocks, heat, first, total, forced, route_in, route_out, up, passed):
    rows, width = blocks[0].shape
    tokens, count = rows * len(blocks), len(blocks)
    units = up.shape[1]
    at, steps = first // TILE, rows // TILE
    share = lambda k: pl.BlockSpec(
        (TILE, width), lambda i: (jnp.clip(i - k * steps, 0, steps - 1), 0)
    )
    before = count + 5
    return pl.pallas_call(
        functools.partial(feed_up_kernel, steps, count, len(passed)),
        grid=(tokens // TILE,),
        in_specs=[share(k) for k in range(count)]
        + [
            pl.BlockSpec(memory_space=pltpu.SMEM),
            tiles(1, at),
            fixed(route_in),
            fixed(route_out),
            fixed(up),
        ]
        + [pl.BlockSpec(memory_space=pl.ANY)] * len(passed),
        out_specs=[tiles(width, at), tiles(units, at), tiles(4), tiles(units)],
        out_shape=[
            jax.ShapeDtypeStruct((total, width), bf16),
            jax.ShapeDtypeStruct((total, units), bf16),
            jax.ShapeDtypeStruct((tokens, 4), f32),
            jax.ShapeDtypeStruct((tokens, units), f32),
        ],
        input_output_aliases={before + i: i for i in range(len(passed))},
        compiler_params=pltpu.CompilerParams(vmem_limit_bytes=VMEM_LIMIT),
        cost_estimate=pl.CostEstimate(
            flops=2 * tokens * width * units,
            bytes_accessed=2 * width * units + 6 * tokens * width,
            transcendentals=0,
        ),
        name="feed_up",
    )(*blocks, heat, forced, route_in, route_out, up, *passed)


def feed_down(adjoint, first, count, scale, rectified, gated, up, down, passed):
    total, width = adjoint.shape
    tokens, units = rectified.shape
    rows = tokens // count
    at, steps = first // TILE, rows // TILE
    share = lambda k, cols: pl.BlockSpec(
        (TILE, cols), lambda i: (jnp.clip(i - k * steps, 0, steps - 1), 0)
    )
    kinds = ((4, f32), (width, bf16), (width, bf16))
    found = pl.pallas_call(
        functools.partial(feed_down_kernel, count, steps, len(passed)),
        grid=(tokens // TILE,),
        in_specs=[
            tiles(width, at),
            tiles(4),
            tiles(units),
            tiles(units, at),
            fixed(up),
            fixed(down),
        ]
        + [pl.BlockSpec(memory_space=pl.ANY)] * len(passed),
        out_specs=[tiles(units, at)]
        + [share(k, cols) for cols, _ in kinds for k in range(count)],
        out_shape=[jax.ShapeDtypeStruct((total, units), bf16)]
        + [
            jax.ShapeDtypeStruct((rows, cols), dtype)
            for cols, dtype in kinds
            for _ in range(count)
        ],
        input_output_aliases={6 + i: i for i in range(len(passed))},
        compiler_params=pltpu.CompilerParams(vmem_limit_bytes=VMEM_LIMIT),
        cost_estimate=pl.CostEstimate(
            flops=6 * tokens * width * units,
            bytes_accessed=4 * width * units + 8 * tokens * width,
            transcendentals=0,
        ),
        name="feed_down",
    )(adjoint, scale, rectified, gated, up, down, *passed)
    return found[:1], *[found[1 + k * count : 1 + (k + 1) * count] for k in range(3)]


def columns_kernel(parts, *refs):
    place_ref, piece_refs, out_ref = refs[0], refs[1:-1], refs[-1]
    places = out_ref.shape[1] // piece_refs[0].shape[2]
    cols = piece_refs[0].shape[2] // parts
    place = 0
    for ref in piece_refs:
        for i in range(ref.shape[0]):
            for part in range(parts):
                at = pl.multiple_of((part * places + place_ref[place]) * cols, cols)
                block = ref[i, :, part * cols : (part + 1) * cols]
                out_ref[:, pl.ds(at, cols)] = block.astype(f32)
            place += 1


def columns(pieces, places, parts):
    count = sum(piece.shape[0] for piece in pieces)
    _, rows, cols = pieces[0].shape
    if cols // parts % LANES:
        every = jnp.concatenate(pieces, axis=0)[jnp.argsort(places)]
        every = every.reshape(count, rows, parts, cols // parts)
        return jnp.transpose(every, (1, 2, 0, 3)).reshape(rows, -1).astype(f32)
    return pl.pallas_call(
        functools.partial(columns_kernel, parts),
        in_specs=[pl.BlockSpec(memory_space=pltpu.SMEM)]
        + [pl.BlockSpec(memory_space=pltpu.VMEM)] * len(pieces),
        out_specs=pl.BlockSpec(memory_space=pltpu.VMEM),
        out_shape=jax.ShapeDtypeStruct((rows, count * cols), f32),
        compiler_params=pltpu.CompilerParams(vmem_limit_bytes=VMEM_LIMIT),
        name="columns",
    )(places, *pieces)


def per_device(
    layer_entries,
    incoming_adjoint,
    mixing_rescale_scalers,
    triple_projector_matrix,
    context_exit_matrix,
    dense_center_scaler,
    dense_center_offset,
    expand_matrix,
    shrink_matrix,
    span_chooser_initial,
    span_chooser_final,
    heat_divisor,
    sample_channel_fourths,
    element_preset_span,
    spot_group_table,
):
    block_len, seqs, width = layer_entries.shape
    tokens = block_len * seqs
    ring, plane = lax.axis_size("za"), lax.axis_size("yb")
    cores = lax.axis_size("bc")
    group = plane * lax.axis_size("bx") * cores
    devices = ring * group
    paired = plane == 2 and lax.axis_size("bx") == 2 and cores == 2
    za, yb = lax.axis_index("za"), lax.axis_index("yb")
    bx, bc = lax.axis_index("bx"), lax.axis_index("bc")
    rows = width // devices
    hidden_rows = FF // devices

    def home(array):
        return jnp.transpose(array, (1, 0, 2)).reshape(tokens, width)

    def back(array):
        return jnp.transpose(array.reshape(seqs, block_len, width), (1, 0, 2))

    entries, adjoint = home(layer_entries), home(incoming_adjoint)

    forced_home = jnp.transpose(element_preset_span, (1, 0)).reshape(tokens)
    forced_lanes = tokens // rows
    route_out_rows = span_chooser_final.shape[0]
    small_lanes = jnp.concatenate(
        [
            mixing_rescale_scalers[:, None],
            dense_center_scaler[:, None],
            dense_center_offset[:, None],
            jnp.pad(span_chooser_final, ((0, rows - route_out_rows), (0, 0))),
            forced_home.astype(bf16).reshape(rows, forced_lanes),
            jnp.zeros((rows, LANES - 7 - forced_lanes), bf16),
        ],
        axis=1,
    )
    qkv_cut = jnp.concatenate(
        [
            jnp.transpose(
                triple_projector_matrix.reshape(rows, 3, ring, GROUP_WIDTH),
                (2, 0, 1, 3),
            ).reshape(ring, rows, 3 * GROUP_WIDTH),
            jnp.broadcast_to(small_lanes, (ring, rows, LANES)),
            jnp.broadcast_to(span_chooser_initial, (ring, rows, RH)),
        ],
        axis=2,
    )
    units = ring * hidden_rows
    up_cut = jnp.transpose(
        expand_matrix.reshape(rows, ring, group, hidden_rows), (2, 0, 1, 3)
    ).reshape(group, rows, units)
    up_cut = lax.all_to_all(up_cut, PLANE, 0, 0, tiled=True).reshape(group * rows, units)
    qkv_cut = after(exchange(qkv_cut, "za"), up_cut)
    qkv_own = lax.all_gather(qkv_cut, PLANE, axis=1, tiled=False).reshape(width, 3 * GROUP_WIDTH + LANES + RH)
    small_lanes = qkv_own[:, 3 * GROUP_WIDTH : 3 * GROUP_WIDTH + LANES]
    route_in = qkv_own[:, 3 * GROUP_WIDTH + LANES :]
    gain_one, gain_two, bias_two = jnp.split(
        dot_cols(jnp.eye(8, LANES, dtype=bf16), small_lanes)[:3], 3, axis=0
    )
    by_device = small_lanes.reshape(devices, rows, LANES)
    route_out = by_device[:, :route_out_rows, 3:7].reshape(RH, 4)
    forced_all = by_device[:, :, 7 : 7 + forced_lanes].reshape(devices, tokens)
    out_own = lax.all_gather(context_exit_matrix, PLANE, axis=0, tiled=True)
    units = ring * hidden_rows
    entry_slots = ring_gather(entries, "za")
    up_own = lax.all_gather(
        after(up_cut, out_own, entry_slots[-1]), "za", axis=0, tiled=True
    )
    slot_ids = jnp.arange(ring, dtype=jnp.int32)
    table_ids = jnp.arange(spot_group_table.shape[0], dtype=jnp.int32)

    def places_of(piece):
        index = ((za - slot_ids) % ring) * plane + (yb - piece) % plane
        spots = jnp.sum(
            jnp.where(index[:, None] == table_ids[None, :], spot_group_table, 0), axis=1
        )
        return spots[:, None] * block_len + jnp.arange(block_len, dtype=jnp.int32)

    all_places = [places_of(piece) for piece in range(plane)]
    query_places = all_places[0].reshape(ring * block_len, 1)
    key_places = jnp.stack(all_places).reshape(plane, 1, ring * block_len)
    half = HD // 2
    inverse = theta_base ** (-(jnp.arange(half, dtype=f32) * (2.0 / HD)))
    angles = all_places[0].astype(f32)[:, :, None] * inverse
    cosine = jnp.concatenate([jnp.cos(angles), jnp.cos(angles)], axis=-1)
    sine = jnp.concatenate([-jnp.sin(angles), jnp.sin(angles)], axis=-1)
    active = (za < sample_channel_fourths).astype(f32)
    active_rows = jnp.broadcast_to(
        active[:, None, None], (seqs, block_len, 1)
    ).reshape(tokens, 1)

    if paired:
        spread = plane_gather
        at = jnp.stack(
            [
                (
                    (za * group + ((yb ^ y) * 2 + (bx ^ x)) * 2 + (bc ^ c)) * seqs + h
                ).astype(jnp.int32)
                for h, x, y, c in CHUNKS
            ]
        )
    else:
        spread = lambda block, between=None: [
            (lax.all_gather(block, PLANE, axis=0, tiled=True),)
        ]
        at = za * group * seqs + jnp.arange(group * seqs, dtype=jnp.int32)
    wide_adjoint = jnp.concatenate(sum(spread(adjoint), ()), axis=0)

    normed_slots, queries, boths = [], [], []
    for slot in range(ring):
        held = after(entry_slots[slot], entry_slots[2 if slot < 2 else ring - 1])
        if slot > 0:
            held = after(held, boths[-1][0])
        held = held.astype(f32)
        inv_rms = lax.rsqrt(jnp.mean(held * held, axis=1, keepdims=True) + epsilon)
        normed_slots.append((held * inv_rms * gain_one).astype(bf16))
        joint = dot(normed_slots[slot], qkv_own)
        query, both = rope(
            joint.reshape(seqs, block_len, joint.shape[1]), cosine[slot], sine[slot]
        )
        queries.append(query)
        boths.append(ring_gather(both, "yb"))
    boths = [[slot[piece] for slot in boths] for piece in range(plane)]
    heads_out, attended, logs = attend(active, queries, boths, query_places, key_places)
    attended = attended.reshape(ring * tokens, GROUP_WIDTH)
    inputs = entries.astype(f32)
    hops = []
    parts = [
        lambda s=s: dot(attended[s * tokens : (s + 1) * tokens], out_own).astype(bf16)
        for s in range(ring)
    ]
    for slot, needed in ((0, wide_adjoint), (2, up_own)):
        block = after(attended[slot * tokens : (slot + 1) * tokens], needed)
        parts[slot] = lambda block=block: dot(block, out_own).astype(bf16)
    hidden = inputs + ring_scatter(parts, "za", hops)
    down_own = lax.all_gather(after(shrink_matrix, hidden), "za", axis=0, tiled=True)

    centre = jnp.mean(hidden, axis=1, keepdims=True)
    centered = hidden - centre
    variance = jnp.mean(centered * centered, axis=1, keepdims=True)
    inv_std = lax.rsqrt(variance + epsilon)
    normal = centered * inv_std
    ffn_in = (normal * gain_two + bias_two).astype(bf16)

    picks = (at[:, None] == jnp.arange(devices * seqs)[None, :]).astype(bf16)
    wide_forced = dot(picks, forced_all.reshape(devices * seqs, block_len)).reshape(
        -1, 1
    )
    route_out_lanes = jnp.pad(route_out, ((0, 0), (0, LANES - 4)))

    def gather_back(groups, came=None, sums=None):
        if paired:
            came = came or plane_scatter_late(groups[1])
            return plane_scatter(groups[0], came, sums)
        return lax.psum_scatter(
            groups[0][0], PLANE, scatter_dimension=0, tiled=True
        ).astype(f32)

    total = wide_adjoint.shape[0]
    kept, firsts, passed = [], [], ()

    def up_part(blocks):
        nonlocal passed
        firsts.append(sum(scale.shape[0] for scale, _ in kept))
        found = feed_up(
            blocks,
            heat_divisor,
            firsts[-1],
            total,
            wide_forced,
            route_in,
            route_out_lanes,
            up_own,
            passed,
        )
        passed = found[:2]
        kept.append(found[2:])
        return found[2]

    groups = spread(ffn_in, up_part)
    up_part(groups[-1])
    wide_in, gated = passed
    down_terms = dot_rows(gated, after(wide_adjoint, down_own)).astype(bf16)
    grad_down = lax.psum_scatter(down_terms, "za", scatter_dimension=0, tiled=True)
    late_adjoint = after(wide_adjoint, down_terms)
    count = len(groups)
    grad_bands, grad_ins, outs = [[None] * count for _ in range(3)]
    passed, came, band_came = (), None, None
    for turn in range(count)[::-1]:
        passed, grad_bands[turn], grad_ins[turn], outs[turn] = feed_down(
            late_adjoint,
            firsts[turn],
            len(groups[turn]),
            *kept[turn],
            gated,
            up_own,
            down_own,
            passed,
        )
        if paired and turn == 1:
            band_came = plane_scatter_late(grad_bands[1])
            came = plane_scatter_late(grad_ins[1])
            passed = after(passed, came[0])
    (grad_up,) = passed
    if paired:
        grad_ins[0] = after(grad_ins[0], came)
    sums = []
    grad_ffn_in = gather_back(grad_ins, came, sums)
    grad_bands[0] = after(grad_bands[0], sums)
    grad_band_home = gather_back(grad_bands, band_came)

    temperature = heat_divisor[0]
    squashed = jnp.tanh(dot(ffn_in, route_in))
    routed = jax.nn.softmax(dot(squashed.astype(bf16), route_out) / temperature, axis=1)
    is_forced = (forced_home > 0)[:, None]
    grad_mix = jnp.cumsum(grad_band_home, axis=1)
    grad_logits = jnp.where(
        is_forced,
        0.0,
        routed
        * (grad_mix - jnp.sum(routed * grad_mix, axis=1, keepdims=True))
        / temperature,
    ).astype(bf16)
    grad_pre = (dot_cols(grad_logits, route_out) * (1.0 - squashed * squashed)).astype(
        bf16
    )
    grad_ffn_in = grad_ffn_in + dot_cols(grad_pre, route_in)
    grad_gain_two = jnp.sum(grad_ffn_in * normal, axis=0)
    grad_bias_two = jnp.sum(grad_ffn_in, axis=0)
    grad_normal = grad_ffn_in * gain_two
    grad_hidden = adjoint.astype(f32) + inv_std * (
        grad_normal
        - jnp.mean(grad_normal, axis=1, keepdims=True)
        - normal * jnp.mean(grad_normal * normal, axis=1, keepdims=True)
    )
    grad_low = after(grad_hidden.astype(bf16), grad_down)
    outs = after(outs, grad_low)
    came, steps = None, []
    if paired:
        came = plane_scatter_late(outs[1])
    out_sum = None
    if paired:
        early_outs = add_low(outs[0][0], swap(outs[0][1], "bc"))
        half_rows = early_outs.shape[0] // 2
        steps.append(add_low(early_outs[:half_rows], came[1]))
        steps.append(add_low(early_outs[half_rows:], came[2]))
    else:
        out_sum = gather_back(outs)
    grad_attn = [grad_low, onward(grad_low, "za")]
    up_terms = dot_rows(wide_in, after(grad_up, grad_low)).astype(bf16)
    grad_attn.append(onward(after(grad_attn[1], came[0] if came else (), up_terms), "za"))
    grad_attn.append(onward(after(grad_attn[2], steps), "za"))
    router_parts = after(
        (ffn_in, grad_pre, squashed, grad_logits), grad_attn[2]
    )
    grad_route_in = dot_rows(router_parts[0], router_parts[1]).astype(bf16)
    grad_route_out = dot_rows(router_parts[2].astype(bf16), router_parts[3])
    others = jnp.concatenate(
        [
            grad_gain_two.reshape(devices, rows),
            grad_bias_two.reshape(devices, rows),
            grad_route_out.reshape(devices, 4 * route_out_rows),
            jnp.zeros((devices, RH - 2 * rows - 4 * route_out_rows), f32),
        ],
        axis=1,
    ).astype(bf16)
    small_rows = rows + 16
    small_terms = jnp.concatenate(
        [
            grad_route_in.reshape(devices, rows, RH),
            others[:, None],
            jnp.zeros((devices, 15, RH), bf16),
        ],
        axis=1,
    )
    if paired:
        half_rows = steps[0].shape[0] // 2
        out_sum = jnp.concatenate(
            [
                part[:half_rows].astype(f32) + swap(part[half_rows:], axis).astype(f32)
                for part, axis in zip(steps, ("bx", "yb"))
            ],
            axis=0,
        )
        small_terms = keep_and_swap(
            small_terms.reshape(ring, plane, 2, cores, small_rows, RH), "bc", 3
        )
    else:
        small_terms = lax.psum_scatter(
            small_terms.reshape(ring, group, small_rows, RH),
            PLANE,
            scatter_dimension=1,
            tiled=False,
        )
    result = back((hidden + out_sum).astype(bf16))
    grad_attn[3] = after(grad_attn[3], result, small_terms)
    up_terms = after(up_terms, grad_attn[3])
    up_terms = lax.psum_scatter(up_terms, "za", scatter_dimension=0, tiled=True)
    up_sums = up_terms
    grad_heads = [
        (dot_cols(block, out_own) * active_rows)
        .astype(bf16)
        .reshape(seqs, block_len, GROUP_WIDTH)
        for block in grad_attn
    ]
    grad_queries, grad_keys, grad_values = [], [], []
    for name, chosen in (
        ("attend_back_far", range(1, plane)),
        ("attend_back", range(1)),
    ):
        if len(chosen) == 0:
            continue
        found = attend_back(
            queries,
            [boths[piece] for piece in chosen],
            grad_heads,
            heads_out,
            logs,
            query_places,
            key_places[jnp.array(chosen)],
            name,
        )
        if name == "attend_back_far":
            found, grad_heads = lax.optimization_barrier((found, grad_heads))

            def from_others(grads):
                running = grads[0]
                for term in grads[1:]:
                    running = add_low(term, onward(running, "yb"))
                return onward(running, "yb")

            grad_keys.append(from_others(found[1]))
            grad_values.append(from_others(found[2]))
        else:
            grad_keys.append(found[1][0])
            grad_values.append(found[2][0])
        grad_queries.append(found[0])
    if paired:
        small_terms = keep_and_swap(after(small_terms, grad_queries[0]), "bx", 2)
    joint = query_back(grad_queries, cosine, sine)
    attn_wide = jnp.concatenate(grad_attn, axis=0)
    normed_wide = jnp.concatenate(normed_slots, axis=0)

    def to_rows(terms, stages, ready):
        cols = terms.shape[-1]
        if paired:
            terms = plane_reduce(
                terms.reshape(ring, plane, 2, cores, rows, cols), stages, ready
            )
        else:
            terms = lax.psum_scatter(
                terms.reshape(ring, group, rows, cols),
                PLANE,
                scatter_dimension=1,
                tiled=False,
            )
        return rotate(lambda i: lax.dynamic_index_in_dim(terms, i, 0), "za")

    flat_joint = lambda array: array.reshape(ring * tokens, 3 * GROUP_WIDTH)
    query_terms = dot_cols(
        flat_joint(after(joint, grad_keys, grad_values, small_terms))[:, :GROUP_WIDTH],
        qkv_own[:, :GROUP_WIDTH],
    )
    grad_out_terms = dot_rows(after(attended, grad_keys, grad_values), attn_wide).astype(bf16)
    grad_wout = lax.psum_scatter(
        grad_out_terms, PLANE, scatter_dimension=0, tiled=True
    ).astype(f32)
    grad_keys = after(grad_keys, query_terms, grad_out_terms)
    joint = flat_joint(both_back(grad_keys, grad_values, cosine, sine, joint))
    both_own = qkv_own[:, GROUP_WIDTH : 3 * GROUP_WIDTH]
    def low_term(s, ready):
        rows_of = after(joint, ready)[s * tokens : (s + 1) * tokens, GROUP_WIDTH:]
        terms = query_terms[s * tokens : (s + 1) * tokens] + dot_cols(rows_of, both_own)
        return terms.astype(bf16)

    running = after(low_term(1, ()), up_sums)
    moved_once = onward(running, "za")
    weight_terms = dot_rows(normed_wide, after(joint, running)).astype(bf16)
    running = add_low(after(low_term(2, ()), weight_terms), moved_once)
    moved_twice = onward(running, "za")
    stages = []
    qkv_rows = to_rows(weight_terms, stages, (moved_once, moved_twice))
    if paired:
        small_terms = keep_and_swap(after(small_terms, stages[0]), "yb", 1)
    up_terms = lax.all_to_all(
        after(up_sums, moved_once, stages[:1]).reshape(group, rows, units), PLANE, 0, 0, tiled=True
    )
    grad_wup = columns([up_terms], jnp.arange(group, dtype=jnp.int32), ring)
    running = add_low(after(low_term(3, (running, stages[:1])), stages[:1]), moved_twice)
    moved = onward(running, "za")
    small_sum = sum(
        part.astype(f32)
        for part in rotate(
            lambda i: lax.dynamic_index_in_dim(
                after(small_terms, running), i, 0, keepdims=False
            ),
            "za",
        )
    )
    last = after(low_term(0, running), stages[2:], grad_wup, result, small_sum)
    grad_normed = last.astype(f32) + moved.astype(f32)
    grad_wqkv = columns(qkv_rows, ((za - slot_ids) % ring).astype(jnp.int32), 3)
    weight_rows = triple_projector_matrix.astype(f32)
    grad_gain_one = jnp.sum(grad_wqkv * weight_rows, axis=1) / (
        mixing_rescale_scalers.astype(f32)
    )
    inv_home = lax.rsqrt(jnp.mean(inputs * inputs, axis=1, keepdims=True) + epsilon)
    scaled = inputs * inv_home
    grad_scaled = grad_normed * gain_one
    grad_inputs = grad_hidden + inv_home * (
        grad_scaled - scaled * jnp.mean(grad_scaled * scaled, axis=1, keepdims=True)
    )
    grad_tokens = back(grad_inputs.astype(bf16))
    return (
        result,
        grad_tokens,
        grad_gain_one,
        grad_wqkv,
        grad_wout,
        small_sum[rows, :rows],
        small_sum[rows, rows : 2 * rows],
        grad_wup,
        grad_down.astype(f32),
        small_sum[:rows],
        small_sum[rows, 2 * rows : 2 * rows + 4 * route_out_rows].reshape(-1, 4),
    )


def solution(mesh):
    seq, batch = mesh.shape["seq"], mesh.shape["batch"]
    inner = Mesh(
        mesh.devices.reshape(RING, seq // RING, batch // 2, 2),
        ("za", "yb", "bx", "bc"),
    )
    along, across = ("za", "yb"), ("bx", "bc")
    tokens = P(along, across, None)
    vector = P(along + across)
    matrix = P(along + across, None)
    return jax.shard_map(
        per_device,
        mesh=inner,
        in_specs=(
            tokens,
            tokens,
            vector,
            matrix,
            matrix,
            vector,
            vector,
            matrix,
            matrix,
            matrix,
            matrix,
            P(),
            P(across),
            P(along, across),
            P(),
        ),
        out_specs=(
            tokens,
            tokens,
            vector,
            matrix,
            matrix,
            vector,
            vector,
            matrix,
            matrix,
            matrix,
            matrix,
        ),
        check_vma=False,
    )
```
